128 devices in a mesh: row: 4 (over z), col: 32 (over x, y, core).
Axes of the slice: x: 4, y: 4, z: 4, core: 2. Of those that a mesh axis runs over, the one named last changes fastest.
Arguments:
- layer_input: bfloat16 [1088, 16384], P('col', 'row'), may hold values from -6 to 6
- cotangent: bfloat16 [1088, 16384], P('col', 'row'), may hold values from -6 to 6
- segments: int32 [16, 1024], P('row'), may hold values from 0 to 3, as said below
- qkv_weight: bfloat16 [1088, 3, 1088], P('row', None, 'col'), may hold values from -0.1875 to 0.1875
- qv_bias: bfloat16 [2, 1088], P(None, 'col'), may hold values from -1 to 1
- out_weight: bfloat16 [1088, 1088], P('row', 'col'), may hold values from -1.5 to 1.5
- out_bias: bfloat16 [1088], P('col'), may hold values from -1 to 1
- up_weight: bfloat16 [1088, 4352], P('row', 'col'), may hold values from -0.1875 to 0.1875
- up_bias: bfloat16 [4352], P('col'), may hold values from -1 to 1
- down_weight: bfloat16 [4352, 1088], P('col', 'row'), may hold values from -0.09375 to 0.09375
- down_bias: bfloat16 [1088], P('col'), may hold values from -1 to 1
- first_gain: bfloat16 [1088], P('col'), may hold values from 0.5 to 1.5
- first_shift: bfloat16 [1088], P('col'), may hold values from -1 to 1
- second_gain: bfloat16 [1088], P('col'), may hold values from 0.5 to 1.5
- second_shift: bfloat16 [1088], P('col'), may hold values from -1 to 1
Outputs:
- layer_output: float32 [1088, 16384], P('col', 'row')
- input_grad: float32 [1088, 16384], P('col', 'row')
- qkv_grad: float32 [1088, 3, 1088], P('row', None, 'col')
- qvbias_grad: float32 [2, 1088], P(None, 'col')
- out_grad: float32 [1088, 1088], P('row', 'col')
- outbias_grad: float32 [1088], P('col')
- up_grad: float32 [1088, 4352], P('row', 'col')
- upbias_grad: float32 [4352], P('col')
- down_grad: float32 [4352, 1088], P('col', 'row')
- downbias_grad: float32 [1088], P('col')
- firstgain_grad: float32 [1088], P('col')
- firstshift_grad: float32 [1088], P('col')
- secondgain_grad: float32 [1088], P('col')
- secondshift_grad: float32 [1088], P('col')
The draws below stay inside these ranges and needn't reach their ends.
Inputs may be any that keep to these rules, and one draw needn't show every extreme that they name: `segments`: segment numbers never fall along a sequence. In each row index's 4 sequences one sequence is a single document.
All inputs are finite; a program needn't handle non-finite values.
Results may differ from the reference program's by a relative error of at most 0.014.
Values may be sent and summed in bfloat16 or wider, within the bound.
A program may use at most 256 MiB of HBM per device.

```python
import jax
import jax.numpy as jnp
from jax import lax

D = 1088
HEADS = 17
HD = 64
FF = 4352
LEN = 1024
SEQ_ROW = 4
SEQS = 16
TOKENS = 16384


def draw_segments(key, part):
    key = jax.random.fold_in(key, 11)
    key_cuts, key_used, key_whole = jax.random.split(key, 3)
    cut_points = jax.random.randint(key_cuts, (SEQS, 3), 1, LEN)
    cut_used = jax.random.randint(key_used, (SEQS, 3), 0, 2)
    group_count = SEQS // SEQ_ROW
    single_doc = jax.random.randint(key_whole, (group_count,), 0, SEQ_ROW)
    seq_ids = jnp.arange(SEQS)
    whole_doc = seq_ids % SEQ_ROW == single_doc[seq_ids // SEQ_ROW]
    cut_used = jnp.where(whole_doc[:, None], 0, cut_used)
    positions = jnp.arange(LEN)
    passed = (positions[None, :, None] >= cut_points[:, None, :]).astype(jnp.int32)
    return jnp.sum(passed * cut_used[:, None, :], axis=-1).astype(jnp.int32)


def block_scale(rng, dims, shards, smallest, largest):
    factor_of = 1.0
    for axis_at, shards_of in shards:
        steps = jax.random.uniform(jax.random.fold_in(jax.random.fold_in(rng, 6), axis_at), (shards_of,), jnp.float32, smallest / len(shards), largest / len(shards))
        factor_of = factor_of * jnp.repeat(jnp.exp(steps), dims[axis_at] // shards_of).reshape((-1,) + (1,) * (len(dims) - 1 - axis_at))
    return factor_of


def scatter_about(rng, dims, deviation, reach, cuts=(), dtype=jnp.bfloat16):
    gain = block_scale(rng, dims, cuts, -0.22, 0.18) if cuts else 1.0
    values = jax.random.normal(rng, dims, jnp.float32) * deviation * gain
    return jnp.minimum(jnp.maximum(values, -reach), reach).astype(dtype)


def setup_inputs(seed: int = 0) -> dict:
    seeds = jax.random.split(jax.random.key(seed), 16)
    return {
        "layer_input": scatter_about(seeds[0], (D, TOKENS), 1.0, 6.0, ((0, 32), (1, 4))),
        "cotangent": scatter_about(seeds[1], (D, TOKENS), 1.0, 6.0, ((0, 32), (1, 4))),
        "segments": draw_segments(jax.random.fold_in(seeds[15], 71), 0),
        "qkv_weight": scatter_about(seeds[3], (D, 3, D), D ** -0.5, 0.1875, ((0, 4), (2, 32))),
        "qv_bias": scatter_about(seeds[4], (2, D), 0.2, 1.0, ((1, 32),)),
        "out_weight": scatter_about(seeds[5], (D, D), (D // 64) ** -0.5, 1.5, ((0, 4), (1, 32))),
        "out_bias": scatter_about(seeds[6], (D,), 0.2, 1.0, ((0, 32),)),
        "up_weight": scatter_about(seeds[7], (D, FF), D ** -0.5, 0.1875, ((0, 4), (1, 32))),
        "up_bias": scatter_about(seeds[8], (FF,), 0.2, 1.0, ((0, 32),)),
        "down_weight": scatter_about(seeds[9], (FF, D), FF ** -0.5, 0.09375, ((0, 32), (1, 4))),
        "down_bias": scatter_about(seeds[10], (D,), 0.2, 1.0, ((0, 32),)),
        "first_gain": jnp.clip(1.0 + 0.1 * jax.random.normal(seeds[11], (D,), jnp.float32), 0.5, 1.5).astype(jnp.bfloat16),
        "first_shift": scatter_about(seeds[12], (D,), 0.2, 1.0, ((0, 32),)),
        "second_gain": jnp.clip(1.0 + 0.1 * jax.random.normal(seeds[13], (D,), jnp.float32), 0.5, 1.5).astype(jnp.bfloat16),
        "second_shift": scatter_about(seeds[14], (D,), 0.2, 1.0, ((0, 32),)),
    }


@jax.custom_vjp
def low(v):
    return lax.optimization_barrier(v.astype(jnp.bfloat16)).astype(jnp.float32)

@jax.custom_vjp
def low_back(v):
    return v

def low_keep(v):
    return (low(v), None)

def low_pass(kept, grad):
    return (grad,)

def back_keep(v):
    return (v, None)

def back_low(kept, grad):
    return (low(grad),)
low.defvjp(low_keep, low_pass)
low_back.defvjp(back_keep, back_low)
highest = lax.Precision.HIGHEST

def layer_norm(rows_in, gain_row, shift_row):
    row_mean = lax.optimization_barrier(jnp.mean(rows_in, -1, keepdims=True))
    centred = rows_in - row_mean
    variance = lax.optimization_barrier(jnp.mean(centred * centred, -1, keepdims=True))
    return centred * lax.rsqrt(variance + 1e-05) * gain_row + shift_row

def attend_sequence(slot_pair):
    seq_qkv, seq_segs = slot_pair
    query_rows = seq_qkv[:, 0]
    key_rows = seq_qkv[:, 1]
    value_rows = seq_qkv[:, 2]
    scaling = HD ** (-0.5)
    scores = jnp.einsum('qhd,khd->hqk', query_rows, key_rows, precision=highest) * scaling
    scores = low_back(scores)
    positions = jnp.arange(LEN)
    allowed = (positions[None, :] <= positions[:, None]) & (seq_segs[None, :] == seq_segs[:, None])
    scores = jnp.where(allowed[None], scores, -1e+30)
    row_max = lax.optimization_barrier(jnp.max(scores, -1, keepdims=True))
    exponents = jnp.exp(scores - row_max)
    weights = low(exponents / lax.optimization_barrier(jnp.sum(exponents, -1, keepdims=True)))
    result = jnp.einsum('hqk,khd->qhd', weights, value_rows, precision=highest)
    return low(low_back(result))

def forward(layer_input, qkv_weight, qv_bias, out_weight, out_bias, up_weight, up_bias, down_weight, down_bias, first_gain, first_shift, second_gain, second_shift, segments):
    normed_first = low(layer_norm(layer_input, first_gain, first_shift))
    bias_three = jnp.stack([qv_bias[0], jnp.zeros_like(qv_bias[0]), qv_bias[1]])
    qkv = jnp.einsum('td,dje->tje', normed_first, qkv_weight, precision=highest) + bias_three
    qkv = low(low_back(qkv))
    qkv_seq = qkv.reshape(SEQS, LEN, 3, HEADS, HD)
    attn = lax.map(jax.checkpoint(attend_sequence), (qkv_seq, segments))
    attn = attn.reshape(SEQS * LEN, HEADS * HD)
    projected = low_back(jnp.dot(attn, out_weight, precision=highest) + out_bias)
    resid = layer_input + projected
    normed_second = low(layer_norm(resid, second_gain, second_shift))
    hidden = low_back(jnp.dot(normed_second, up_weight, precision=highest) + up_bias)
    active = low(jax.nn.gelu(hidden, approximate=True))
    return resid + jnp.dot(active, down_weight, precision=highest) + down_bias

def reference(layer_input, cotangent, segments, qkv_weight, qv_bias, out_weight, out_bias, up_weight, up_bias, down_weight, down_bias, first_gain, first_shift, second_gain, second_shift):
    params = (layer_input.T, qkv_weight, qv_bias, out_weight, out_bias, up_weight, up_bias, down_weight, down_bias, first_gain, first_shift, second_gain, second_shift)
    params = tuple((p.astype(jnp.float32) for p in params))

    def wrapped(*args):
        return forward(*args, segments)
    layer_output, backward = jax.vjp(wrapped, *params)
    grads = backward(cotangent.astype(jnp.float32).T)
    return (layer_output.T, grads[0].T, grads[1], grads[2], grads[3], grads[4], grads[5], grads[6], grads[7], grads[8], grads[9], grads[10], grads[11], grads[12])
```

```python
import functools

import jax
import jax.numpy as jnp
from jax import lax
from jax.experimental import pallas as pl
from jax.experimental.pallas import tpu as pltpu
from jax.sharding import Mesh, PartitionSpec as P

HEADS = 17
HD = 64
EPS = 1e-05
XY = ("x", "y")
COL = ("x", "y", "core")
F32 = jnp.float32
BF16 = jnp.bfloat16
QB = 256


def nn(a, b):
    return lax.dot_general(a, b, (((1,), (0,)), ((), ())), preferred_element_type=F32)


def nt(a, b):
    return lax.dot_general(a, b, (((1,), (1,)), ((), ())), preferred_element_type=F32)


def masked_scores(k, q_block, seg_col, seg_row, start, keys):
    scores = nn(k[:keys], q_block)
    key_pos = lax.broadcasted_iota(jnp.int32, scores.shape, 0)
    query_pos = lax.broadcasted_iota(jnp.int32, scores.shape, 1) + start
    allowed = (key_pos <= query_pos) & (seg_col[:keys] == seg_row[:, start : start + QB])
    return jnp.where(allowed, scores, -1e30)


def attend_kernel(count_ref, qkv_ref, seg_row_ref, seg_col_ref, out_ref, lse_ref):
    valid = pl.program_id(0) < count_ref[0]

    @pl.when(valid)
    def _():
        q = qkv_ref[0, 0] * (HD**-0.5)
        k = qkv_ref[0, 1].T
        v = qkv_ref[0, 2]
        length = q.shape[1]
        for start in range(0, length, QB):
            keys = start + QB
            scores = masked_scores(
                k, q[:, start:keys], seg_col_ref[...], seg_row_ref[...], start, keys
            )
            top = jnp.max(scores, 0, keepdims=True)
            weights = jnp.exp(scores - top)
            total = jnp.sum(weights, 0, keepdims=True)
            result = nn(v[:, :keys], weights.astype(BF16)) * (1.0 / total)
            out_ref[0, :, start:keys] = result.astype(BF16)
            lse_ref[0, :, start:keys] = top + jnp.log(total)

    @pl.when(jnp.logical_not(valid))
    def _():
        out_ref[...] = jnp.zeros_like(out_ref)
        lse_ref[...] = jnp.zeros_like(lse_ref)


def attend_back_kernel(
    count_ref, qkv_ref, seg_row_ref, seg_col_ref, out_ref, lse_ref, grad_ref, dqkv_ref, dk_ref, dv_ref
):
    valid = pl.program_id(0) < count_ref[0]

    @pl.when(valid)
    def _():
        q = qkv_ref[0, 0] * (HD**-0.5)
        key_cols = qkv_ref[0, 1]
        k = key_cols.T
        v = qkv_ref[0, 2].T
        grad = grad_ref[0]
        length = q.shape[1]
        delta = jnp.sum(grad.astype(F32) * out_ref[0].astype(F32), 0, keepdims=True)
        dk_ref[...] = jnp.zeros_like(dk_ref)
        dv_ref[...] = jnp.zeros_like(dv_ref)
        for start in range(0, length, QB):
            keys = start + QB
            scores = masked_scores(
                k, q[:, start:keys], seg_col_ref[...], seg_row_ref[...], start, keys
            )
            weights = jnp.exp(scores - lse_ref[0, :, start:keys])
            dweights = nn(v[:keys], grad[:, start:keys])
            dscores = (weights * (dweights - delta[:, start:keys])).astype(BF16)
            dq = nn(key_cols[:, :keys], dscores) * (HD**-0.5)
            dqkv_ref[0, 0, :, start:keys] = dq.astype(BF16)
            dk_ref[:, :keys] += nt(q[:, start:keys], dscores)
            dv_ref[:, :keys] += nt(grad[:, start:keys], weights.astype(BF16))
        dqkv_ref[0, 1] = dk_ref[...].astype(BF16)
        dqkv_ref[0, 2] = dv_ref[...].astype(BF16)

    @pl.when(jnp.logical_not(valid))
    def _():
        dqkv_ref[...] = jnp.zeros_like(dqkv_ref)


def slot_spec(*dims):
    return pl.BlockSpec((1,) + dims, lambda s: (s,) + (0,) * len(dims))


def whole_spec(*dims):
    return pl.BlockSpec(dims, lambda s: (0,) * len(dims))


def attend(count, qkv, seg_row, seg_col):
    slots, _, _, length = qkv.shape
    return pl.pallas_call(
        attend_kernel,
        grid=(slots,),
        in_specs=[
            pl.BlockSpec(memory_space=pltpu.SMEM),
            slot_spec(3, HD, length),
            whole_spec(1, length),
            whole_spec(length, 1),
        ],
        out_specs=[slot_spec(HD, length), slot_spec(1, length)],
        out_shape=[
            jax.ShapeDtypeStruct((slots, HD, length), BF16),
            jax.ShapeDtypeStruct((slots, 1, length), F32),
        ],
        compiler_params=pltpu.CompilerParams(vmem_limit_bytes=40 * 2**20),
    )(count, qkv, seg_row, seg_col)


def attend_back(count, qkv, seg_row, seg_col, out, lse, grad):
    slots, _, _, length = qkv.shape
    return pl.pallas_call(
        attend_back_kernel,
        grid=(slots,),
        in_specs=[
            pl.BlockSpec(memory_space=pltpu.SMEM),
            slot_spec(3, HD, length),
            whole_spec(1, length),
            whole_spec(length, 1),
            slot_spec(HD, length),
            slot_spec(1, length),
            slot_spec(HD, length),
        ],
        out_specs=slot_spec(3, HD, length),
        out_shape=jax.ShapeDtypeStruct((slots, 3, HD, length), BF16),
        scratch_shapes=[pltpu.VMEM((HD, length), F32), pltpu.VMEM((HD, length), F32)],
        compiler_params=pltpu.CompilerParams(vmem_limit_bytes=40 * 2**20),
    )(count, qkv, seg_row, seg_col, out, lse, grad)


def norm(v, gain, shift):
    centred = v - jnp.mean(v, 0, keepdims=True)
    inv_std = lax.rsqrt(jnp.mean(centred * centred, 0, keepdims=True) + EPS)
    standard = centred * inv_std
    return (standard * gain + shift).astype(BF16), standard, inv_std


def norm_back(dn, standard, inv_std, gain):
    dv = dn * gain
    back = inv_std * (
        dv - jnp.mean(dv, 0, keepdims=True) - standard * jnp.mean(dv * standard, 0, keepdims=True)
    )
    return back, jnp.sum(dn * standard, 1), jnp.sum(dn, 1)


def to_heads(v, core):
    n, _, tokens = v.shape
    heads = v.reshape(n, HEADS, HD, tokens).transpose(1, 0, 2, 3)
    pairs = heads[:16].reshape(2, 4, 2, n, HD, tokens)
    mine = lax.dynamic_index_in_dim(pairs, core, 2, keepdims=False)
    last = jnp.broadcast_to(heads[16:], (4, n, HD, tokens))
    return jnp.concatenate([mine.transpose(1, 0, 2, 3, 4), last[:, None]], 1)


def swap_heads(send):
    got = lax.all_to_all(send, "y", split_axis=0, concat_axis=0, tiled=True)
    _, slots, n, _, tokens = got.shape
    return got.transpose(1, 2, 3, 0, 4).reshape(slots, n, HD, 4 * tokens)


def from_heads(v):
    slots, n, _, length = v.shape
    send = v.reshape(slots, n, HD, 4, length // 4).transpose(3, 0, 1, 2, 4)
    send = jnp.repeat(send, 2, axis=0)
    got = lax.all_to_all(send, ("y", "core"), split_axis=0, concat_axis=0, tiled=True)
    got = got.transpose(2, 1, 0, 3, 4).reshape(n, slots * 8, HD, length // 4)
    return got[:, :HEADS].reshape(n, HEADS * HD, length // 4)


def shards(
    layer_input,
    cotangent,
    segments,
    qkv_weight,
    qv_bias,
    out_weight,
    out_bias,
    up_weight,
    up_bias,
    down_weight,
    down_bias,
    first_gain,
    first_shift,
    second_gain,
    second_shift,
):
    ix, iy, core = lax.axis_index("x"), lax.axis_index("y"), lax.axis_index("core")
    width = layer_input.shape[0]
    rows = qkv_weight.shape[0]
    full = 4 * rows
    units = up_weight.shape[1]

    small = jnp.concatenate(
        [qv_bias, jnp.stack([out_bias, first_gain, first_shift, second_gain, second_shift])], 0
    ).reshape(1, 7 * width)
    block = jnp.concatenate(
        [
            qkv_weight.transpose(1, 2, 0).reshape(3 * width, rows),
            jnp.pad(small, ((0, 0), (0, rows - 7 * width))),
            jnp.pad(up_bias[None], ((0, 0), (0, rows - units))),
            out_weight.T,
            jnp.zeros((6, rows), BF16),
            up_weight.T,
            down_weight,
        ],
        0,
    )
    block = lax.all_gather(block, "row", axis=0).transpose(1, 0, 2).reshape(-1, full)
    attn_w = lax.all_gather(block[:144], COL, axis=0)
    up_w = lax.all_gather(block[144:280], XY, axis=0)
    down_w = lax.all_gather(block[280:], XY, axis=0)

    both = jnp.concatenate([layer_input, cotangent], 0).reshape(2 * width, 16, 256).transpose(1, 0, 2)
    got = lax.all_to_all(jnp.repeat(both, 2, axis=0), COL, split_axis=0, concat_axis=0, tiled=True)
    x_in = got[:, :width].reshape(full, 256).astype(F32)
    g_low = got[:, width:].reshape(full, 256)
    g = g_low.astype(F32)

    vectors = attn_w[:, 102, : 7 * width].reshape(32, 7, width).transpose(1, 0, 2).reshape(7, full, 1)
    vectors = vectors.astype(F32)
    q_bias, v_bias, o_bias, gain1, shift1, gain2, shift2 = (vectors[i] for i in range(7))
    hidden_bias = lax.dynamic_index_in_dim(
        attn_w[:, 103, :units].reshape(16, 2, units), core, 1, keepdims=False
    ).astype(F32)

    normed1, standard1, inv_std1 = norm(x_in, gain1, shift1)
    qkv = jnp.einsum("crd,dt->crt", attn_w[:, :102], normed1, preferred_element_type=F32)
    qkv = qkv.reshape(32, 3, width, 256).transpose(1, 0, 2, 3).reshape(3, full, 256)
    qkv = (qkv + jnp.stack([q_bias, jnp.zeros_like(q_bias), v_bias])).astype(BF16)

    seg = lax.dynamic_index_in_dim(segments, ix, 0, keepdims=False)
    seg_row, seg_col = seg[None], seg[:, None]
    count = jnp.where((iy == 0) & (core == 0), 3, 2).astype(jnp.int32).reshape(1)
    units_qkv = swap_heads(to_heads(qkv, core))
    units_out, lse = attend(count, units_qkv, seg_row, seg_col)
    attn = from_heads(units_out[:, None])[0]

    out_w = attn_w[:, 104:138]
    resid = (
        x_in
        + jnp.einsum("ced,dt->cet", out_w, attn, preferred_element_type=F32).reshape(full, 256)
        + o_bias
    )
    normed2, standard2, inv_std2 = norm(resid, gain2, shift2)
    hidden = jnp.einsum("xfd,dt->xft", up_w, normed2, preferred_element_type=F32) + hidden_bias[..., None]
    active, gelu_back = jax.vjp(lambda h: jax.nn.gelu(h, approximate=True), hidden)
    active = active.astype(BF16)
    down_part = jnp.einsum("xfd,xft->dt", down_w, active, preferred_element_type=F32)
    send_out = (down_part + jnp.where(core == 0, 1.0, 0.0) * resid).astype(BF16)
    got_out = lax.all_to_all(
        send_out.reshape(32, width, 256), COL, split_axis=0, concat_axis=0, tiled=True
    )
    layer_output = jnp.sum(got_out.reshape(16, 2, width, 256).astype(F32), 1)
    layer_output = layer_output.transpose(1, 0, 2).reshape(width, 4096)
    layer_output = layer_output + down_bias.astype(F32)[:, None]

    dactive = jnp.einsum("xfd,dt->xft", down_w, g_low, preferred_element_type=F32)
    dhidden = gelu_back(dactive)[0].astype(BF16)
    down_grad = jnp.einsum("xft,dt->xfd", active, g_low, preferred_element_type=F32).astype(BF16)
    up_grad = jnp.einsum("xft,dt->xfd", dhidden, normed2, preferred_element_type=F32).astype(BF16)
    upbias = jnp.sum(dhidden.astype(F32), -1)
    dn2 = jnp.einsum("xfd,xft->dt", up_w, dhidden, preferred_element_type=F32)
    dn2 = lax.psum(dn2, "core")
    back2, gain2_grad, shift2_grad = norm_back(dn2, standard2, inv_std2, gain2)
    dresid = g + back2
    dproj = dresid.astype(BF16)
    dattn = jnp.einsum(
        "ced,cet->dt", out_w, dproj.reshape(32, width, 256), preferred_element_type=F32
    ).astype(BF16)
    units_grad = swap_heads(to_heads(dattn[None], core))[:, 0]
    units_dqkv = attend_back(count, units_qkv, seg_row, seg_col, units_out, lse, units_grad)
    dqkv = from_heads(units_dqkv)
    by_block = dqkv.reshape(3, 32, width, 256).transpose(1, 0, 2, 3).reshape(32, 102, 256)
    dn1 = jnp.einsum("crd,crt->dt", attn_w[:, :102], by_block, preferred_element_type=F32)
    back1, gain1_grad, shift1_grad = norm_back(dn1, standard1, inv_std1, gain1)
    dqkv_sums = jnp.sum(dqkv.astype(F32), -1)
    vecs = jnp.stack(
        [
            dqkv_sums[0],
            dqkv_sums[2],
            jnp.sum(dproj.astype(F32), -1),
            jnp.sum(g, -1),
            gain1_grad,
            shift1_grad,
            gain2_grad,
            shift2_grad,
        ]
    ).reshape(8, 16, 2, width)
    vecs = lax.dynamic_index_in_dim(vecs, core, 2, keepdims=False).transpose(1, 0, 2).reshape(16, 8 * width)
    vecs = jnp.concatenate([vecs, upbias, jnp.zeros((16, 512 - 8 * width - units), F32)], 1)
    input_back = (dresid + back1).astype(BF16).reshape(16, 2, width, 256)
    input_back = lax.dynamic_index_in_dim(input_back, core, 1, keepdims=False)
    input_back = jnp.concatenate([input_back, vecs.astype(BF16).reshape(16, 2, 256)], 1)
    input_grad = lax.all_to_all(input_back, XY, split_axis=0, concat_axis=0, tiled=True)
    vecs = jnp.sum(input_grad[:, width:].reshape(16, 512).astype(F32), 0)
    vecs = lax.psum(vecs, "row")
    input_grad = input_grad[:, :width].transpose(1, 0, 2).reshape(width, 4096).astype(F32)

    mine = lax.dynamic_index_in_dim(by_block.reshape(16, 2, 102, 256), core, 1, keepdims=False)
    qkv_part = jnp.einsum("xrt,dt->xrd", mine, normed1, preferred_element_type=F32).astype(BF16)
    mine = lax.dynamic_index_in_dim(dproj.reshape(16, 2, width, 256), core, 1, keepdims=False)
    out_part = jnp.einsum("xrt,dt->xrd", mine, attn, preferred_element_type=F32).astype(BF16)
    attn_part = jnp.concatenate([qkv_part, out_part], 1)

    def scatter(part):
        return lax.psum_scatter(part, XY, scatter_dimension=0, tiled=False)

    sums = jnp.concatenate([scatter(attn_part), scatter(up_grad), scatter(down_grad)], 0)
    sums = sums.reshape(-1, 4, rows).transpose(1, 0, 2)
    sums = lax.psum_scatter(sums, "row", scatter_dimension=0, tiled=False).astype(F32)
    qkv_out = sums[:102].reshape(3, width, rows).transpose(2, 0, 1)
    out_out = sums[102:136].T
    up_out = sums[136:272].T
    down_out = sums[272:]

    small_out = vecs[: 8 * width].reshape(8, width)
    return (
        layer_output,
        input_grad,
        qkv_out,
        small_out[:2],
        out_out,
        small_out[2],
        up_out,
        vecs[8 * width : 8 * width + units],
        down_out,
        small_out[3],
        small_out[4],
        small_out[5],
        small_out[6],
        small_out[7],
    )


def solution(mesh):
    split = Mesh(mesh.devices.reshape(4, 4, 4, 2), ("row", "x", "y", "core"))
    vec = P(COL)
    return jax.shard_map(
        shards,
        mesh=split,
        in_specs=(
            P(COL, "row"),
            P(COL, "row"),
            P("row", None),
            P("row", None, COL),
            P(None, COL),
            P("row", COL),
            vec,
            P("row", COL),
            vec,
            P(COL, "row"),
            vec,
            vec,
            vec,
            vec,
            vec,
        ),
        out_specs=(
            P(COL, "row"),
            P(COL, "row"),
            P("row", None, COL),
            P(None, COL),
            P("row", COL),
            vec,
            P("row", COL),
            vec,
            P(COL, "row"),
            vec,
            vec,
            vec,
            vec,
            vec,
        ),
        check_vma=False,
    )
```

```python
import jax
import jax.numpy as jnp
from jax import lax
from jax.experimental import pallas as pl
from jax.experimental.pallas import tpu as pltpu
from jax.sharding import Mesh, PartitionSpec as P

HEADS = 17
HD = 64
EPS = 1e-05
XY = ("x", "y")
COL = ("x", "y", "core")
F32 = jnp.float32
BF16 = jnp.bfloat16
QB = 256


def nn(a, b):
    return lax.dot_general(a, b, (((1,), (0,)), ((), ())), preferred_element_type=F32)


def nt(a, b):
    return lax.dot_general(a, b, (((1,), (1,)), ((), ())), preferred_element_type=F32)


MESH = pl.DeviceIdType.MESH
ANY = pl.BlockSpec(memory_space=pl.ANY)
VMEM = pl.BlockSpec(memory_space=pltpu.VMEM)
DMA = pltpu.SemaphoreType.DMA


def params(collective_id, vmem=56):
    return pltpu.CompilerParams(
        collective_id=collective_id, has_side_effects=True, vmem_limit_bytes=vmem * 2**20
    )


def remote(src, dst, send_sem, recv_sem, where):
    return pltpu.make_async_remote_copy(
        src_ref=src,
        dst_ref=dst,
        send_sem=send_sem,
        recv_sem=recv_sem,
        device_id=where,
        device_id_type=MESH,
    )


def signal(where):
    pl.semaphore_signal(
        pltpu.get_barrier_semaphore(), inc=1, device_id=where, device_id_type=MESH
    )


def col_place():
    return (lax.axis_index("x") * 4 + lax.axis_index("y")) * 2 + lax.axis_index("core")


def col_device(place):
    return {"x": place // 8, "y": place // 2 % 4, "core": place % 2}


def greet_col():
    me = col_place()

    def greet(step, _):
        signal(col_device((me + step) % 32))
        return 0

    lax.fori_loop(1, 32, greet, 0)
    return me


def rows_of(n):
    return pl.ds(pl.multiple_of(n, 256), 256)


def enter_kernel(both, block, both_out, block_out, send, recv, zsend, zrecv, local):
    me = greet_col()
    iz = lax.axis_index("row")
    for step in range(1, 4):
        signal({"row": (iz + step) % 4})
    pl.semaphore_wait(pltpu.get_barrier_semaphore(), 34)

    def zcopy(step, owner):
        return remote(
            block, block_out.at[owner], zsend.at[step - 1], zrecv.at[step - 1], {"row": (iz + step) % 4}
        )

    def copy(step, owner):
        peer = (me + step) % 32
        return remote(
            both.at[:, rows_of(peer // 2 * 256)],
            both_out.at[owner],
            send.at[step],
            recv.at[step],
            col_device(peer),
        )

    for step in range(1, 4):
        zcopy(step, iz).start()

    def begin(step, _):
        copy(step, me).start()
        return 0

    lax.fori_loop(1, 32, begin, 0)
    own = pltpu.make_async_copy(both.at[:, rows_of(me // 2 * 256)], both_out.at[me], local.at[0])
    own_z = pltpu.make_async_copy(block, block_out.at[iz], local.at[1])
    own.start()
    own_z.start()
    own.wait()
    own_z.wait()
    for step in range(1, 4):
        zcopy(step, (iz + 4 - step) % 4).wait()

    def end(step, _):
        copy(step, (me + 32 - step) % 32).wait()
        return 0

    lax.fori_loop(1, 32, end, 0)


def enter(both, block):
    return pl.pallas_call(
        enter_kernel,
        in_specs=[ANY, ANY],
        out_specs=[ANY, ANY],
        out_shape=[
            jax.ShapeDtypeStruct((32, both.shape[0], 256), both.dtype),
            jax.ShapeDtypeStruct((4,) + block.shape, block.dtype),
        ],
        scratch_shapes=[DMA((32,)), DMA((32,)), DMA((3,)), DMA((3,)), DMA((2,))],
        compiler_params=params(0),
    )(both, block)


ATTN_ROWS = 144
FF_ROWS = 272
FLOWS = ((0, 0, 80, 32), (0, 80, 64, 32), (1, 0, 128, 64), (1, 128, 144, 64))


def ring(axis, step):
    return {axis: (lax.axis_index(axis) + 4 + step) % 4}


def greet_rings(*others):
    for axis in XY:
        for step in (1, -1):
            signal(ring(axis, step))
    for where in others:
        signal(where)
    pl.semaphore_wait(pltpu.get_barrier_semaphore(), 4 + len(others))


def gather_kernel(block, attn_out, ff_out, send, recv, core_send, core_recv, local):
    ix, iy, core = (lax.axis_index(a) for a in COL)
    partner = {"core": 1 - core}
    greet_rings(partner)

    def place(flow, x, y, row=0, rows=None):
        ff, first, count, _ = FLOWS[flow]
        window = pl.ds(first + row, count if rows is None else rows)
        return ff_out.at[x, y, window] if ff else attn_out.at[x, y, core, window]

    def region(flow, stage, owner, half=None):
        by_x = (flow % 2 == 0) == (stage == 0)
        if stage == 0:
            _, _, count, cut = FLOWS[flow]
            row, rows = ((0, count), (0, cut), (cut, count - cut))[0 if half is None else half + 1]
            return place(flow, owner if by_x else ix, iy if by_x else owner, row, rows)
        part = pl.ds(0, 4) if half is None else pl.ds(2 * half, 2)
        return place(flow, owner if by_x else part, part if by_x else owner)

    def axis_of(flow, stage):
        return "x" if (flow % 2 == 0) == (stage == 0) else "y"

    def copy(flow, stage, kind, src_owner, dst_owner):
        half = None if kind < 2 else kind - 2
        if stage == 0 and kind < 2:
            ff, first, count, _ = FLOWS[flow]
            src = block.at[pl.ds(ff * ATTN_ROWS + first, count)]
        else:
            src = region(flow, stage, src_owner, half)
        return remote(
            src,
            region(flow, stage, dst_owner, half),
            send.at[flow, stage, kind],
            recv.at[flow, stage, kind],
            ring(axis_of(flow, stage), 1 if kind % 2 == 0 else -1),
        )

    def at(flow, stage, step):
        return (lax.axis_index(axis_of(flow, stage)) + 4 + step) % 4

    for flow in range(4):
        for kind in range(2):
            copy(flow, 0, kind, at(flow, 0, 0), at(flow, 0, 0)).start()
    own = [
        pltpu.make_async_copy(block.at[pl.ds(0, ATTN_ROWS)], attn_out.at[ix, iy, core], local.at[0]),
        pltpu.make_async_copy(block.at[pl.ds(ATTN_ROWS, FF_ROWS)], ff_out.at[ix, iy], local.at[1]),
    ]
    for c in own:
        c.start()
    for c in own:
        c.wait()
    for stage in range(2):
        for flow in range(4):
            for kind in range(2):
                src = at(flow, stage, -1 if kind == 0 else 1)
                copy(flow, stage, kind, src, src).wait_recv()
                copy(flow, stage, kind + 2, src, src).start()
        for flow in range(4):
            far = at(flow, stage, 2)
            for kind in (2, 3):
                copy(flow, stage, kind, far, far).wait_recv()
            if stage == 0:
                me = at(flow, 1, 0)
                for kind in range(2):
                    copy(flow, 1, kind, me, me).start()
            elif flow == 1:
                swap = remote(
                    attn_out.at[:, :, core], attn_out.at[:, :, core], core_send, core_recv, partner
                )
                swap.start()
    for stage in range(2):
        for flow in range(4):
            for kind in range(4):
                me = at(flow, stage, 0)
                copy(flow, stage, kind, me, me).wait_send()
    swap.wait_send()
    remote(
        attn_out.at[:, :, 1 - core], attn_out.at[:, :, 1 - core], core_send, core_recv, partner
    ).wait_recv()


def gather_weights(block):
    full = block.shape[1]
    return pl.pallas_call(
        gather_kernel,
        in_specs=[ANY],
        out_specs=[ANY, ANY],
        out_shape=[
            jax.ShapeDtypeStruct((4, 4, 2, ATTN_ROWS, full), block.dtype),
            jax.ShapeDtypeStruct((4, 4, FF_ROWS, full), block.dtype),
        ],
        scratch_shapes=[DMA((4, 2, 4)), DMA((4, 2, 4)), DMA, DMA, DMA((2,))],
        compiler_params=params(1),
    )(block)


def add_rows(out, *terms):
    def one(i, _):
        out[i] = sum(t[i].astype(F32) for t in terms).astype(out.dtype)
        return 0

    lax.fori_loop(0, out.shape[0], one, 0)


def scatter_kernel(attn_in, ff_in, back, sums, back_out, *scratch):
    send, recv, bsend, brecv, local = scratch[:5]
    bufs = scratch[5:]
    ix, iy, core = (lax.axis_index(a) for a in COL)
    me = ix * 4 + iy

    def peer_at(step):
        return (me + step) % 16

    def greet(step, _):
        peer = peer_at(step)
        signal({"x": peer // 4, "y": peer % 4})
        return 0

    lax.fori_loop(1, 16, greet, 0)
    pl.semaphore_wait(pltpu.get_barrier_semaphore(), 15)

    def axis_of(flow, stage):
        return "y" if (flow % 2 == 0) == (stage == 0) else "x"

    def at(flow, stage, step):
        return (lax.axis_index(axis_of(flow, stage)) + 4 + step) % 4

    def held(flow, stage):
        return bufs[flow * 9 + stage * 5 : flow * 9 + stage * 5 + 5 - stage]

    def chunk(flow, stage, owner, half=None):
        ff, first, count, cut = FLOWS[flow]
        if stage == 1:
            row, rows = ((0, count), (0, cut), (cut, count - cut))[0 if half is None else half + 1]
            return held(flow, 0)[4].at[pl.ds(owner, 1), pl.ds(row, rows)]
        part = pl.ds(0, 4) if half is None else pl.ds(2 * half, 2)
        window = pl.ds(first, count)
        ref = ff_in if ff else attn_in
        return ref.at[part, owner, window] if axis_of(flow, 0) == "y" else ref.at[owner, part, window]

    def part_of(flow, stage, ref, half):
        if stage == 0:
            return ref.at[pl.ds(2 * half, 2)]
        _, _, count, cut = FLOWS[flow]
        return ref.at[:, pl.ds(0, cut) if half == 0 else pl.ds(cut, count - cut)]

    def copy(flow, stage, kind):
        from_left, from_right, all_left, all_right = held(flow, stage)[:4]
        right = kind % 2 == 0
        if kind < 2:
            src, dst = chunk(flow, stage, at(flow, stage, 2), kind), (from_left, from_right)[kind]
        elif kind < 4:
            src = chunk(flow, stage, at(flow, stage, 1 if right else -1), 1 if right else 0)
            dst = part_of(flow, stage, all_left if right else all_right, 1 if right else 0)
        else:
            src = from_left if right else from_right
            dst = part_of(flow, stage, all_left if right else all_right, 0 if right else 1)
        return remote(
            src,
            dst,
            send.at[flow, stage, kind],
            recv.at[flow, stage, kind],
            ring(axis_of(flow, stage), 1 if right else -1),
        )

    def copy_back(step, owner):
        peer = peer_at(step)
        return remote(
            back.at[peer],
            back_out.at[owner],
            bsend.at[step],
            brecv.at[step],
            {"x": peer // 4, "y": peer % 4},
        )

    def begin(flow, stage):
        for kind in (0, 1, 2, 3):
            copy(flow, stage, kind).start()

    def middle(flow, stage):
        from_left, from_right = held(flow, stage)[:2]
        for kind, buf, step in ((0, from_left, 1), (1, from_right, -1)):
            copy(flow, stage, kind).wait_recv()
            add_rows(buf, buf, chunk(flow, stage, at(flow, stage, step), kind))
            copy(flow, stage, kind + 4).start()

    def finish(flow, stage):
        all_left, all_right = held(flow, stage)[2:4]
        for kind in (2, 3, 4, 5):
            copy(flow, stage, kind).wait_recv()
        if stage == 0:
            out = held(flow, 0)[4]
        else:
            ff, first, count, _ = FLOWS[flow]
            out = sums.at[:, pl.ds(ff * ATTN_ROWS + first, count)]
        add_rows(out, chunk(flow, stage, at(flow, stage, 0)), all_left, all_right)

    order = (2, 3, 0, 1)
    for flow in order:
        begin(flow, 0)

    def begin_back(step, _):
        copy_back(step, me).start()
        return 0

    lax.fori_loop(1, 16, begin_back, 0)
    own = pltpu.make_async_copy(back.at[me], back_out.at[me], local)
    own.start()
    for flow in order:
        middle(flow, 0)
    for flow in order:
        finish(flow, 0)
        begin(flow, 1)
    for flow in order:
        middle(flow, 1)
    for flow in order:
        finish(flow, 1)
    for stage in range(2):
        for flow in order:
            for kind in range(6):
                copy(flow, stage, kind).wait_send()
    own.wait()

    def end_back(step, _):
        copy_back(step, (me + 16 - step) % 16).wait()
        return 0

    lax.fori_loop(1, 16, end_back, 0)


def scatter_grads(attn_part, ff_part, back):
    full = attn_part.shape[-1]
    bufs = []
    for _, _, count, cut in FLOWS:
        bufs += [(2, count), (2, count), (4, count), (4, count), (4, count)]
        bufs += [(1, cut), (1, count - cut), (1, count), (1, count)]
    return pl.pallas_call(
        scatter_kernel,
        in_specs=[VMEM, VMEM, ANY],
        out_specs=[VMEM, ANY],
        out_shape=[
            jax.ShapeDtypeStruct((1, ATTN_ROWS + FF_ROWS, full), BF16),
            jax.ShapeDtypeStruct(back.shape, BF16),
        ],
        scratch_shapes=[DMA((4, 2, 6)), DMA((4, 2, 6)), DMA((16,)), DMA((16,)), DMA]
        + [pltpu.VMEM((n, rows, full), BF16) for n, rows in bufs],
        compiler_params=params(2),
    )(attn_part, ff_part, back)


def z_kernel(part, vecs, part_out, vecs_out, send, recv, vsend, vrecv, local):
    iz = lax.axis_index("row")
    for step in range(1, 4):
        signal({"row": (iz + step) % 4})
    pl.semaphore_wait(pltpu.get_barrier_semaphore(), 3)

    def copies(step, owner):
        peer = (iz + step) % 4
        return (
            remote(part.at[peer], part_out.at[owner], send.at[step - 1], recv.at[step - 1], {"row": peer}),
            remote(vecs, vecs_out.at[owner], vsend.at[step - 1], vrecv.at[step - 1], {"row": peer}),
        )

    for step in range(1, 4):
        for c in copies(step, iz):
            c.start()
    own = [
        pltpu.make_async_copy(part.at[iz], part_out.at[iz], local.at[0]),
        pltpu.make_async_copy(vecs, vecs_out.at[iz], local.at[1]),
    ]
    for c in own:
        c.start()
    for c in own:
        c.wait()
    for step in range(1, 4):
        for c in copies(step, (iz + 4 - step) % 4):
            c.wait()


def z_swap(part, vecs):
    return pl.pallas_call(
        z_kernel,
        in_specs=[ANY, ANY],
        out_specs=[ANY, ANY],
        out_shape=[
            jax.ShapeDtypeStruct(part.shape, part.dtype),
            jax.ShapeDtypeStruct((4,) + vecs.shape, vecs.dtype),
        ],
        scratch_shapes=[DMA((3,)), DMA((3,)), DMA((3,)), DMA((3,)), DMA((2,))],
        compiler_params=params(3),
    )(part, vecs)


def core_kernel(mine, total, got, send, recv):
    partner = {"core": 1 - lax.axis_index("core")}
    signal(partner)
    pl.semaphore_wait(pltpu.get_barrier_semaphore(), 1)
    copy = remote(mine, got, send, recv, partner)
    copy.start()
    copy.wait()
    total[...] = mine[...] + got[...]


def core_sum(mine):
    return pl.pallas_call(
        core_kernel,
        in_specs=[VMEM],
        out_specs=VMEM,
        out_shape=jax.ShapeDtypeStruct(mine.shape, F32),
        scratch_shapes=[pltpu.VMEM(mine.shape, F32), DMA, DMA],
        compiler_params=params(4),
    )(mine)


def masked_scores(k, q_block, seg_col, seg_row, start, keys):
    scores = nn(k[:keys], q_block)
    key_pos = lax.broadcasted_iota(jnp.int32, scores.shape, 0)
    query_pos = lax.broadcasted_iota(jnp.int32, scores.shape, 1) + start
    allowed = (key_pos <= query_pos) & (seg_col[:keys] == seg_row[:, start : start + QB])
    return jnp.where(allowed, scores, -1e30)


def unit_place():
    return lax.axis_index("y") * 2 + lax.axis_index("core")


def unit_device(place):
    return {"y": place // 2, "core": place % 2}


def head_swap(send, units, sems, rsems):
    iy = lax.axis_index("y")

    def copy(slot, step, owner):
        return remote(
            send.at[(iy + step) % 4, slot],
            units.at[slot, :, :, rows_of(owner * 256)],
            sems.at[slot, step - 1],
            rsems.at[slot, step - 1],
            {"y": (iy + step) % 4},
        )

    def begin(slot):
        for step in range(1, 4):
            if slot < 2:
                copy(slot, step, iy).start()
            else:
                pl.when(((iy + step) % 4 == 0) & (lax.axis_index("core") == 0))(
                    lambda step=step: copy(2, step, iy).start()
                )

    def arrive(slot):
        units[slot, :, :, rows_of(iy * 256)] = send[iy, slot]
        for step in range(1, 4):
            copy(slot, step, (iy + 4 - step) % 4).wait_recv()

    def sent():
        for slot in range(2):
            for step in range(1, 4):
                copy(slot, step, iy).wait_send()
        for step in range(1, 4):
            pl.when(((iy + step) % 4 == 0) & (lax.axis_index("core") == 0))(
                lambda step=step: copy(2, step, iy).wait_send()
            )

    return begin, arrive, sent


def result_swap(units, got, sems, rsems):
    me = unit_place()

    def copy(slot, step, owner):
        peer = (me + step) % 8
        return remote(
            units.at[slot, :, :, rows_of(peer // 2 * 256)],
            got.at[owner, slot],
            sems.at[slot, step - 1],
            rsems.at[slot, step - 1],
            unit_device(peer),
        )

    def begin(slot):
        got[me, slot] = units[slot, :, :, rows_of(me // 2 * 256)]
        for step in range(1, 8):
            copy(slot, step, me).start()

    def finish(count):
        def slots(slot, _):
            for step in range(1, 8):
                copy(slot, step, (me + 8 - step) % 8).wait_recv()
            return 0

        lax.fori_loop(0, 2, slots, 0)
        for step in range(1, 8):
            pl.when((me + 8 - step) % 8 == 0)(lambda step=step: copy(2, step, 0).wait_recv())

        def ends(slot, _):
            for step in range(1, 8):
                copy(slot, step, me).wait_send()
            return 0

        lax.fori_loop(0, count, ends, 0)

    return begin, finish


def attend_kernel(send, seg_row_ref, seg_col_ref, qkv_ref, out_ref, lse_ref, got, *sems):
    me = unit_place()
    count = jnp.where(me == 0, 3, 2)
    for step in range(1, 8):
        signal(unit_device((me + step) % 8))
    pl.semaphore_wait(pltpu.get_barrier_semaphore(), 7)
    begin, arrive, sent = head_swap(send, qkv_ref, sems[0], sems[1])
    begin_result, finish = result_swap(out_ref, got, sems[2], sems[3])
    for slot in range(3):
        begin(slot)

    def unit(slot, _):
        arrive(slot)
        q = qkv_ref[slot, 0] * (HD**-0.5)
        k = qkv_ref[slot, 1].T
        v = qkv_ref[slot, 2]
        for start in range(0, q.shape[1], QB):
            keys = start + QB
            scores = masked_scores(
                k, q[:, start:keys], seg_col_ref[...], seg_row_ref[...], start, keys
            )
            top = jnp.max(scores, 0, keepdims=True)
            weights = jnp.exp(scores - top)
            total = jnp.sum(weights, 0, keepdims=True)
            result = nn(v[:, :keys], weights.astype(BF16)) * (1.0 / total)
            out_ref[slot, 0, :, start:keys] = result.astype(BF16)
            lse_ref[slot, :, start:keys] = top + jnp.log(total)
        begin_result(slot)
        return 0

    lax.fori_loop(0, count, unit, 0)
    sent()
    finish(count)


def attend(send, seg_row, seg_col):
    length = seg_row.shape[1]
    return pl.pallas_call(
        attend_kernel,
        in_specs=[VMEM] * 3,
        out_specs=[VMEM] * 4,
        out_shape=[
            jax.ShapeDtypeStruct((3, 3, HD, length), BF16),
            jax.ShapeDtypeStruct((3, 1, HD, length), BF16),
            jax.ShapeDtypeStruct((3, 1, length), F32),
            jax.ShapeDtypeStruct((8, 3, 1, HD, 256), BF16),
        ],
        scratch_shapes=[DMA((3, 3)), DMA((3, 3)), DMA((3, 7)), DMA((3, 7))],
        compiler_params=params(5, 40),
    )(send, seg_row, seg_col)


def attend_back_kernel(
    send,
    seg_row_ref,
    seg_col_ref,
    qkv_ref,
    out_ref,
    lse_ref,
    wide,
    got,
    wide_out,
    grad_ref,
    dqkv_ref,
    dk_ref,
    dv_ref,
    wsend,
    wrecv,
    local,
    *sems,
):
    place = greet_col()
    pl.semaphore_wait(pltpu.get_barrier_semaphore(), 31)
    me = unit_place()
    count = jnp.where(me == 0, 3, 2)
    begin, arrive, sent = head_swap(send, grad_ref, sems[0], sems[1])
    begin_result, finish = result_swap(dqkv_ref, got, sems[2], sems[3])
    for slot in range(3):
        begin(slot)

    def copy_wide(step, owner):
        peer = (place + step) % 32
        return remote(
            wide.at[peer], wide_out.at[owner], wsend.at[step], wrecv.at[step], col_device(peer)
        )

    def begin_wide(step, _):
        copy_wide(step, place).start()
        return 0

    lax.fori_loop(1, 32, begin_wide, 0)
    own = pltpu.make_async_copy(wide.at[place], wide_out.at[place], local)
    own.start()

    def unit(slot, _):
        arrive(slot)
        q = qkv_ref[slot, 0] * (HD**-0.5)
        key_cols = qkv_ref[slot, 1]
        k = key_cols.T
        v = qkv_ref[slot, 2].T
        grad = grad_ref[slot, 0]
        delta = jnp.sum(grad.astype(F32) * out_ref[slot, 0].astype(F32), 0, keepdims=True)
        dk_ref[...] = jnp.zeros_like(dk_ref)
        dv_ref[...] = jnp.zeros_like(dv_ref)
        for start in range(0, q.shape[1], QB):
            keys = start + QB
            scores = masked_scores(
                k, q[:, start:keys], seg_col_ref[...], seg_row_ref[...], start, keys
            )
            weights = jnp.exp(scores - lse_ref[slot, :, start:keys])
            dweights = nn(v[:keys], grad[:, start:keys])
            dscores = (weights * (dweights - delta[:, start:keys])).astype(BF16)
            dq = nn(key_cols[:, :keys], dscores) * (HD**-0.5)
            dqkv_ref[slot, 0, :, start:keys] = dq.astype(BF16)
            dk_ref[:, :keys] += nt(q[:, start:keys], dscores)
            dv_ref[:, :keys] += nt(grad[:, start:keys], weights.astype(BF16))
        dqkv_ref[slot, 1] = dk_ref[...].astype(BF16)
        dqkv_ref[slot, 2] = dv_ref[...].astype(BF16)
        begin_result(slot)
        return 0

    lax.fori_loop(0, count, unit, 0)
    sent()
    finish(count)
    own.wait()

    def end_wide(step, _):
        copy_wide(step, (place + 32 - step) % 32).wait()
        return 0

    lax.fori_loop(1, 32, end_wide, 0)


def attend_back(send, seg_row, seg_col, qkv, out, lse, wide):
    length = seg_row.shape[1]
    return pl.pallas_call(
        attend_back_kernel,
        in_specs=[VMEM] * 6 + [ANY],
        out_specs=[VMEM, ANY],
        out_shape=[
            jax.ShapeDtypeStruct((8, 3, 3, HD, 256), BF16),
            jax.ShapeDtypeStruct(wide.shape, wide.dtype),
        ],
        scratch_shapes=[
            pltpu.VMEM((3, 1, HD, length), BF16),
            pltpu.VMEM((3, 3, HD, length), BF16),
            pltpu.VMEM((HD, length), F32),
            pltpu.VMEM((HD, length), F32),
            DMA((32,)),
            DMA((32,)),
            DMA,
            DMA((3, 3)),
            DMA((3, 3)),
            DMA((3, 7)),
            DMA((3, 7)),
        ],
        compiler_params=params(6, 40),
    )(send, seg_row, seg_col, qkv, out, lse, wide)


def norm(v, gain, shift):
    centred = v - jnp.mean(v, 0, keepdims=True)
    inv_std = lax.rsqrt(jnp.mean(centred * centred, 0, keepdims=True) + EPS)
    standard = centred * inv_std
    return (standard * gain + shift).astype(BF16), standard, inv_std


def norm_back(dn, standard, inv_std, gain):
    dv = dn * gain
    back = inv_std * (
        dv - jnp.mean(dv, 0, keepdims=True) - standard * jnp.mean(dv * standard, 0, keepdims=True)
    )
    return back, jnp.sum(dn * standard, 1), jnp.sum(dn, 1)


def to_heads(v, core):
    n, _, tokens = v.shape
    heads = v.reshape(n, HEADS, HD, tokens).transpose(1, 0, 2, 3)
    pairs = heads[:16].reshape(2, 4, 2, n, HD, tokens)
    mine = lax.dynamic_index_in_dim(pairs, core, 2, keepdims=False)
    last = jnp.broadcast_to(heads[16:], (4, n, HD, tokens))
    return jnp.concatenate([mine.transpose(1, 0, 2, 3, 4), last[:, None]], 1)


def from_heads(got):
    _, slots, n, _, tokens = got.shape
    got = got.transpose(2, 1, 0, 3, 4).reshape(n, slots * 8, HD, tokens)
    return got[:, :HEADS].reshape(n, HEADS * HD, tokens)


def shards(
    layer_input,
    cotangent,
    segments,
    qkv_weight,
    qv_bias,
    out_weight,
    out_bias,
    up_weight,
    up_bias,
    down_weight,
    down_bias,
    first_gain,
    first_shift,
    second_gain,
    second_shift,
):
    ix, iy, core = lax.axis_index("x"), lax.axis_index("y"), lax.axis_index("core")
    width = layer_input.shape[0]
    rows = qkv_weight.shape[0]
    full = 4 * rows
    units = up_weight.shape[1]

    small = jnp.concatenate(
        [qv_bias, jnp.stack([out_bias, first_gain, first_shift, second_gain, second_shift])], 0
    ).reshape(1, 7 * width)
    block = jnp.concatenate(
        [
            qkv_weight.transpose(1, 2, 0).reshape(3 * width, rows),
            jnp.pad(small, ((0, 0), (0, rows - 7 * width))),
            jnp.pad(up_bias[None], ((0, 0), (0, rows - units))),
            out_weight.T,
            jnp.zeros((6, rows), BF16),
            up_weight.T,
            down_weight,
        ],
        0,
    )
    both = jnp.concatenate([layer_input, cotangent, jnp.zeros((12, 4096), BF16)], 0)
    got, blocks = enter(both, block)
    block = blocks.transpose(1, 0, 2).reshape(-1, full)
    attn_w, ff_w = gather_weights(block)
    attn_w = attn_w.reshape(32, ATTN_ROWS, full)
    ff_w = ff_w.reshape(16, FF_ROWS, full)
    up_w = ff_w[:, :units]
    down_w = ff_w[:, units:]
    x_in = got[:, :width].reshape(full, 256).astype(F32)
    g_low = got[:, width : 2 * width].reshape(full, 256)
    g = g_low.astype(F32)

    vectors = attn_w[:, 102, : 7 * width].reshape(32, 7, width).transpose(1, 0, 2).reshape(7, full, 1)
    vectors = vectors.astype(F32)
    q_bias, v_bias, o_bias, gain1, shift1, gain2, shift2 = (vectors[i] for i in range(7))
    hidden_bias = lax.dynamic_index_in_dim(
        attn_w[:, 103, :units].reshape(16, 2, units), core, 1, keepdims=False
    ).astype(F32)

    normed1, standard1, inv_std1 = norm(x_in, gain1, shift1)
    qkv = jnp.einsum("crd,dt->crt", attn_w[:, :102], normed1, preferred_element_type=F32)
    qkv = qkv.reshape(32, 3, width, 256).transpose(1, 0, 2, 3).reshape(3, full, 256)
    qkv = (qkv + jnp.stack([q_bias, jnp.zeros_like(q_bias), v_bias])).astype(BF16)

    seg = lax.dynamic_index_in_dim(segments, ix, 0, keepdims=False)
    seg_row, seg_col = seg[None], seg[:, None]
    units_qkv, units_out, lse, attn_got = attend(to_heads(qkv, core), seg_row, seg_col)
    attn = from_heads(attn_got)[0]

    out_w = attn_w[:, 104:138]
    resid = (
        x_in
        + jnp.einsum("ced,dt->cet", out_w, attn, preferred_element_type=F32).reshape(full, 256)
        + o_bias
    )
    normed2, standard2, inv_std2 = norm(resid, gain2, shift2)
    hidden = jnp.einsum("xfd,dt->xft", up_w, normed2, preferred_element_type=F32) + hidden_bias[..., None]
    active, gelu_back = jax.vjp(lambda h: jax.nn.gelu(h, approximate=True), hidden)
    active = active.astype(BF16)
    down_part = jnp.einsum("xfd,xft->dt", down_w, active, preferred_element_type=F32)
    send_out = (down_part + jnp.where(core == 0, 1.0, 0.0) * resid).astype(BF16)
    send_out = jnp.pad(send_out.reshape(32, width, 256), ((0, 0), (0, 48 - width), (0, 0)))
    dactive = jnp.einsum("xfd,dt->xft", down_w, g_low, preferred_element_type=F32)
    dhidden = gelu_back(dactive)[0].astype(BF16)
    down_grad = jnp.einsum("xft,dt->xfd", active, g_low, preferred_element_type=F32).astype(BF16)
    up_grad = jnp.einsum("xft,dt->xfd", dhidden, normed2, preferred_element_type=F32).astype(BF16)
    upbias = jnp.sum(dhidden.astype(F32), -1)
    dn2 = jnp.einsum("xfd,xft->dt", up_w, dhidden, preferred_element_type=F32)
    dn2 = core_sum(dn2)
    back2, gain2_grad, shift2_grad = norm_back(dn2, standard2, inv_std2, gain2)
    dresid = g + back2
    dproj = dresid.astype(BF16)
    dattn = jnp.einsum(
        "ced,cet->dt", out_w, dproj.reshape(32, width, 256), preferred_element_type=F32
    ).astype(BF16)
    dqkv_got, got_out = attend_back(
        to_heads(dattn[None], core), seg_row, seg_col, units_qkv, units_out, lse, send_out
    )
    layer_output = jnp.sum(got_out[:, :width].reshape(16, 2, width, 256).astype(F32), 1)
    layer_output = layer_output.transpose(1, 0, 2).reshape(width, 4096)
    layer_output = layer_output + down_bias.astype(F32)[:, None]
    dqkv = from_heads(dqkv_got)
    by_block = dqkv.reshape(3, 32, width, 256).transpose(1, 0, 2, 3).reshape(32, 102, 256)
    dn1 = jnp.einsum("crd,crt->dt", attn_w[:, :102], by_block, preferred_element_type=F32)
    back1, gain1_grad, shift1_grad = norm_back(dn1, standard1, inv_std1, gain1)
    dqkv_sums = jnp.sum(dqkv.astype(F32), -1)
    vecs = jnp.stack(
        [
            dqkv_sums[0],
            dqkv_sums[2],
            jnp.sum(dproj.astype(F32), -1),
            jnp.sum(g, -1),
            gain1_grad,
            shift1_grad,
            gain2_grad,
            shift2_grad,
        ]
    ).reshape(8, 16, 2, width)
    vecs = lax.dynamic_index_in_dim(vecs, core, 2, keepdims=False).transpose(1, 0, 2).reshape(16, 8 * width)
    vecs = jnp.concatenate([vecs, upbias, jnp.zeros((16, 512 - 8 * width - units), F32)], 1)
    input_back = (dresid + back1).astype(BF16).reshape(16, 2, width, 256)
    input_back = lax.dynamic_index_in_dim(input_back, core, 1, keepdims=False)
    input_back = jnp.concatenate(
        [input_back, vecs.astype(BF16).reshape(16, 2, 256), jnp.zeros((16, 12, 256), BF16)], 1
    )

    mine = lax.dynamic_index_in_dim(by_block.reshape(16, 2, 102, 256), core, 1, keepdims=False)
    qkv_part = jnp.einsum("xrt,dt->xrd", mine, normed1, preferred_element_type=F32).astype(BF16)
    mine = lax.dynamic_index_in_dim(dproj.reshape(16, 2, width, 256), core, 1, keepdims=False)
    out_part = jnp.einsum("xrt,dt->xrd", mine, attn, preferred_element_type=F32).astype(BF16)
    attn_part = jnp.concatenate([qkv_part, out_part, jnp.zeros((16, 8, full), BF16)], 1)
    ff_part = jnp.concatenate([up_grad, down_grad], 1)
    sums, input_got = scatter_grads(
        attn_part.reshape(4, 4, ATTN_ROWS, full), ff_part.reshape(4, 4, FF_ROWS, full), input_back
    )
    input_grad = input_got[:, :width].transpose(1, 0, 2).reshape(width, 4096).astype(F32)
    vecs = jnp.sum(input_got[:, width : width + 2].astype(F32), 0)
    sums = sums.reshape(-1, 4, rows).transpose(1, 0, 2)
    sums, vecs = z_swap(sums, vecs)
    sums = jnp.sum(sums.astype(F32), 0)
    vecs = jnp.sum(vecs, 0).reshape(512)
    qkv_out = sums[:102].reshape(3, width, rows).transpose(2, 0, 1)
    out_out = sums[102:136].T
    up_out = sums[144:280].T
    down_out = sums[280:]

    small_out = vecs[: 8 * width].reshape(8, width)
    return (
        layer_output,
        input_grad,
        qkv_out,
        small_out[:2],
        out_out,
        small_out[2],
        up_out,
        vecs[8 * width : 8 * width + units],
        down_out,
        small_out[3],
        small_out[4],
        small_out[5],
        small_out[6],
        small_out[7],
    )


def solution(mesh):
    split = Mesh(mesh.devices.reshape(4, 4, 4, 2), ("row", "x", "y", "core"))
    vec = P(COL)
    return jax.shard_map(
        shards,
        mesh=split,
        in_specs=(
            P(COL, "row"),
            P(COL, "row"),
            P("row", None),
            P("row", None, COL),
            P(None, COL),
            P("row", COL),
            vec,
            P("row", COL),
            vec,
            P(COL, "row"),
            vec,
            vec,
            vec,
            vec,
            vec,
        ),
        out_specs=(
            P(COL, "row"),
            P(COL, "row"),
            P("row", None, COL),
            P(None, COL),
            P("row", COL),
            vec,
            P("row", COL),
            vec,
            P(COL, "row"),
            vec,
            vec,
            vec,
            vec,
            vec,
        ),
        check_vma=False,
    )
```

```python
import jax
import jax.numpy as jnp
from jax import lax
from jax.experimental import pallas as pl
from jax.experimental.pallas import tpu as pltpu
from jax.sharding import Mesh, PartitionSpec as P

HEADS = 17
HD = 64
EPS = 1e-05
XY = ("x", "y")
COL = ("x", "y", "core")
F32 = jnp.float32
BF16 = jnp.bfloat16
QB = 256


def nn(a, b):
    return lax.dot_general(a, b, (((1,), (0,)), ((), ())), preferred_element_type=F32)


def nt(a, b):
    return lax.dot_general(a, b, (((1,), (1,)), ((), ())), preferred_element_type=F32)


MESH = pl.DeviceIdType.MESH
ANY = pl.BlockSpec(memory_space=pl.ANY)
VMEM = pl.BlockSpec(memory_space=pltpu.VMEM)
DMA = pltpu.SemaphoreType.DMA


def params(collective_id, vmem=56):
    return pltpu.CompilerParams(
        collective_id=collective_id, has_side_effects=True, vmem_limit_bytes=vmem * 2**20
    )


def remote(src, dst, send_sem, recv_sem, where):
    return pltpu.make_async_remote_copy(
        src_ref=src,
        dst_ref=dst,
        send_sem=send_sem,
        recv_sem=recv_sem,
        device_id=where,
        device_id_type=MESH,
    )


def signal(where):
    pl.semaphore_signal(
        pltpu.get_barrier_semaphore(), inc=1, device_id=where, device_id_type=MESH
    )


def col_place():
    return (lax.axis_index("x") * 4 + lax.axis_index("y")) * 2 + lax.axis_index("core")


def col_device(place):
    return {"x": place // 8, "y": place // 2 % 4, "core": place % 2}


def greet_col():
    me = col_place()

    def greet(step, _):
        signal(col_device((me + step) % 32))
        return 0

    lax.fori_loop(1, 32, greet, 0)
    return me


def rows_of(n):
    return pl.ds(pl.multiple_of(n, 256), 256)


def token_swap(src, out, send, recv, local, me):
    def copy(step, owner):
        peer = (me + step) % 32
        return remote(
            src.at[:, rows_of(peer // 2 * 256)], out.at[owner], send.at[step], recv.at[step], col_device(peer)
        )

    own = pltpu.make_async_copy(src.at[:, rows_of(me // 2 * 256)], out.at[me], local)

    def begin():
        def one(step, _):
            copy(step, me).start()
            return 0

        lax.fori_loop(1, 32, one, 0)
        own.start()

    def end():
        def one(step, _):
            copy(step, (me + 32 - step) % 32).wait()
            return 0

        lax.fori_loop(1, 32, one, 0)
        own.wait()

    return begin, end


def ring(axis, step):
    return {axis: (lax.axis_index(axis) + 4 + step) % 4}


QKV_ROWS, OUT_ROWS, FF_ROWS = 112, 48, 144
ATTN_ROWS = QKV_ROWS + OUT_ROWS
ATTN_FLOWS = ((0, 0, 32, 16, 0), (1, 0, 48, 16, 0), (0, 32, 80, 32, 1))
UP_FLOWS = ((0, 0, 64, 32, 0), (0, 64, 80, 32, 1))
DOWN_FLOWS = ((0, 0, 160, 80, 1),)
DOWN_ROWS, DOWN_MAIN = 160, 256
FIRST_FLOWS = ((0, 0, 48, 16, 0), (1, 0, 48, 16, 0), (1, 48, 96, 48, 1))
LAST_FLOWS = ((0, 0, 48, 16, 0), (0, 48, 64, 32, 1))
COLUMN_FLOWS = ((0, 0, 48, 16, 0),)
WIDE, WINDOW, LANE = 1152, 384, 128
SUM_ROWS = (OUT_ROWS, FF_ROWS, QKV_ROWS)
SUM_FIRST = (0, 48, 192)


def ring_gather(flows, blocks, place, send, recv, stages=2):
    ix, iy, iz = (lax.axis_index(a) for a in ("x", "y", "row"))
    every = range(len(flows))

    def axis_of(flow, stage):
        return "row" if stage == 2 else "xy"[(flows[flow][4] + stage) % 2]

    def region(flow, stage, owner, half=None):
        by_x = axis_of(flow, stage) == "x"
        slab, first, count, cut, _ = flows[flow]
        if stage == 0:
            row, rows = ((0, count), (0, cut), (cut, count - cut))[0 if half is None else half + 1]
            return place(slab, owner if by_x else ix, iy if by_x else owner, pl.ds(first + row, rows), iz)
        part = pl.ds(0, 4) if half is None else pl.ds(2 * half, 2)
        if stage == 2:
            return place(slab, part, pl.ds(0, 4), pl.ds(first, count), owner)
        return place(slab, owner if by_x else part, part if by_x else owner, pl.ds(first, count), iz)

    def copy(flow, stage, kind, owner):
        half = None if kind < 2 else kind - 2
        there = region(flow, stage, owner, half)
        if stage == 0 and kind < 2:
            slab, first, count, _, _ = flows[flow]
            here = blocks[slab].at[pl.ds(first, count)]
        else:
            here = there
        return remote(
            here,
            there,
            send.at[flow, stage, kind],
            recv.at[flow, stage, kind],
            ring(axis_of(flow, stage), 1 if kind % 2 == 0 else -1),
        )

    def at(flow, stage, step):
        return (lax.axis_index(axis_of(flow, stage)) + 4 + step) % 4

    def begin(stage):
        for flow in every:
            for kind in (0, 1):
                copy(flow, stage, kind, at(flow, stage, 0)).start()

    def middle(stage, then=None):
        for flow in every:
            for kind, step in ((0, -1), (1, 1)):
                owner = at(flow, stage, step)
                copy(flow, stage, kind, owner).wait_recv()
                copy(flow, stage, kind + 2, owner).start()
                if then is not None:
                    then(flow, 1 + kind, owner)

    def finish(stage, then=None):
        for flow in every:
            owner = at(flow, stage, 2)
            for kind in (2, 3):
                copy(flow, stage, kind, owner).wait_recv()
            if then is not None:
                then(flow, 3, owner)

    def end():
        for stage in range(stages):
            for flow in every:
                for kind in range(4):
                    copy(flow, stage, kind, at(flow, stage, 0)).wait_send()

    return begin, middle, finish, end, at


def lay_out(source, quad, target, lanes=slice(None)):
    def one(step, _):
        for part in range(4):
            quad[34 * part : 34 * part + 34] = source(step * 4 + part)
        target[pl.ds(pl.multiple_of(step * 136, 8), 136)] = quad[...].astype(target.dtype)
        return 0

    lax.fori_loop(0, 8, one, 0)


def norm_in(v, gain, shift):
    centred = v - jnp.mean(v, 0, keepdims=True)
    inv_std = lax.rsqrt(jnp.mean(centred * centred, 0, keepdims=True) + EPS)
    standard = centred * inv_std
    return (standard * gain + shift).astype(BF16), standard, inv_std


def add_rows(out, *terms):
    def one(i, _):
        out[i] = sum(t[i].astype(F32) for t in terms).astype(out.dtype)
        return 0

    lax.fori_loop(0, out.shape[0], one, 0)


def ring_reduce(flows, ins, outs, bufs, send, recv, by_z=False):
    every = range(len(flows))
    stages = 3 if by_z else 2

    def axis_of(flow, stage):
        return ("row", "x", "y")[stage] if by_z else "yx"[(flows[flow][4] + stage) % 2]

    def at(flow, stage, step):
        return (lax.axis_index(axis_of(flow, stage)) + 4 + step) % 4

    def held(flow, stage):
        first = (flow * stages + stage) * 4
        return bufs[first : first + 4]

    def chunk(flow, stage, owner, half=None):
        slab, first, count, cut, _ = flows[flow]
        if stage == stages - 1:
            row, rows = ((0, count), (0, cut), (cut, count - cut))[0 if half is None else half + 1]
            return held(flow, stage - 1)[2].at[pl.ds(owner, 1), pl.ds(row, rows)]
        if stage == 1:
            return held(flow, 0)[2].at[pl.ds(owner * 4, 4) if half is None else pl.ds(owner * 4 + 2 * half, 2)]
        window = pl.ds(first, count)
        ref = ins[slab]
        if by_z:
            return ref.at[owner, pl.ds(0, 16) if half is None else pl.ds(8 * half, 8), window]
        part = pl.ds(0, 4) if half is None else pl.ds(2 * half, 2)
        return ref.at[part, owner, window] if axis_of(flow, 0) == "y" else ref.at[owner, part, window]

    def part_of(flow, stage, ref, half):
        if stage < stages - 1:
            count = ref.shape[0] // 2
            return ref.at[pl.ds(count * half, count)]
        _, _, count, cut, _ = flows[flow]
        return ref.at[:, pl.ds(0, cut) if half == 0 else pl.ds(cut, count - cut)]

    def copy(flow, stage, kind):
        from_left, from_right, all_left, all_right = held(flow, stage)
        right = kind % 2 == 0
        if kind < 2:
            src, dst = chunk(flow, stage, at(flow, stage, 2), kind), (from_left, from_right)[kind]
        elif kind < 4:
            src = chunk(flow, stage, at(flow, stage, 1 if right else -1), 1 if right else 0)
            dst = part_of(flow, stage, all_left if right else all_right, 1 if right else 0)
        else:
            src = from_left if right else from_right
            dst = part_of(flow, stage, all_left if right else all_right, 0 if right else 1)
        return remote(
            src,
            dst,
            send.at[flow, stage, kind],
            recv.at[flow, stage, kind],
            ring(axis_of(flow, stage), 1 if right else -1),
        )

    def begin(stage, kinds=(0, 1, 2, 3)):
        for kind in kinds:
            for flow in every:
                copy(flow, stage, kind).start()

    def middle(stage):
        for flow in every:
            from_left, from_right = held(flow, stage)[:2]
            for kind, buf, step in ((0, from_left, 1), (1, from_right, -1)):
                copy(flow, stage, kind).wait_recv()
                add_rows(buf, buf, chunk(flow, stage, at(flow, stage, step), kind))
                copy(flow, stage, kind + 4).start()

    def finish(stage):
        for flow in every:
            all_left, all_right = held(flow, stage)[2:4]
            for kind in (2, 3, 4, 5):
                copy(flow, stage, kind).wait_recv()
            out = all_left
            if stage == stages - 1:
                slab, first, count, _, _ = flows[flow]
                out = outs[slab].at[:, pl.ds(first, count)]
            add_rows(out, chunk(flow, stage, at(flow, stage, 0)), all_left, all_right)

    def end():
        for stage in range(stages):
            for flow in every:
                for kind in range(6):
                    copy(flow, stage, kind).wait_send()

    return begin, middle, finish, end


def ring_bufs(flows, columns, by_z=False):
    stages = 3 if by_z else 2
    bufs = []
    for _, _, count, cut, _ in flows:
        for n in (16, 4) if by_z else (4,):
            bufs += [(n // 2, count), (n // 2, count), (n, count), (n, count)]
        bufs += [(1, cut), (1, count - cut), (1, count), (1, count)]
    sems = [DMA((len(flows), stages, 6)), DMA((len(flows), stages, 6))]
    return sems, [pltpu.VMEM((n, rows, columns), BF16) for n, rows in bufs]


def core_kernel(mine, total, got, send, recv):
    partner = {"core": 1 - lax.axis_index("core")}
    signal(partner)
    pl.semaphore_wait(pltpu.get_barrier_semaphore(), 1)
    copy = remote(mine, got, send, recv, partner)
    copy.start()
    copy.wait()
    total[...] = mine[...] + got[...]


def core_sum(mine):
    return pl.pallas_call(
        core_kernel,
        in_specs=[VMEM],
        out_specs=VMEM,
        out_shape=jax.ShapeDtypeStruct(mine.shape, F32),
        scratch_shapes=[pltpu.VMEM(mine.shape, F32), DMA, DMA],
        compiler_params=params(4),
    )(mine)


def masked_scores(k, q_block, seg_col, seg_row, start, keys):
    scores = nn(k[:keys], q_block)
    key_pos = lax.broadcasted_iota(jnp.int32, scores.shape, 0)
    query_pos = lax.broadcasted_iota(jnp.int32, scores.shape, 1) + start
    allowed = (key_pos <= query_pos) & (seg_col[:keys] == seg_row[:, start : start + QB])
    return jnp.where(allowed, scores, -1e30)


def unit_place():
    return lax.axis_index("y") * 2 + lax.axis_index("core")


def unit_device(place):
    return {"y": place // 2, "core": place % 2}


def head_swap(send, units, sems, rsems):
    iy = lax.axis_index("y")

    def copy(slot, step, owner):
        return remote(
            send.at[(iy + step) % 4, slot],
            units.at[slot, :, :, rows_of(owner * 256)],
            sems.at[slot, step - 1],
            rsems.at[slot, step - 1],
            {"y": (iy + step) % 4},
        )

    def begin(slot):
        for step in range(1, 4):
            if slot < 2:
                copy(slot, step, iy).start()
            else:
                pl.when(((iy + step) % 4 == 0) & (lax.axis_index("core") == 0))(
                    lambda step=step: copy(2, step, iy).start()
                )

    def arrive(slot):
        units[slot, :, :, rows_of(iy * 256)] = send[iy, slot]
        for step in range(1, 4):
            copy(slot, step, (iy + 4 - step) % 4).wait_recv()

    def sent():
        for slot in range(2):
            for step in range(1, 4):
                copy(slot, step, iy).wait_send()
        for step in range(1, 4):
            pl.when(((iy + step) % 4 == 0) & (lax.axis_index("core") == 0))(
                lambda step=step: copy(2, step, iy).wait_send()
            )

    return begin, arrive, sent


def result_swap(units, got, sems, rsems):
    iy, core = lax.axis_index("y"), lax.axis_index("core")

    def copy(slot, step, owner):
        to = (iy + step) % 4
        return remote(
            units.at[slot, :, :, rows_of(to * 256)],
            got.at[owner, core, slot],
            sems.at[slot, step - 1],
            rsems.at[slot, step - 1],
            {"y": to},
        )

    def hand_on(slot, which):
        part = got.at[:, which, slot] if slot < 2 else got.at[pl.ds(0, 1), 0, 2]
        return remote(part, part, sems.at[slot, 3], rsems.at[slot, 3], {"core": 1 - core})

    def begin(slot):
        got[iy, core, slot] = units[slot, :, :, rows_of(iy * 256)]
        for step in range(1, 4):
            copy(slot, step, iy).start()

    def pass_on():
        for slot in range(2):
            for step in range(1, 4):
                copy(slot, step, (iy + 4 - step) % 4).wait_recv()
            hand_on(slot, core).start()

        @pl.when(core == 0)
        def _():
            for step in range(1, 4):
                pl.when(iy == step)(lambda step=step: copy(2, step, 0).wait_recv())
            hand_on(2, 0).start()

    def finish(count):
        for slot in range(2):
            hand_on(slot, 1 - core).wait_recv()
            hand_on(slot, core).wait_send()
        pl.when(core == 1)(lambda: hand_on(2, 0).wait_recv())
        pl.when(core == 0)(lambda: hand_on(2, 0).wait_send())

        def ends(slot, _):
            for step in range(1, 4):
                copy(slot, step, iy).wait_send()
            return 0

        lax.fori_loop(0, count, ends, 0)

    return begin, pass_on, finish


def front_kernel(
    x_src,
    g_src,
    block,
    down_block,
    seg_row_ref,
    seg_col_ref,
    qkv_w,
    out_w,
    up_w,
    down_w,
    g_ref,
    normed1_ref,
    standard1_ref,
    inv_std1_ref,
    qkv_ref,
    out_ref,
    lse_ref,
    attn_ref,
    resid_ref,
    normed2_ref,
    standard2_ref,
    inv_std2_ref,
    vector_ref,
    z_blocks,
    blocks,
    x_got,
    g_got,
    quad,
    quads,
    vector_quad,
    natural,
    x_ref,
    slabs_q,
    slabs_o,
    send,
    got,
    xsend,
    xrecv,
    gsend,
    grecv,
    zsend,
    zrecv,
    core_send,
    core_recv,
    local,
    *sems,
):
    me = greet_col()
    ix, iy, core, iz = (lax.axis_index(a) for a in ("x", "y", "core", "row"))
    for step in (1, -1):
        signal(ring("row", step))
    pl.semaphore_wait(pltpu.get_barrier_semaphore(), 33)
    groups = ((0, ATTN_ROWS), (ATTN_ROWS, FF_ROWS))

    d_begin, d_middle, d_finish, d_end, _ = ring_gather(
        DOWN_FLOWS, (down_block,), lambda slab, x, y, rows, z: down_w.at[z, x, y, rows], sems[8], sems[9], 3
    )

    def zcopy(group, kind, owner):
        first, count = groups[group]
        cut = count // 32 * 16
        part = (pl.ds(first, count), pl.ds(first, cut), pl.ds(first + cut, count - cut))[max(kind - 1, 0)]
        return remote(
            block.at[part] if kind < 2 else z_blocks.at[owner, part],
            z_blocks.at[owner, part],
            zsend.at[group, kind],
            zrecv.at[group, kind],
            ring("row", 1 if kind % 2 == 0 else -1),
        )

    for group in range(2):
        for kind in (0, 1):
            zcopy(group, kind, iz).start()
    x_begin, x_end = token_swap(x_src, x_got, xsend, xrecv, local.at[0], me)
    g_begin, g_end = token_swap(g_src, g_got, gsend, grecv, local.at[1], me)
    d_begin(0)
    own = pltpu.make_async_copy(down_block, down_w.at[iz, ix, iy], local.at[2])
    own.start()
    z_blocks[iz] = block[...]
    d_middle(0)
    d_finish(0)
    own.wait()
    d_begin(1)
    x_begin()
    for group in range(2):
        for kind in (0, 1):
            near = (iz + (3 if kind == 0 else 1)) % 4
            zcopy(group, kind, near).wait_recv()
            zcopy(group, kind + 2, near).start()

    def join(group):
        first, count = groups[group]
        for kind in (2, 3):
            zcopy(group, kind, (iz + 2) % 4).wait_recv()
        total = None
        for owner in range(4):
            shape = (block.shape[1], blocks.shape[1])
            row = lax.broadcasted_iota(jnp.int32, shape, 0) + owner * shape[0]
            place = (row == lax.broadcasted_iota(jnp.int32, shape, 1)).astype(F32).astype(BF16)
            part = nn(z_blocks[owner, first : first + count], place)
            total = part if total is None else total + part
        blocks[first : first + count] = total.astype(BF16)

    attn_blocks = (blocks.at[pl.ds(0, QKV_ROWS)], blocks.at[pl.ds(QKV_ROWS, OUT_ROWS)])
    up_block = blocks.at[pl.ds(ATTN_ROWS, FF_ROWS)]
    a_begin, a_middle, a_finish, a_end, a_at = ring_gather(
        ATTN_FLOWS,
        attn_blocks,
        lambda slab, x, y, rows, z: (slabs_q, slabs_o)[slab].at[x, y, core, rows],
        sems[0],
        sems[1],
    )
    f_begin, f_middle, f_finish, f_end, _ = ring_gather(
        UP_FLOWS, (up_block,), lambda slab, x, y, rows, z: up_w.at[x, y, rows], sems[2], sems[3]
    )
    swaps = []

    def swap(flow, part, owner):
        slab, first, count, _, _ = ATTN_FLOWS[flow]
        rows = pl.ds(first, count)
        every = pl.ds(0, 4)
        by_x = "xy"[(ATTN_FLOWS[flow][4] + 1) % 2] == "x"

        def view(which):
            ref = (slabs_q, slabs_o)[slab]
            return ref.at[owner if by_x else every, every if by_x else owner, which, rows]

        def copy(which):
            return remote(
                view(which), view(which), core_send.at[flow, part], core_recv.at[flow, part], {"core": 1 - core}
            )

        copy(core).start()
        swaps.append((copy(core), copy(1 - core)))

    join(0)
    slabs_q[ix, iy, core] = blocks[:QKV_ROWS]
    slabs_o[ix, iy, core] = blocks[QKV_ROWS:ATTN_ROWS]
    a_begin(0)
    join(1)
    f_begin(0)
    own_up = pltpu.make_async_copy(up_block, up_w.at[ix, iy], local.at[3])
    own_up.start()
    a_middle(0)
    a_finish(0)
    a_begin(1)
    for flow in range(len(ATTN_FLOWS)):
        swap(flow, 0, a_at(flow, 1, 0))
    d_middle(1)
    d_finish(1)
    d_begin(2)
    f_middle(0)
    f_finish(0)
    own_up.wait()

    x_end()
    lay_out(lambda device: x_got[device, :34].astype(F32), quad, x_ref)
    eye_shape = (48, 128)
    eye = lax.broadcasted_iota(jnp.int32, eye_shape, 0) == lax.broadcasted_iota(jnp.int32, eye_shape, 1)
    eye = eye.astype(F32).astype(BF16)

    def vectors(device):
        rows = x_got[device, 32:48, :128]
        turned = nt(eye, rows)
        return turned[:34]

    lay_out(vectors, vector_quad, vector_ref)

    def vector(i):
        return vector_ref[:, 2 + i : 3 + i]

    normed1, standard1, inv_std1 = norm_in(x_ref[...], vector(3), vector(4))
    full = x_ref.shape[0]
    extra = normed1_ref.shape[0] - full
    ones_row = (lax.broadcasted_iota(jnp.int32, (extra, 256), 0) == 0).astype(F32).astype(BF16)
    normed1_ref[:full] = normed1
    normed1_ref[full:] = ones_row
    standard1_ref[...] = standard1
    inv_std1_ref[...] = inv_std1

    a_middle(1, swap)
    f_begin(1)
    g_begin()
    a_finish(1, swap)
    for out, come in swaps:
        come.wait_recv()

    keep = [
        pltpu.make_async_copy(slabs_q, qkv_w, local.at[4]),
        pltpu.make_async_copy(slabs_o, out_w, local.at[5]),
    ]
    for c in keep:
        c.start()

    def project(step, _):
        w = slabs_q[step // 2, pl.ds(step % 2 * 2, 2)]
        quads[...] = nn(w.reshape(4 * QKV_ROWS, full), normed1_ref[:full])
        rows = pl.ds(pl.multiple_of(step * 136, 8), 136)
        for j in range(3):
            for part in range(4):
                quad[34 * part : 34 * part + 34] = quads[112 * part + 34 * j : 112 * part + 34 * j + 34]
            value = quad[...]
            if j != 1:
                value = value + vector_ref[rows, 2 + j // 2 : 3 + j // 2]
            natural[j, rows] = value
        return 0

    lax.fori_loop(0, 8, project, 0)
    count = jnp.where(unit_place() == 0, 3, 2)
    begin, arrive, sent = head_swap(send, qkv_ref, sems[4], sems[5])
    begin_result, pass_on, finish = result_swap(out_ref, got, sems[6], sems[7])
    for slot in range(3):

        def heads(y, _, slot=slot):
            head = slot * 8 + y * 2 + core if slot < 2 else HEADS - 1
            start = head * HD if slot == 2 else pl.multiple_of(head * HD, HD)
            for j in range(3):
                send[y, slot, j] = natural[j, pl.ds(start, HD)].astype(BF16)
            return 0

        lax.fori_loop(0, 4, heads, 0)
        begin(slot)

    def unit(slot, _):
        arrive(slot)
        q = qkv_ref[slot, 0] * (HD**-0.5)
        k = qkv_ref[slot, 1].T
        v = qkv_ref[slot, 2]
        for start in range(0, q.shape[1], QB):
            keys = start + QB
            scores = masked_scores(
                k, q[:, start:keys], seg_col_ref[...], seg_row_ref[...], start, keys
            )
            top = jnp.max(scores, 0, keepdims=True)
            weights = jnp.exp(scores - top)
            total = jnp.sum(weights, 0, keepdims=True)
            result = nn(v[:, :keys], weights.astype(BF16)) * (1.0 / total)
            out_ref[slot, 0, :, start:keys] = result.astype(BF16)
            lse_ref[slot, :, start:keys] = top + jnp.log(total)
        begin_result(slot)
        return 0

    d_middle(2)
    lax.fori_loop(0, count, unit, 0)
    f_middle(1)
    sent()
    pass_on()
    finish(count)

    for head in range(HEADS):
        owner = head % 8
        attn_ref[head * HD : head * HD + HD] = got[owner // 2, owner % 2, head // 8, 0]

    def project_out(step, _):
        w = slabs_o[step // 2, pl.ds(step % 2 * 2, 2)]
        result = nn(w.reshape(4 * OUT_ROWS, full), attn_ref[...])
        quads[: 4 * OUT_ROWS] = result
        rows = pl.ds(pl.multiple_of(step * 136, 8), 136)
        for part in range(4):
            quad[34 * part : 34 * part + 34] = quads[48 * part : 48 * part + 34]
        resid_ref[rows] = x_ref[rows] + quad[...] + vector_ref[rows, 4:5]
        return 0

    lax.fori_loop(0, 8, project_out, 0)
    normed2, standard2, inv_std2 = norm_in(resid_ref[...], vector(5), vector(6))
    normed2_ref[...] = normed2
    standard2_ref[...] = standard2
    inv_std2_ref[...] = inv_std2
    g_end()
    lay_out(lambda device: g_got[device, :34].astype(F32), quad, natural.at[0])
    g_ref[...] = natural[0].astype(BF16)

    f_finish(1)
    d_finish(2)
    a_end()
    f_end()
    d_end()
    for group in range(2):
        for kind in range(4):
            zcopy(group, kind, iz).wait_send()
    for out, _ in swaps:
        out.wait_send()
    for c in keep:
        c.wait()


def front(x_src, g_src, block, down_block, seg_row, seg_col):
    length = seg_row.shape[1]
    full = 4 * block.shape[1]
    total = block.shape[0]
    flat = jax.ShapeDtypeStruct((full, 256), F32)
    low = jax.ShapeDtypeStruct((full, 256), BF16)
    stat = jax.ShapeDtypeStruct((1, 256), F32)
    return pl.pallas_call(
        front_kernel,
        in_specs=[ANY, ANY, VMEM, ANY, VMEM, VMEM],
        out_specs=[ANY] * 4 + [VMEM] * 13,
        out_shape=[
            jax.ShapeDtypeStruct((4, 4, 2, QKV_ROWS, full), BF16),
            jax.ShapeDtypeStruct((4, 4, 2, OUT_ROWS, full), BF16),
            jax.ShapeDtypeStruct((4, 4, FF_ROWS, full), BF16),
            jax.ShapeDtypeStruct((4, 4, 4, DOWN_ROWS, DOWN_MAIN), BF16),
            low,
            jax.ShapeDtypeStruct((WIDE, 256), BF16),
            flat,
            stat,
            jax.ShapeDtypeStruct((3, 3, HD, length), BF16),
            jax.ShapeDtypeStruct((3, 1, HD, length), BF16),
            jax.ShapeDtypeStruct((3, 1, length), F32),
            low,
            flat,
            low,
            flat,
            stat,
            jax.ShapeDtypeStruct((full, 16), F32),
        ],
        scratch_shapes=[
            pltpu.VMEM((4, total, block.shape[1]), BF16),
            pltpu.VMEM((total, full), BF16),
            pltpu.VMEM((32, 48, 256), BF16),
            pltpu.VMEM((32, 48, 256), BF16),
            pltpu.VMEM((136, 256), F32),
            pltpu.VMEM((4 * QKV_ROWS, 256), F32),
            pltpu.VMEM((136, 16), F32),
            pltpu.VMEM((3, full, 256), F32),
            pltpu.VMEM((full, 256), F32),
            pltpu.VMEM((4, 4, 2, QKV_ROWS, full), BF16),
            pltpu.VMEM((4, 4, 2, OUT_ROWS, full), BF16),
            pltpu.VMEM((4, 3, 3, HD, 256), BF16),
            pltpu.VMEM((4, 2, 3, 1, HD, 256), BF16),
            DMA((32,)),
            DMA((32,)),
            DMA((32,)),
            DMA((32,)),
            DMA((2, 4)),
            DMA((2, 4)),
            DMA((3, 4)),
            DMA((3, 4)),
            DMA((6,)),
            DMA((3, 2, 4)),
            DMA((3, 2, 4)),
            DMA((2, 2, 4)),
            DMA((2, 2, 4)),
            DMA((3, 3)),
            DMA((3, 3)),
            DMA((3, 4)),
            DMA((3, 4)),
            DMA((1, 3, 4)),
            DMA((1, 3, 4)),
        ],
        compiler_params=params(0, 60),
    )(x_src, g_src, block, down_block, seg_row, seg_col)


def regroup(step, source, target):
    quad = source[pl.ds(pl.multiple_of(step * 136, 8), 136)]
    for part in range(4):
        target(part, quad[34 * part : 34 * part + 34])


def back_kernel(
    send,
    seg_row_ref,
    seg_col_ref,
    qkv_ref,
    out_ref,
    lse_ref,
    wide,
    out_in,
    up_in,
    active_ref,
    g_ref,
    qkv_w,
    normed_ref,
    standard_ref,
    inv_std_ref,
    gain_ref,
    dresid_ref,
    wide_out,
    input_out,
    main_out,
    tail_out,
    down_out,
    column_out,
    down_in,
    grad_ref,
    dqkv_ref,
    dk_ref,
    dv_ref,
    got,
    natural,
    slab_ref,
    slabs,
    w_buf,
    acc,
    columns,
    column_slab,
    column_part,
    column_sum,
    z_column,
    input_slab,
    input_slabs,
    qkv_part,
    sums,
    z_main,
    z_tail,
    wsend,
    wrecv,
    isend,
    irecv,
    zsend,
    zrecv,
    local,
    w_sem,
    *rest,
):
    place = greet_col()
    ix, iy, core, iz = (lax.axis_index(a) for a in ("x", "y", "core", "row"))
    xy = ix * 4 + iy
    for step in range(1, 4):
        signal(ring("row", step))
    pl.semaphore_wait(pltpu.get_barrier_semaphore(), 34)
    count = jnp.where(unit_place() == 0, 3, 2)
    begin, arrive, sent = head_swap(send, grad_ref, rest[0], rest[1])
    begin_result, pass_on, finish = result_swap(dqkv_ref, got, rest[2], rest[3])
    counts = (len(FIRST_FLOWS) * 8, len(LAST_FLOWS) * 8)
    bufs = rest[12:]
    sum_refs = [sums.at[:, pl.ds(at, rows)] for at, rows in zip(SUM_FIRST, SUM_ROWS)]
    first = ring_reduce(FIRST_FLOWS, (out_in, up_in), sum_refs[:2], bufs[: counts[0]], rest[4], rest[5])
    last = ring_reduce(
        LAST_FLOWS, (qkv_part,), sum_refs[2:], bufs[counts[0] : sum(counts)], rest[6], rest[7]
    )
    down = ring_reduce(
        DOWN_FLOWS, (down_in,), (down_out,), bufs[sum(counts) : sum(counts) + 12], rest[8], rest[9], True
    )
    cols = ring_reduce(
        COLUMN_FLOWS, (column_part,), (column_sum,), bufs[sum(counts) + 12 :], rest[10], rest[11]
    )
    for slot in range(3):
        begin(slot)
    first[0](0)

    tail_rows = g_ref.shape[0] // 4 - DOWN_MAIN

    def down_part(z):
        start = z * (DOWN_MAIN + tail_rows)
        main = g_ref[pl.ds(pl.multiple_of(start, 16), DOWN_MAIN)]
        tail = g_ref[pl.ds(pl.multiple_of(start + DOWN_MAIN, 16), tail_rows)]

        def one(slab, _):
            units = active_ref[slab]
            down_in[z, slab, :FF_ROWS] = nt(units, main).astype(BF16)
            turned = nt(tail, units).astype(BF16)
            down_in[z, slab, FF_ROWS:] = jnp.concatenate(
                [turned, jnp.zeros((tail_rows, DOWN_MAIN - FF_ROWS), BF16)], 1
            )
            return 0

        lax.fori_loop(0, 16, one, 0)

    down_part((iz + 2) % 4)
    down[0](0, (0, 1))
    down_part((iz + 1) % 4)
    down_part((iz + 3) % 4)
    down[0](0, (2, 3))

    def copy_wide(step, owner):
        peer = (place + step) % 32
        return remote(
            wide.at[peer], wide_out.at[owner], wsend.at[step], wrecv.at[step], col_device(peer)
        )

    def begin_wide(step, _):
        copy_wide(step, place).start()
        return 0

    lax.fori_loop(1, 32, begin_wide, 0)
    own = pltpu.make_async_copy(wide.at[place], wide_out.at[place], local)
    own.start()

    def copy_w(step):
        return pltpu.make_async_copy(
            qkv_w.at[pl.ds(step * 4, 4)], w_buf.at[step % 2], w_sem.at[step % 2]
        )

    copy_w(0).start()

    def unit(slot, _):
        arrive(slot)
        q = qkv_ref[slot, 0] * (HD**-0.5)
        key_cols = qkv_ref[slot, 1]
        k = key_cols.T
        v = qkv_ref[slot, 2].T
        grad = grad_ref[slot, 0]
        delta = jnp.sum(grad.astype(F32) * out_ref[slot, 0].astype(F32), 0, keepdims=True)
        dk_ref[...] = jnp.zeros_like(dk_ref)
        dv_ref[...] = jnp.zeros_like(dv_ref)
        for start in range(0, q.shape[1], QB):
            keys = start + QB
            scores = masked_scores(
                k, q[:, start:keys], seg_col_ref[...], seg_row_ref[...], start, keys
            )
            weights = jnp.exp(scores - lse_ref[slot, :, start:keys])
            dweights = nn(v[:keys], grad[:, start:keys])
            dscores = (weights * (dweights - delta[:, start:keys])).astype(BF16)
            dq = nn(key_cols[:, :keys], dscores) * (HD**-0.5)
            dqkv_ref[slot, 0, :, start:keys] = dq.astype(BF16)
            dk_ref[:, :keys] += nt(q[:, start:keys], dscores)
            dv_ref[:, :keys] += nt(grad[:, start:keys], weights.astype(BF16))
        dqkv_ref[slot, 1] = dk_ref[...].astype(BF16)
        dqkv_ref[slot, 2] = dv_ref[...].astype(BF16)
        begin_result(slot)
        return 0

    lax.fori_loop(0, count, unit, 0)
    first[1](0)
    down[1](0)
    down_part(iz)
    sent()
    pass_on()
    finish(count)

    for head in range(HEADS):
        owner = head % 8
        for j in range(3):
            natural[j, head * HD : head * HD + HD] = got[owner // 2, owner % 2, head // 8, j].astype(F32)
    slab_ref[...] = jnp.zeros_like(slab_ref)
    acc[...] = jnp.zeros_like(acc)

    def by_slab(step, _):
        for j in range(3):

            def put(part, rows, j=j):
                slab_ref[part, 34 * j : 34 * j + 34] = rows

            regroup(step, natural.at[j], put)
        four = slab_ref[...].astype(BF16)
        slabs[pl.ds(step * 4, 4)] = four
        return 0

    lax.fori_loop(0, 8, by_slab, 0)

    def weight_part(step, _):
        index = step * 2 + core
        part = nt(slabs[index], normed_ref[...])
        qkv_part[step // 4, step % 4] = part.astype(BF16)
        return 0

    lax.fori_loop(0, 16, weight_part, 0)
    last[0](0)

    def product(step, _):
        @pl.when(step < 7)
        def _():
            copy_w(step + 1).start()

        copy_w(step).wait()
        acc[...] += lax.dot_general(
            slabs[pl.ds(step * 4, 4)].reshape(4 * QKV_ROWS, 256),
            w_buf[step % 2].reshape(4 * QKV_ROWS, -1),
            (((0,), (0,)), ((), ())),
            preferred_element_type=F32,
        )
        return 0

    lax.fori_loop(0, 8, product, 0)
    first[2](0)
    first[0](1)

    late = [
        pltpu.make_async_copy(standard_ref, natural.at[1], w_sem.at[0]),
        pltpu.make_async_copy(dresid_ref, natural.at[2], w_sem.at[1]),
    ]
    for c in late:
        c.start()
    dnormed = acc[...].T
    for c in late:
        c.wait()
    standard = natural[1]
    dv = dnormed * gain_ref[...]
    back = inv_std_ref[...] * (
        dv - jnp.mean(dv, 0, keepdims=True) - standard * jnp.mean(dv * standard, 0, keepdims=True)
    )
    natural[0] = natural[2] + back
    lane = lax.broadcasted_iota(jnp.int32, columns.shape, 1)
    gain_col = jnp.sum(dnormed * standard, 1, keepdims=True)
    shift_col = jnp.sum(dnormed, 1, keepdims=True)
    columns[...] = jnp.where(lane == 65, gain_col, jnp.where(lane == 66, shift_col, 0.0))
    input_slab[...] = jnp.zeros_like(input_slab)
    column_slab[...] = jnp.zeros_like(column_slab)

    def spread(step, _):
        def put(part, rows):
            input_slab[part, :34] = rows

        def put_column(part, rows):
            column_slab[step * 4 + part, :34] = rows

        regroup(step, natural.at[0], put)
        regroup(step, columns, put_column)
        input_slabs[pl.ds(step * 4, 4)] = input_slab[...].astype(BF16)
        return 0

    lax.fori_loop(0, 8, spread, 0)

    def copy_input(step, owner):
        peer = (xy + step) % 16
        return remote(
            input_slabs.at[peer * 2 + core],
            input_out.at[owner],
            isend.at[step],
            irecv.at[step],
            {"x": peer // 4, "y": peer % 4},
        )

    def own_columns(step, _):
        column_part[step // 4, step % 4] = column_slab[step * 2 + core].astype(BF16)
        return 0

    lax.fori_loop(0, 16, own_columns, 0)
    cols[0](0)
    down[2](0)
    down[0](1)

    def begin_input(step, _):
        copy_input(step, xy).start()
        return 0

    lax.fori_loop(1, 16, begin_input, 0)
    input_out[xy] = input_slabs[xy * 2 + core]

    def z_columns(step):
        return remote(
            column_sum, z_column.at[pl.ds(step - 1, 1)], zsend.at[2, 0, step - 1], zrecv.at[2, 0, step - 1], ring("row", step)
        )

    def z_copies(group, step):
        rows = pl.ds(0, SUM_FIRST[2]) if group == 0 else pl.ds(SUM_FIRST[2], QKV_ROWS)
        window = pl.ds(pl.multiple_of((iz + step) % 4 * 256, 256), WINDOW)
        return [
            remote(
                sums.at[0, rows, lanes],
                out.at[step - 1, rows],
                zsend.at[group, i, step - 1],
                zrecv.at[group, i, step - 1],
                ring("row", step),
            )
            for i, (lanes, out) in enumerate(((window, z_main), (pl.ds(WIDE - LANE, LANE), z_tail)))
        ]

    def begin_z(group):
        for step in range(1, 4):
            for c in z_copies(group, step):
                c.start()

    first[1](1)
    down[1](1)
    last[1](0)
    first[2](1)
    begin_z(0)
    cols[1](0)
    last[2](0)
    last[0](1)
    cols[2](0)
    cols[0](1)
    down[2](1)
    down[0](2)
    last[1](1)
    cols[1](1)
    down[1](2)
    last[2](1)
    begin_z(1)
    cols[2](1)
    for step in range(1, 4):
        z_columns(step).start()
    down[2](2)
    first[3]()
    last[3]()
    down[3]()
    cols[3]()
    own.wait()

    def end_wide(step, _):
        copy_wide(step, (place + 32 - step) % 32).wait()
        return 0

    lax.fori_loop(1, 32, end_wide, 0)

    def end_input(step, _):
        copy_input(step, (xy + 16 - step) % 16).wait()
        return 0

    lax.fori_loop(1, 16, end_input, 0)
    for group in range(2):
        for step in range(1, 4):
            for c in z_copies(group, step):
                c.wait()
    for step in range(1, 4):
        z_columns(step).wait()
    column_out[...] = column_sum[0].astype(F32) + sum(z_column[i].astype(F32) for i in range(3))
    window = pl.ds(pl.multiple_of(iz * 256, 256), WINDOW)
    main_out[...] = sums[0, :, window].astype(F32) + sum(z_main[i].astype(F32) for i in range(3))
    tail_out[...] = sums[0, :, WIDE - LANE :].astype(F32) + sum(z_tail[i].astype(F32) for i in range(3))


def attend_back(
    send, seg_row, seg_col, qkv, out, lse, wide, out_part, up_part, active, g, qkv_w, normed, standard, inv_std, gain, dresid
):
    length = seg_row.shape[1]
    full = qkv_w.shape[-1]
    first_sems, first_bufs = ring_bufs(FIRST_FLOWS, WIDE)
    last_sems, last_bufs = ring_bufs(LAST_FLOWS, WIDE)
    down_sems, down_bufs = ring_bufs(DOWN_FLOWS, DOWN_MAIN, True)
    column_sems, column_bufs = ring_bufs(COLUMN_FLOWS, LANE)
    total = sum(SUM_ROWS)
    return pl.pallas_call(
        back_kernel,
        in_specs=[VMEM] * 6 + [ANY] + [VMEM] * 4 + [ANY, VMEM, ANY, VMEM, VMEM, ANY],
        out_specs=[ANY] + [VMEM] * 5,
        out_shape=[
            jax.ShapeDtypeStruct(wide.shape, wide.dtype),
            jax.ShapeDtypeStruct((16, 48, 256), BF16),
            jax.ShapeDtypeStruct((total, WINDOW), F32),
            jax.ShapeDtypeStruct((total, LANE), F32),
            jax.ShapeDtypeStruct((1, DOWN_ROWS, DOWN_MAIN), F32),
            jax.ShapeDtypeStruct((48, LANE), F32),
        ],
        scratch_shapes=[
            pltpu.VMEM((4, 16, DOWN_ROWS, DOWN_MAIN), BF16),
            pltpu.VMEM((3, 1, HD, length), BF16),
            pltpu.VMEM((3, 3, HD, length), BF16),
            pltpu.VMEM((HD, length), F32),
            pltpu.VMEM((HD, length), F32),
            pltpu.VMEM((4, 2, 3, 3, HD, 256), BF16),
            pltpu.VMEM((3, full, 256), F32),
            pltpu.VMEM((4, QKV_ROWS, 256), F32),
            pltpu.VMEM((32, QKV_ROWS, 256), BF16),
            pltpu.VMEM((2, 4, QKV_ROWS, full), BF16),
            pltpu.VMEM((256, full), F32),
            pltpu.VMEM((full, LANE), F32),
            pltpu.VMEM((32, 48, LANE), F32),
            pltpu.VMEM((4, 4, 48, LANE), BF16),
            pltpu.VMEM((1, 48, LANE), BF16),
            pltpu.VMEM((3, 48, LANE), BF16),
            pltpu.VMEM((4, 48, 256), F32),
            pltpu.VMEM((32, 48, 256), BF16),
            pltpu.VMEM((4, 4, QKV_ROWS, WIDE), BF16),
            pltpu.VMEM((1, total, WIDE), BF16),
            pltpu.VMEM((3, total, WINDOW), BF16),
            pltpu.VMEM((3, total, LANE), BF16),
            DMA((32,)),
            DMA((32,)),
            DMA((16,)),
            DMA((16,)),
            DMA((3, 2, 3)),
            DMA((3, 2, 3)),
            DMA,
            DMA((2,)),
            DMA((3, 3)),
            DMA((3, 3)),
            DMA((3, 4)),
            DMA((3, 4)),
        ]
        + first_sems
        + last_sems
        + down_sems
        + column_sems
        + first_bufs
        + last_bufs
        + down_bufs
        + column_bufs,
        compiler_params=params(6, 62),
    )(
        send, seg_row, seg_col, qkv, out, lse, wide, out_part, up_part, active, g, qkv_w, normed, standard, inv_std, gain, dresid
    )


def norm_back(dn, standard, inv_std, gain):
    dv = dn * gain
    back = inv_std * (
        dv - jnp.mean(dv, 0, keepdims=True) - standard * jnp.mean(dv * standard, 0, keepdims=True)
    )
    return back, jnp.sum(dn * standard, 1), jnp.sum(dn, 1)


def to_heads(v, core):
    n, _, tokens = v.shape
    heads = v.reshape(n, HEADS, HD, tokens).transpose(1, 0, 2, 3)
    pairs = heads[:16].reshape(2, 4, 2, n, HD, tokens)
    mine = lax.dynamic_index_in_dim(pairs, core, 2, keepdims=False)
    last = jnp.broadcast_to(heads[16:], (4, n, HD, tokens))
    return jnp.concatenate([mine.transpose(1, 0, 2, 3, 4), last[:, None]], 1)


def shards(
    layer_input,
    cotangent,
    segments,
    qkv_weight,
    qv_bias,
    out_weight,
    out_bias,
    up_weight,
    up_bias,
    down_weight,
    down_bias,
    first_gain,
    first_shift,
    second_gain,
    second_shift,
):
    ix, iy, core = lax.axis_index("x"), lax.axis_index("y"), lax.axis_index("core")
    width = layer_input.shape[0]
    rows = qkv_weight.shape[0]
    full = 4 * rows
    units = up_weight.shape[1]

    block = jnp.concatenate(
        [
            qkv_weight.transpose(1, 2, 0).reshape(3 * width, rows),
            jnp.pad(up_bias[None], ((0, QKV_ROWS - 3 * width - 1), (0, rows - units))),
            jnp.pad(out_weight.T, ((0, OUT_ROWS - width), (0, 0))),
            jnp.pad(up_weight.T, ((0, FF_ROWS - units), (0, 0))),
        ],
        0,
    )
    down_block = jnp.concatenate(
        [
            jnp.pad(down_weight[:, :DOWN_MAIN], ((0, FF_ROWS - units), (0, 0))),
            jnp.pad(down_weight[:, DOWN_MAIN:].T, ((0, 0), (0, DOWN_MAIN - units))),
        ],
        0,
    )
    small = jnp.concatenate(
        [qv_bias, jnp.stack([out_bias, first_gain, first_shift, second_gain, second_shift])], 0
    )
    small = jnp.tile(jnp.pad(small, ((0, 48 - width - 7), (0, 256 - width))), (1, 16))
    x_src = jnp.concatenate([layer_input, small], 0)
    g_src = jnp.pad(cotangent, ((0, 48 - width), (0, 0)))
    seg = lax.dynamic_index_in_dim(segments, ix, 0, keepdims=False)
    seg_row, seg_col = seg[None], seg[:, None]
    (
        qkv_w,
        out_w,
        up_w,
        down_w,
        g_low,
        normed1,
        standard1,
        inv_std1,
        units_qkv,
        units_out,
        lse,
        attn,
        resid,
        normed2,
        standard2,
        inv_std2,
        vectors,
    ) = front(x_src, g_src, block, down_block, seg_row, seg_col)
    qkv_w = qkv_w.reshape(32, QKV_ROWS, full)
    out_w = out_w.reshape(32, OUT_ROWS, full)
    up_w = up_w.reshape(16, FF_ROWS, full)
    down_w = down_w.reshape(4, 16, DOWN_ROWS, DOWN_MAIN)
    down_tail = down_w[:, :, FF_ROWS:, :FF_ROWS]
    g = g_low.astype(F32)
    gain1, gain2 = vectors[:, 5:6], vectors[:, 7:8]
    hidden_bias = lax.dynamic_index_in_dim(
        qkv_w[:, 3 * width, :units].reshape(16, 2, units), core, 1, keepdims=False
    ).astype(F32)
    hidden_bias = jnp.pad(hidden_bias, ((0, 0), (0, FF_ROWS - units)))
    hidden = jnp.einsum("xfd,dt->xft", up_w, normed2, preferred_element_type=F32) + hidden_bias[..., None]
    active, gelu_back = jax.vjp(lambda h: jax.nn.gelu(h, approximate=True), hidden)
    active = active.astype(BF16)
    active_rows = jnp.pad(active, ((0, 0), (0, DOWN_ROWS - FF_ROWS), (0, 0)))
    out_main = [
        jnp.einsum("xfd,xft->dt", down_w[z], active_rows, preferred_element_type=F32) for z in range(4)
    ]
    out_tail = jnp.einsum("zxdf,xft->zdt", down_tail, active, preferred_element_type=F32)
    ff_out = jnp.concatenate([p for z in range(4) for p in (out_main[z], out_tail[z])], 0)
    send_out = (ff_out + jnp.where(core == 0, 1.0, 0.0) * resid).astype(BF16)
    send_out = jnp.pad(send_out.reshape(32, width, 256), ((0, 0), (0, 48 - width), (0, 0)))
    g_main = [g_low[z * rows : z * rows + DOWN_MAIN] for z in range(4)]
    g_tail = jnp.stack([g_low[z * rows + DOWN_MAIN : z * rows + rows] for z in range(4)])
    dactive = sum(
        jnp.einsum("xfd,dt->xft", down_w[z], g_main[z], preferred_element_type=F32) for z in range(4)
    )[:, :FF_ROWS]
    dactive = dactive + jnp.einsum("zxdf,zdt->xft", down_tail, g_tail, preferred_element_type=F32)
    dhidden = gelu_back(dactive)[0].astype(BF16)
    extra = WIDE - full
    ones_row = jnp.pad(jnp.ones((1, 256), BF16), ((0, extra - 1), (0, 0)))

    def widen(v):
        return jnp.concatenate([v, ones_row], 0)

    up_part = jnp.einsum("xft,dt->xfd", dhidden, widen(normed2), preferred_element_type=F32).astype(BF16)
    dn2 = jnp.einsum("xfd,xft->dt", up_w, dhidden, preferred_element_type=F32)
    dn2 = core_sum(dn2)
    back2, gain2_grad, shift2_grad = norm_back(dn2, standard2, inv_std2, gain2)
    dresid = g + back2
    dproj = dresid.astype(BF16)
    dproj_block = jnp.pad(dproj.reshape(32, width, 256), ((0, 0), (0, OUT_ROWS - width), (0, 0)))
    dattn = jnp.einsum("ced,cet->dt", out_w, dproj_block, preferred_element_type=F32).astype(BF16)
    mine = lax.dynamic_index_in_dim(dproj_block.reshape(16, 2, OUT_ROWS, 256), core, 1, keepdims=False)
    cols = jnp.stack([jnp.sum(g, -1), gain2_grad, shift2_grad], -1).reshape(16, 2, width, 3)
    cols = lax.dynamic_index_in_dim(cols, core, 1, keepdims=False)
    cols = jnp.pad(cols, ((0, 0), (0, OUT_ROWS - width), (full + 1, extra - 4)))
    out_part = jnp.einsum("xrt,dt->xrd", mine, widen(attn), preferred_element_type=F32) + cols
    got_out, input_got, main, tail, down_sum, columns = attend_back(
        to_heads(dattn[None], core),
        seg_row,
        seg_col,
        units_qkv,
        units_out,
        lse,
        send_out,
        out_part.astype(BF16).reshape(4, 4, OUT_ROWS, WIDE),
        up_part.reshape(4, 4, FF_ROWS, WIDE),
        active,
        g_low,
        qkv_w,
        normed1,
        standard1,
        inv_std1,
        gain1,
        dresid,
    )
    layer_output = jnp.sum(got_out[:, :width].reshape(16, 2, width, 256).astype(F32), 1)
    layer_output = layer_output.transpose(1, 0, 2).reshape(width, 4096)
    layer_output = layer_output + down_bias.astype(F32)[:, None]
    input_grad = input_got[:, :width].transpose(1, 0, 2).reshape(width, 4096).astype(F32)
    main = lax.dynamic_slice_in_dim(main, lax.axis_index("row") * (rows - 256), rows, 1)
    out_first, up_first, qkv_first = SUM_FIRST
    qkv_out = main[qkv_first : qkv_first + 3 * width].reshape(3, width, rows).transpose(2, 0, 1)
    qkv_tail = tail[qkv_first:, LANE - extra :]
    out_tail = tail[out_first : out_first + width, LANE - extra :]
    return (
        layer_output,
        input_grad,
        qkv_out,
        jnp.stack([qkv_tail[:width, 0], qkv_tail[2 * width : 3 * width, 0]]),
        main[out_first : out_first + width].T,
        out_tail[:, 0],
        main[up_first : up_first + units].T,
        tail[up_first : up_first + units, LANE - extra],
        jnp.concatenate([down_sum[0, :units], down_sum[0, FF_ROWS:, :units].T], 1),
        out_tail[:, 1],
        columns[:width, 65],
        columns[:width, 66],
        out_tail[:, 2],
        out_tail[:, 3],
    )


def solution(mesh):
    split = Mesh(mesh.devices.reshape(4, 4, 4, 2), ("row", "x", "y", "core"))
    vec = P(COL)
    return jax.shard_map(
        shards,
        mesh=split,
        in_specs=(
            P(COL, "row"),
            P(COL, "row"),
            P("row", None),
            P("row", None, COL),
            P(None, COL),
            P("row", COL),
            vec,
            P("row", COL),
            vec,
            P(COL, "row"),
            vec,
            vec,
            vec,
            vec,
            vec,
        ),
        out_specs=(
            P(COL, "row"),
            P(COL, "row"),
            P("row", None, COL),
            P(None, COL),
            P("row", COL),
            vec,
            P("row", COL),
            vec,
            P(COL, "row"),
            vec,
            vec,
            vec,
            vec,
            vec,
        ),
        check_vma=False,
    )
```

```python
import jax
import jax.numpy as jnp
from jax import lax
from jax.experimental import pallas as pl
from jax.experimental.pallas import tpu as pltpu
from jax.sharding import Mesh, PartitionSpec as P

HEADS = 17
HD = 64
EPS = 1e-05
XY = ("x", "y")
COL = ("x", "y", "core")
F32 = jnp.float32
BF16 = jnp.bfloat16
QB = 256


def nn(a, b):
    return lax.dot_general(a, b, (((1,), (0,)), ((), ())), preferred_element_type=F32)


def nt(a, b):
    return lax.dot_general(a, b, (((1,), (1,)), ((), ())), preferred_element_type=F32)


MESH = pl.DeviceIdType.MESH
ANY = pl.BlockSpec(memory_space=pl.ANY)
VMEM = pl.BlockSpec(memory_space=pltpu.VMEM)
DMA = pltpu.SemaphoreType.DMA


def params(collective_id, vmem=56):
    return pltpu.CompilerParams(
        collective_id=collective_id, has_side_effects=True, vmem_limit_bytes=vmem * 2**20
    )


def remote(src, dst, send_sem, recv_sem, where):
    return pltpu.make_async_remote_copy(
        src_ref=src,
        dst_ref=dst,
        send_sem=send_sem,
        recv_sem=recv_sem,
        device_id=where,
        device_id_type=MESH,
    )


def signal(where):
    pl.semaphore_signal(
        pltpu.get_barrier_semaphore(), inc=1, device_id=where, device_id_type=MESH
    )


def col_place():
    return (lax.axis_index("x") * 4 + lax.axis_index("y")) * 2 + lax.axis_index("core")


def col_device(place):
    return {"x": place // 8, "y": place // 2 % 4, "core": place % 2}


def greet_col():
    me = col_place()

    def greet(step, _):
        signal(col_device((me + step) % 32))
        return 0

    lax.fori_loop(1, 32, greet, 0)
    return me


def rows_of(n):
    return pl.ds(pl.multiple_of(n, 256), 256)


def token_swap(src, out, send, recv, local, me):
    def copy(step, owner):
        peer = (me + step) % 32
        return remote(
            src.at[:, rows_of(peer // 2 * 256)], out.at[owner], send.at[step], recv.at[step], col_device(peer)
        )

    own = pltpu.make_async_copy(src.at[:, rows_of(me // 2 * 256)], out.at[me], local)

    def begin():
        def one(step, _):
            copy(step, me).start()
            return 0

        lax.fori_loop(1, 32, one, 0)
        own.start()

    def end():
        def one(step, _):
            copy(step, (me + 32 - step) % 32).wait()
            return 0

        lax.fori_loop(1, 32, one, 0)
        own.wait()

    return begin, end


def ring(axis, step):
    return {axis: (lax.axis_index(axis) + 4 + step) % 4}


QKV_ROWS, OUT_ROWS, FF_ROWS = 112, 48, 144
ATTN_ROWS = QKV_ROWS + OUT_ROWS
ATTN_FLOWS = ((0, 0, 32, 16, 0), (1, 0, 48, 16, 0), (0, 32, 80, 32, 1))
UP_FLOWS = ((0, 0, 64, 32, 0), (0, 64, 80, 32, 1))
DOWN_FLOWS = ((0, 0, 160, 80, 1),)
DOWN_ROWS, DOWN_MAIN = 160, 256
FIRST_FLOWS = ((0, 0, 48, 16, 0), (1, 0, 48, 16, 0), (1, 48, 96, 48, 1))
LAST_FLOWS = ((0, 0, 48, 16, 0), (0, 48, 64, 32, 1))
COLUMN_FLOWS = ((0, 0, 48, 16, 0),)
WIDE, WINDOW, LANE = 1152, 384, 128
SUM_ROWS = (OUT_ROWS, FF_ROWS, QKV_ROWS)
SUM_FIRST = (0, 48, 192)


def ring_gather(flows, blocks, place, send, recv, stages=2):
    ix, iy, iz = (lax.axis_index(a) for a in ("x", "y", "row"))
    every = range(len(flows))

    def axis_of(flow, stage):
        return "row" if stage == 2 else "xy"[(flows[flow][4] + stage) % 2]

    def region(flow, stage, owner, half=None):
        by_x = axis_of(flow, stage) == "x"
        slab, first, count, cut, _ = flows[flow]
        if stage == 0:
            row, rows = ((0, count), (0, cut), (cut, count - cut))[0 if half is None else half + 1]
            return place(slab, owner if by_x else ix, iy if by_x else owner, pl.ds(first + row, rows), iz)
        part = pl.ds(0, 4) if half is None else pl.ds(2 * half, 2)
        if stage == 2:
            return place(slab, part, pl.ds(0, 4), pl.ds(first, count), owner)
        return place(slab, owner if by_x else part, part if by_x else owner, pl.ds(first, count), iz)

    def copy(flow, stage, kind, owner):
        half = None if kind < 2 else kind - 2
        there = region(flow, stage, owner, half)
        if stage == 0 and kind < 2:
            slab, first, count, _, _ = flows[flow]
            here = blocks[slab].at[pl.ds(first, count)]
        else:
            here = there
        return remote(
            here,
            there,
            send.at[flow, stage, kind],
            recv.at[flow, stage, kind],
            ring(axis_of(flow, stage), 1 if kind % 2 == 0 else -1),
        )

    def at(flow, stage, step):
        return (lax.axis_index(axis_of(flow, stage)) + 4 + step) % 4

    def begin(stage):
        for flow in every:
            for kind in (0, 1):
                copy(flow, stage, kind, at(flow, stage, 0)).start()

    def middle(stage, then=None):
        for flow in every:
            for kind, step in ((0, -1), (1, 1)):
                owner = at(flow, stage, step)
                copy(flow, stage, kind, owner).wait_recv()
                copy(flow, stage, kind + 2, owner).start()
                if then is not None:
                    then(flow, 1 + kind, owner)

    def finish(stage, then=None):
        for flow in every:
            owner = at(flow, stage, 2)
            for kind in (2, 3):
                copy(flow, stage, kind, owner).wait_recv()
            if then is not None:
                then(flow, 3, owner)

    def end():
        for stage in range(stages):
            for flow in every:
                for kind in range(4):
                    copy(flow, stage, kind, at(flow, stage, 0)).wait_send()

    return begin, middle, finish, end, at


def lay_out(source, quad, target, lanes=slice(None)):
    def one(step, _):
        for part in range(4):
            quad[34 * part : 34 * part + 34] = source(step * 4 + part)
        target[pl.ds(pl.multiple_of(step * 136, 8), 136)] = quad[...].astype(target.dtype)
        return 0

    lax.fori_loop(0, 8, one, 0)


def norm_in(v, gain, shift):
    centred = v - jnp.mean(v, 0, keepdims=True)
    inv_std = lax.rsqrt(jnp.mean(centred * centred, 0, keepdims=True) + EPS)
    standard = centred * inv_std
    return (standard * gain + shift).astype(BF16), standard, inv_std


def add_rows(out, *terms):
    def one(i, _):
        out[i] = sum(t[i].astype(F32) for t in terms).astype(out.dtype)
        return 0

    lax.fori_loop(0, out.shape[0], one, 0)


def ring_reduce(flows, ins, outs, bufs, send, recv, by_z=False):
    every = range(len(flows))
    stages = 3 if by_z else 2

    def axis_of(flow, stage):
        return ("row", "x", "y")[stage] if by_z else "yx"[(flows[flow][4] + stage) % 2]

    def at(flow, stage, step):
        return (lax.axis_index(axis_of(flow, stage)) + 4 + step) % 4

    def held(flow, stage):
        first = (flow * stages + stage) * 4
        return bufs[first : first + 4]

    def chunk(flow, stage, owner, half=None):
        slab, first, count, cut, _ = flows[flow]
        if stage == stages - 1:
            row, rows = ((0, count), (0, cut), (cut, count - cut))[0 if half is None else half + 1]
            return held(flow, stage - 1)[2].at[pl.ds(owner, 1), pl.ds(row, rows)]
        if stage == 1:
            return held(flow, 0)[2].at[pl.ds(owner * 4, 4) if half is None else pl.ds(owner * 4 + 2 * half, 2)]
        window = pl.ds(first, count)
        ref = ins[slab]
        if by_z:
            return ref.at[owner, pl.ds(0, 16) if half is None else pl.ds(8 * half, 8), window]
        part = pl.ds(0, 4) if half is None else pl.ds(2 * half, 2)
        return ref.at[part, owner, window] if axis_of(flow, 0) == "y" else ref.at[owner, part, window]

    def part_of(flow, stage, ref, half):
        if stage < stages - 1:
            count = ref.shape[0] // 2
            return ref.at[pl.ds(count * half, count)]
        _, _, count, cut, _ = flows[flow]
        return ref.at[:, pl.ds(0, cut) if half == 0 else pl.ds(cut, count - cut)]

    def copy(flow, stage, kind):
        from_left, from_right, all_left, all_right = held(flow, stage)
        right = kind % 2 == 0
        if kind < 2:
            src, dst = chunk(flow, stage, at(flow, stage, 2), kind), (from_left, from_right)[kind]
        elif kind < 4:
            src = chunk(flow, stage, at(flow, stage, 1 if right else -1), 1 if right else 0)
            dst = part_of(flow, stage, all_left if right else all_right, 1 if right else 0)
        else:
            src = from_left if right else from_right
            dst = part_of(flow, stage, all_left if right else all_right, 0 if right else 1)
        return remote(
            src,
            dst,
            send.at[flow, stage, kind],
            recv.at[flow, stage, kind],
            ring(axis_of(flow, stage), 1 if right else -1),
        )

    def begin(stage, kinds=(0, 1, 2, 3)):
        for kind in kinds:
            for flow in every:
                copy(flow, stage, kind).start()

    def middle(stage):
        for flow in every:
            from_left, from_right = held(flow, stage)[:2]
            for kind, buf, step in ((0, from_left, 1), (1, from_right, -1)):
                copy(flow, stage, kind).wait_recv()
                add_rows(buf, buf, chunk(flow, stage, at(flow, stage, step), kind))
                copy(flow, stage, kind + 4).start()

    def finish(stage):
        for flow in every:
            all_left, all_right = held(flow, stage)[2:4]
            for kind in (2, 3, 4, 5):
                copy(flow, stage, kind).wait_recv()
            out = all_left
            if stage == stages - 1:
                slab, first, count, _, _ = flows[flow]
                out = outs[slab].at[:, pl.ds(first, count)]
            add_rows(out, chunk(flow, stage, at(flow, stage, 0)), all_left, all_right)

    def end():
        for stage in range(stages):
            for flow in every:
                for kind in range(6):
                    copy(flow, stage, kind).wait_send()

    return begin, middle, finish, end


def ring_bufs(flows, columns, by_z=False):
    stages = 3 if by_z else 2
    bufs = []
    for _, _, count, cut, _ in flows:
        for n in (16, 4) if by_z else (4,):
            bufs += [(n // 2, count), (n // 2, count), (n, count), (n, count)]
        bufs += [(1, cut), (1, count - cut), (1, count), (1, count)]
    sems = [DMA((len(flows), stages, 6)), DMA((len(flows), stages, 6))]
    return sems, [pltpu.VMEM((n, rows, columns), BF16) for n, rows in bufs]


def core_kernel(mine, total, got, send, recv):
    partner = {"core": 1 - lax.axis_index("core")}
    signal(partner)
    pl.semaphore_wait(pltpu.get_barrier_semaphore(), 1)
    copy = remote(mine, got, send, recv, partner)
    copy.start()
    copy.wait()
    total[...] = mine[...].astype(F32) + got[...].astype(F32)


def core_sum(mine):
    return pl.pallas_call(
        core_kernel,
        in_specs=[VMEM],
        out_specs=VMEM,
        out_shape=jax.ShapeDtypeStruct(mine.shape, F32),
        scratch_shapes=[pltpu.VMEM(mine.shape, mine.dtype), DMA, DMA],
        compiler_params=params(4),
    )(mine)


def masked_scores(k, q_block, seg_col, seg_row, start, keys):
    scores = nn(k[:keys], q_block)
    key_pos = lax.broadcasted_iota(jnp.int32, scores.shape, 0)
    query_pos = lax.broadcasted_iota(jnp.int32, scores.shape, 1) + start
    allowed = (key_pos <= query_pos) & (seg_col[:keys] == seg_row[:, start : start + QB])
    return jnp.where(allowed, scores, -1e30)


def unit_place():
    return lax.axis_index("y") * 2 + lax.axis_index("core")


def unit_device(place):
    return {"y": place // 2, "core": place % 2}


def head_swap(send, units, sems, rsems):
    iy = lax.axis_index("y")

    def copy(slot, step, owner):
        return remote(
            send.at[(iy + step) % 4, slot],
            units.at[slot, :, :, rows_of(owner * 256)],
            sems.at[slot, step - 1],
            rsems.at[slot, step - 1],
            {"y": (iy + step) % 4},
        )

    def begin(slot):
        for step in range(1, 4):
            if slot < 2:
                copy(slot, step, iy).start()
            else:
                pl.when(((iy + step) % 4 == 0) & (lax.axis_index("core") == 0))(
                    lambda step=step: copy(2, step, iy).start()
                )

    def arrive(slot):
        units[slot, :, :, rows_of(iy * 256)] = send[iy, slot]
        for step in range(1, 4):
            copy(slot, step, (iy + 4 - step) % 4).wait_recv()

    def sent():
        for slot in range(2):
            for step in range(1, 4):
                copy(slot, step, iy).wait_send()
        for step in range(1, 4):
            pl.when(((iy + step) % 4 == 0) & (lax.axis_index("core") == 0))(
                lambda step=step: copy(2, step, iy).wait_send()
            )

    return begin, arrive, sent


def result_swap(units, got, sems, rsems):
    iy, core = lax.axis_index("y"), lax.axis_index("core")

    def copy(slot, step, owner):
        to = (iy + step) % 4
        return remote(
            units.at[slot, :, :, rows_of(to * 256)],
            got.at[owner, core, slot],
            sems.at[slot, step - 1],
            rsems.at[slot, step - 1],
            {"y": to},
        )

    def hand_on(slot, which):
        part = got.at[:, which, slot] if slot < 2 else got.at[pl.ds(0, 1), 0, 2]
        return remote(part, part, sems.at[slot, 3], rsems.at[slot, 3], {"core": 1 - core})

    def begin(slot):
        got[iy, core, slot] = units[slot, :, :, rows_of(iy * 256)]
        for step in range(1, 4):
            copy(slot, step, iy).start()

    def pass_on():
        for slot in range(2):
            for step in range(1, 4):
                copy(slot, step, (iy + 4 - step) % 4).wait_recv()
            hand_on(slot, core).start()

        @pl.when(core == 0)
        def _():
            for step in range(1, 4):
                pl.when(iy == step)(lambda step=step: copy(2, step, 0).wait_recv())
            hand_on(2, 0).start()

    def finish(count):
        for slot in range(2):
            hand_on(slot, 1 - core).wait_recv()
            hand_on(slot, core).wait_send()
        pl.when(core == 1)(lambda: hand_on(2, 0).wait_recv())
        pl.when(core == 0)(lambda: hand_on(2, 0).wait_send())

        def ends(slot, _):
            for step in range(1, 4):
                copy(slot, step, iy).wait_send()
            return 0

        lax.fori_loop(0, count, ends, 0)

    return begin, pass_on, finish


def front_kernel(
    x_src,
    g_src,
    block,
    down_block,
    seg_row_ref,
    seg_col_ref,
    qkv_w,
    out_w,
    up_w,
    down_w,
    g_ref,
    normed1_ref,
    standard1_ref,
    inv_std1_ref,
    qkv_ref,
    out_ref,
    lse_ref,
    attn_ref,
    resid_ref,
    normed2_ref,
    standard2_ref,
    inv_std2_ref,
    vector_ref,
    z_blocks,
    blocks,
    x_got,
    g_got,
    quad,
    quads,
    vector_quad,
    natural,
    x_ref,
    slabs_q,
    slabs_o,
    send,
    got,
    xsend,
    xrecv,
    gsend,
    grecv,
    zsend,
    zrecv,
    core_send,
    core_recv,
    local,
    *sems,
):
    me = greet_col()
    ix, iy, core, iz = (lax.axis_index(a) for a in ("x", "y", "core", "row"))
    for step in (1, -1):
        signal(ring("row", step))
    pl.semaphore_wait(pltpu.get_barrier_semaphore(), 33)
    groups = ((0, ATTN_ROWS), (ATTN_ROWS, FF_ROWS))

    d_begin, d_middle, d_finish, d_end, _ = ring_gather(
        DOWN_FLOWS, (down_block,), lambda slab, x, y, rows, z: down_w.at[z, x, y, rows], sems[8], sems[9], 3
    )

    def zcopy(group, kind, owner):
        first, count = groups[group]
        cut = count // 32 * 16
        part = (pl.ds(first, count), pl.ds(first, cut), pl.ds(first + cut, count - cut))[max(kind - 1, 0)]
        return remote(
            block.at[part] if kind < 2 else z_blocks.at[owner, part],
            z_blocks.at[owner, part],
            zsend.at[group, kind],
            zrecv.at[group, kind],
            ring("row", 1 if kind % 2 == 0 else -1),
        )

    for group in range(2):
        for kind in (0, 1):
            zcopy(group, kind, iz).start()
    x_begin, x_end = token_swap(x_src, x_got, xsend, xrecv, local.at[0], me)
    g_begin, g_end = token_swap(g_src, g_got, gsend, grecv, local.at[1], me)
    d_begin(0)
    own = pltpu.make_async_copy(down_block, down_w.at[iz, ix, iy], local.at[2])
    own.start()
    z_blocks[iz] = block[...]
    d_middle(0)
    d_finish(0)
    own.wait()
    d_begin(1)
    x_begin()
    for group in range(2):
        for kind in (0, 1):
            near = (iz + (3 if kind == 0 else 1)) % 4
            zcopy(group, kind, near).wait_recv()
            zcopy(group, kind + 2, near).start()

    def join(group):
        first, count = groups[group]
        for kind in (2, 3):
            zcopy(group, kind, (iz + 2) % 4).wait_recv()
        total = None
        for owner in range(4):
            shape = (block.shape[1], blocks.shape[1])
            row = lax.broadcasted_iota(jnp.int32, shape, 0) + owner * shape[0]
            place = (row == lax.broadcasted_iota(jnp.int32, shape, 1)).astype(F32).astype(BF16)
            part = nn(z_blocks[owner, first : first + count], place)
            total = part if total is None else total + part
        blocks[first : first + count] = total.astype(BF16)

    attn_blocks = (blocks.at[pl.ds(0, QKV_ROWS)], blocks.at[pl.ds(QKV_ROWS, OUT_ROWS)])
    up_block = blocks.at[pl.ds(ATTN_ROWS, FF_ROWS)]
    a_begin, a_middle, a_finish, a_end, a_at = ring_gather(
        ATTN_FLOWS,
        attn_blocks,
        lambda slab, x, y, rows, z: (slabs_q, slabs_o)[slab].at[x, y, core, rows],
        sems[0],
        sems[1],
    )
    f_begin, f_middle, f_finish, f_end, _ = ring_gather(
        UP_FLOWS, (up_block,), lambda slab, x, y, rows, z: up_w.at[x, y, rows], sems[2], sems[3]
    )
    swaps = []

    def swap(flow, part, owner):
        slab, first, count, _, _ = ATTN_FLOWS[flow]
        rows = pl.ds(first, count)
        every = pl.ds(0, 4)
        by_x = "xy"[(ATTN_FLOWS[flow][4] + 1) % 2] == "x"

        def view(which):
            ref = (slabs_q, slabs_o)[slab]
            return ref.at[owner if by_x else every, every if by_x else owner, which, rows]

        def copy(which):
            return remote(
                view(which), view(which), core_send.at[flow, part], core_recv.at[flow, part], {"core": 1 - core}
            )

        copy(core).start()
        swaps.append((copy(core), copy(1 - core)))

    join(0)
    slabs_q[ix, iy, core] = blocks[:QKV_ROWS]
    slabs_o[ix, iy, core] = blocks[QKV_ROWS:ATTN_ROWS]
    a_begin(0)
    join(1)
    f_begin(0)
    own_up = pltpu.make_async_copy(up_block, up_w.at[ix, iy], local.at[3])
    own_up.start()
    a_middle(0)
    a_finish(0)
    a_begin(1)
    for flow in range(len(ATTN_FLOWS)):
        swap(flow, 0, a_at(flow, 1, 0))
    d_middle(1)
    d_finish(1)
    d_begin(2)
    f_middle(0)
    f_finish(0)
    own_up.wait()

    x_end()
    lay_out(lambda device: x_got[device, :34].astype(F32), quad, x_ref)
    eye_shape = (48, 128)
    eye = lax.broadcasted_iota(jnp.int32, eye_shape, 0) == lax.broadcasted_iota(jnp.int32, eye_shape, 1)
    eye = eye.astype(F32).astype(BF16)

    def vectors(device):
        rows = x_got[device, 32:48, :128]
        turned = nt(eye, rows)
        return turned[:34]

    lay_out(vectors, vector_quad, vector_ref)

    def vector(i):
        return vector_ref[:, 2 + i : 3 + i]

    normed1, standard1, inv_std1 = norm_in(x_ref[...], vector(3), vector(4))
    full = x_ref.shape[0]
    extra = normed1_ref.shape[0] - full
    ones_row = (lax.broadcasted_iota(jnp.int32, (extra, 256), 0) == 0).astype(F32).astype(BF16)
    normed1_ref[:full] = normed1
    normed1_ref[full:] = ones_row
    standard1_ref[...] = standard1
    inv_std1_ref[...] = inv_std1

    a_middle(1, swap)
    f_begin(1)
    a_finish(1, swap)
    for out, come in swaps:
        come.wait_recv()

    keep = [
        pltpu.make_async_copy(slabs_q, qkv_w, local.at[4]),
        pltpu.make_async_copy(slabs_o, out_w, local.at[5]),
    ]
    for c in keep:
        c.start()

    def project(step, _):
        w = slabs_q[step // 2, pl.ds(step % 2 * 2, 2)]
        quads[...] = nn(w.reshape(4 * QKV_ROWS, full), normed1_ref[:full])
        rows = pl.ds(pl.multiple_of(step * 136, 8), 136)
        for j in range(3):
            for part in range(4):
                quad[34 * part : 34 * part + 34] = quads[112 * part + 34 * j : 112 * part + 34 * j + 34]
            value = quad[...]
            if j != 1:
                value = value + vector_ref[rows, 2 + j // 2 : 3 + j // 2]
            natural[j, rows] = value
        return 0

    lax.fori_loop(0, 8, project, 0)
    count = jnp.where(unit_place() == 0, 3, 2)
    begin, arrive, sent = head_swap(send, qkv_ref, sems[4], sems[5])
    begin_result, pass_on, finish = result_swap(out_ref, got, sems[6], sems[7])
    for slot in range(3):

        def heads(y, _, slot=slot):
            head = slot * 8 + y * 2 + core if slot < 2 else HEADS - 1
            start = head * HD if slot == 2 else pl.multiple_of(head * HD, HD)
            for j in range(3):
                send[y, slot, j] = natural[j, pl.ds(start, HD)].astype(BF16)
            return 0

        lax.fori_loop(0, 4, heads, 0)
        begin(slot)

    g_begin()

    def unit(slot, _):
        arrive(slot)
        q = qkv_ref[slot, 0] * (HD**-0.5)
        k = qkv_ref[slot, 1].T
        v = qkv_ref[slot, 2]
        for start in range(0, q.shape[1], QB):
            keys = start + QB
            scores = masked_scores(
                k, q[:, start:keys], seg_col_ref[...], seg_row_ref[...], start, keys
            )
            top = jnp.max(scores, 0, keepdims=True)
            weights = jnp.exp(scores - top)
            total = jnp.sum(weights, 0, keepdims=True)
            result = nn(v[:, :keys], weights.astype(BF16)) * (1.0 / total)
            out_ref[slot, 0, :, start:keys] = result.astype(BF16)
            lse_ref[slot, :, start:keys] = top + jnp.log(total)
        begin_result(slot)
        return 0

    d_middle(2)
    lax.fori_loop(0, count, unit, 0)
    f_middle(1)
    sent()
    pass_on()
    finish(count)

    for head in range(HEADS):
        owner = head % 8
        attn_ref[head * HD : head * HD + HD] = got[owner // 2, owner % 2, head // 8, 0]

    def project_out(step, _):
        w = slabs_o[step // 2, pl.ds(step % 2 * 2, 2)]
        result = nn(w.reshape(4 * OUT_ROWS, full), attn_ref[...])
        quads[: 4 * OUT_ROWS] = result
        rows = pl.ds(pl.multiple_of(step * 136, 8), 136)
        for part in range(4):
            quad[34 * part : 34 * part + 34] = quads[48 * part : 48 * part + 34]
        resid_ref[rows] = x_ref[rows] + quad[...] + vector_ref[rows, 4:5]
        return 0

    lax.fori_loop(0, 8, project_out, 0)
    normed2, standard2, inv_std2 = norm_in(resid_ref[...], vector(5), vector(6))
    normed2_ref[:full] = normed2
    normed2_ref[full:] = ones_row
    standard2_ref[...] = standard2
    inv_std2_ref[...] = inv_std2
    g_end()
    lay_out(lambda device: g_got[device, :34].astype(F32), quad, natural.at[0])
    g_ref[...] = natural[0].astype(BF16)

    f_finish(1)
    d_finish(2)
    a_end()
    f_end()
    d_end()
    for group in range(2):
        for kind in range(4):
            zcopy(group, kind, iz).wait_send()
    for out, _ in swaps:
        out.wait_send()
    for c in keep:
        c.wait()


def front(x_src, g_src, block, down_block, seg_row, seg_col):
    length = seg_row.shape[1]
    full = 4 * block.shape[1]
    total = block.shape[0]
    flat = jax.ShapeDtypeStruct((full, 256), F32)
    low = jax.ShapeDtypeStruct((full, 256), BF16)
    stat = jax.ShapeDtypeStruct((1, 256), F32)
    return pl.pallas_call(
        front_kernel,
        in_specs=[ANY, ANY, VMEM, ANY, VMEM, VMEM],
        out_specs=[ANY] * 4 + [VMEM] * 13,
        out_shape=[
            jax.ShapeDtypeStruct((4, 4, 2, QKV_ROWS, full), BF16),
            jax.ShapeDtypeStruct((4, 4, 2, OUT_ROWS, full), BF16),
            jax.ShapeDtypeStruct((4, 4, FF_ROWS, full), BF16),
            jax.ShapeDtypeStruct((4, 4, 4, DOWN_ROWS, DOWN_MAIN), BF16),
            low,
            jax.ShapeDtypeStruct((WIDE, 256), BF16),
            flat,
            stat,
            jax.ShapeDtypeStruct((3, 3, HD, length), BF16),
            jax.ShapeDtypeStruct((3, 1, HD, length), BF16),
            jax.ShapeDtypeStruct((3, 1, length), F32),
            low,
            flat,
            jax.ShapeDtypeStruct((WIDE, 256), BF16),
            flat,
            stat,
            jax.ShapeDtypeStruct((full, 16), F32),
        ],
        scratch_shapes=[
            pltpu.VMEM((4, total, block.shape[1]), BF16),
            pltpu.VMEM((total, full), BF16),
            pltpu.VMEM((32, 48, 256), BF16),
            pltpu.VMEM((32, 48, 256), BF16),
            pltpu.VMEM((136, 256), F32),
            pltpu.VMEM((4 * QKV_ROWS, 256), F32),
            pltpu.VMEM((136, 16), F32),
            pltpu.VMEM((3, full, 256), F32),
            pltpu.VMEM((full, 256), F32),
            pltpu.VMEM((4, 4, 2, QKV_ROWS, full), BF16),
            pltpu.VMEM((4, 4, 2, OUT_ROWS, full), BF16),
            pltpu.VMEM((4, 3, 3, HD, 256), BF16),
            pltpu.VMEM((4, 2, 3, 1, HD, 256), BF16),
            DMA((32,)),
            DMA((32,)),
            DMA((32,)),
            DMA((32,)),
            DMA((2, 4)),
            DMA((2, 4)),
            DMA((3, 4)),
            DMA((3, 4)),
            DMA((6,)),
            DMA((3, 2, 4)),
            DMA((3, 2, 4)),
            DMA((2, 2, 4)),
            DMA((2, 2, 4)),
            DMA((3, 3)),
            DMA((3, 3)),
            DMA((3, 4)),
            DMA((3, 4)),
            DMA((1, 3, 4)),
            DMA((1, 3, 4)),
        ],
        compiler_params=params(0, 60),
    )(x_src, g_src, block, down_block, seg_row, seg_col)


def regroup(step, source, target):
    quad = source[pl.ds(pl.multiple_of(step * 136, 8), 136)]
    for part in range(4):
        target(part, quad[34 * part : 34 * part + 34])


def back_kernel(
    send,
    seg_row_ref,
    seg_col_ref,
    qkv_ref,
    out_ref,
    lse_ref,
    wide,
    out_in,
    dhidden_ref,
    normed2_ref,
    active_ref,
    g_ref,
    qkv_w,
    normed_ref,
    standard_ref,
    inv_std_ref,
    gain_ref,
    dresid_ref,
    bias_ref,
    layer_out,
    input_out,
    main_out,
    tail_out,
    down_out,
    column_out,
    wide_got,
    input_got,
    up_in,
    down_in,
    grad_ref,
    dqkv_ref,
    dk_ref,
    dv_ref,
    got,
    natural,
    slab_ref,
    slabs,
    w_buf,
    acc,
    columns,
    column_slab,
    column_part,
    column_sum,
    z_column,
    input_slab,
    input_slabs,
    qkv_part,
    sums,
    z_main,
    z_tail,
    wsend,
    wrecv,
    isend,
    irecv,
    zsend,
    zrecv,
    local,
    w_sem,
    *rest,
):
    place = greet_col()
    ix, iy, core, iz = (lax.axis_index(a) for a in ("x", "y", "core", "row"))
    xy = ix * 4 + iy
    for step in range(1, 4):
        signal(ring("row", step))
    pl.semaphore_wait(pltpu.get_barrier_semaphore(), 34)
    count = jnp.where(unit_place() == 0, 3, 2)
    begin, arrive, sent = head_swap(send, grad_ref, rest[0], rest[1])
    begin_result, pass_on, finish = result_swap(dqkv_ref, got, rest[2], rest[3])
    counts = (len(FIRST_FLOWS) * 8, len(LAST_FLOWS) * 8)
    bufs = rest[12:]
    sum_refs = [sums.at[:, pl.ds(at, rows)] for at, rows in zip(SUM_FIRST, SUM_ROWS)]
    first = ring_reduce(FIRST_FLOWS, (out_in, up_in), sum_refs[:2], bufs[: counts[0]], rest[4], rest[5])
    last = ring_reduce(
        LAST_FLOWS, (qkv_part,), sum_refs[2:], bufs[counts[0] : sum(counts)], rest[6], rest[7]
    )
    down = ring_reduce(
        DOWN_FLOWS, (down_in,), (down_out,), bufs[sum(counts) : sum(counts) + 12], rest[8], rest[9], True
    )
    cols = ring_reduce(
        COLUMN_FLOWS, (column_part,), (column_sum,), bufs[sum(counts) + 12 :], rest[10], rest[11]
    )
    for slot in range(3):
        begin(slot)

    def up_part(slab, _):
        part = nt(dhidden_ref[slab], normed2_ref[...])
        up_in[slab // 4, slab % 4] = part.astype(BF16)
        return 0

    lax.fori_loop(0, 16, up_part, 0)
    first[0](0)

    tail_rows = g_ref.shape[0] // 4 - DOWN_MAIN

    def down_part(z):
        start = z * (DOWN_MAIN + tail_rows)
        main = g_ref[pl.ds(pl.multiple_of(start, 16), DOWN_MAIN)]
        tail = g_ref[pl.ds(pl.multiple_of(start + DOWN_MAIN, 16), tail_rows)]

        def one(slab, _):
            units = active_ref[slab]
            down_in[z, slab, :FF_ROWS] = nt(units, main).astype(BF16)
            turned = nt(tail, units).astype(BF16)
            down_in[z, slab, FF_ROWS:] = jnp.concatenate(
                [turned, jnp.zeros((tail_rows, DOWN_MAIN - FF_ROWS), BF16)], 1
            )
            return 0

        lax.fori_loop(0, 16, one, 0)

    down_part((iz + 2) % 4)
    down[0](0, (0, 1))

    def copy_wide(step, owner):
        peer = (place + step) % 32
        return remote(
            wide.at[peer], wide_got.at[owner], wsend.at[step], wrecv.at[step], col_device(peer)
        )

    def begin_wide(step, _):
        copy_wide(step, place).start()
        return 0

    own = pltpu.make_async_copy(wide.at[place], wide_got.at[place], local)
    own.start()

    def copy_w(step):
        return pltpu.make_async_copy(
            qkv_w.at[pl.ds(step * 4, 4)], w_buf.at[step % 2], w_sem.at[step % 2]
        )

    copy_w(0).start()

    def unit(slot, _):
        arrive(slot)
        q = qkv_ref[slot, 0] * (HD**-0.5)
        key_cols = qkv_ref[slot, 1]
        k = key_cols.T
        v = qkv_ref[slot, 2].T
        grad = grad_ref[slot, 0]
        delta = jnp.sum(grad.astype(F32) * out_ref[slot, 0].astype(F32), 0, keepdims=True)
        dk_ref[...] = jnp.zeros_like(dk_ref)
        dv_ref[...] = jnp.zeros_like(dv_ref)
        for start in range(0, q.shape[1], QB):
            keys = start + QB
            scores = masked_scores(
                k, q[:, start:keys], seg_col_ref[...], seg_row_ref[...], start, keys
            )
            weights = jnp.exp(scores - lse_ref[slot, :, start:keys])
            dweights = nn(v[:keys], grad[:, start:keys])
            dscores = (weights * (dweights - delta[:, start:keys])).astype(BF16)
            dq = nn(key_cols[:, :keys], dscores) * (HD**-0.5)
            dqkv_ref[slot, 0, :, start:keys] = dq.astype(BF16)
            dk_ref[:, :keys] += nt(q[:, start:keys], dscores)
            dv_ref[:, :keys] += nt(grad[:, start:keys], weights.astype(BF16))
        dqkv_ref[slot, 1] = dk_ref[...].astype(BF16)
        dqkv_ref[slot, 2] = dv_ref[...].astype(BF16)
        begin_result(slot)
        return 0

    lax.fori_loop(0, count, unit, 0)
    first[1](0)
    down_part((iz + 1) % 4)
    down_part((iz + 3) % 4)
    down[0](0, (2, 3))
    down[1](0)
    down_part(iz)
    lax.fori_loop(1, 32, begin_wide, 0)
    sent()
    pass_on()
    finish(count)

    for head in range(HEADS):
        owner = head % 8
        for j in range(3):
            natural[j, head * HD : head * HD + HD] = got[owner // 2, owner % 2, head // 8, j].astype(F32)
    slab_ref[...] = jnp.zeros_like(slab_ref)
    acc[...] = jnp.zeros_like(acc)

    def by_slab(step, _):
        for j in range(3):

            def put(part, rows, j=j):
                slab_ref[part, 34 * j : 34 * j + 34] = rows

            regroup(step, natural.at[j], put)
        four = slab_ref[...].astype(BF16)
        slabs[pl.ds(step * 4, 4)] = four
        return 0

    lax.fori_loop(0, 8, by_slab, 0)

    def weight_part(step, _):
        index = step * 2 + core
        part = nt(slabs[index], normed_ref[...])
        qkv_part[step // 4, step % 4] = part.astype(BF16)
        return 0

    lax.fori_loop(0, 16, weight_part, 0)
    last[0](0)

    def product(step, _):
        @pl.when(step < 7)
        def _():
            copy_w(step + 1).start()

        copy_w(step).wait()
        acc[...] += lax.dot_general(
            slabs[pl.ds(step * 4, 4)].reshape(4 * QKV_ROWS, 256),
            w_buf[step % 2].reshape(4 * QKV_ROWS, -1),
            (((0,), (0,)), ((), ())),
            preferred_element_type=F32,
        )
        return 0

    lax.fori_loop(0, 8, product, 0)
    last[1](0)
    first[2](0)
    first[0](1)

    late = [
        pltpu.make_async_copy(standard_ref, natural.at[1], w_sem.at[0]),
        pltpu.make_async_copy(dresid_ref, natural.at[2], w_sem.at[1]),
    ]
    for c in late:
        c.start()
    dnormed = acc[...].T
    for c in late:
        c.wait()
    standard = natural[1]
    dv = dnormed * gain_ref[...]
    back = inv_std_ref[...] * (
        dv - jnp.mean(dv, 0, keepdims=True) - standard * jnp.mean(dv * standard, 0, keepdims=True)
    )
    natural[0] = natural[2] + back
    lane = lax.broadcasted_iota(jnp.int32, columns.shape, 1)
    gain_col = jnp.sum(dnormed * standard, 1, keepdims=True)
    shift_col = jnp.sum(dnormed, 1, keepdims=True)
    columns[...] = jnp.where(lane == 65, gain_col, jnp.where(lane == 66, shift_col, 0.0))
    input_slab[...] = jnp.zeros_like(input_slab)
    column_slab[...] = jnp.zeros_like(column_slab)

    def spread(step, _):
        def put(part, rows):
            input_slab[part, :34] = rows

        def put_column(part, rows):
            column_slab[step * 4 + part, :34] = rows

        regroup(step, natural.at[0], put)
        regroup(step, columns, put_column)
        input_slabs[pl.ds(step * 4, 4)] = input_slab[...].astype(BF16)
        return 0

    lax.fori_loop(0, 8, spread, 0)

    def copy_input(step, owner):
        peer = (xy + step) % 16
        return remote(
            input_slabs.at[peer * 2 + core],
            input_got.at[owner],
            isend.at[step],
            irecv.at[step],
            {"x": peer // 4, "y": peer % 4},
        )

    def own_columns(step, _):
        column_part[step // 4, step % 4] = column_slab[step * 2 + core].astype(BF16)
        return 0

    lax.fori_loop(0, 16, own_columns, 0)
    cols[0](0)
    down[2](0)
    down[0](1)

    def begin_input(step, _):
        copy_input(step, xy).start()
        return 0

    lax.fori_loop(1, 16, begin_input, 0)
    input_got[xy] = input_slabs[xy * 2 + core]

    def z_columns(step):
        return remote(
            column_sum, z_column.at[pl.ds(step - 1, 1)], zsend.at[2, 0, step - 1], zrecv.at[2, 0, step - 1], ring("row", step)
        )

    def z_copies(group, step):
        rows = pl.ds(0, SUM_FIRST[2]) if group == 0 else pl.ds(SUM_FIRST[2], QKV_ROWS)
        window = pl.ds(pl.multiple_of((iz + step) % 4 * 256, 256), WINDOW)
        return [
            remote(
                sums.at[0, rows, lanes],
                out.at[step - 1, rows],
                zsend.at[group, i, step - 1],
                zrecv.at[group, i, step - 1],
                ring("row", step),
            )
            for i, (lanes, out) in enumerate(((window, z_main), (pl.ds(WIDE - LANE, LANE), z_tail)))
        ]

    def begin_z(group):
        for step in range(1, 4):
            for c in z_copies(group, step):
                c.start()

    first[1](1)
    down[1](1)
    first[2](1)
    begin_z(0)
    cols[1](0)
    last[2](0)
    last[0](1)
    cols[2](0)
    cols[0](1)
    down[2](1)
    down[0](2)
    last[1](1)
    cols[1](1)
    down[1](2)
    last[2](1)
    begin_z(1)
    cols[2](1)
    for step in range(1, 4):
        z_columns(step).start()
    down[2](2)
    first[3]()
    last[3]()
    down[3]()
    cols[3]()
    own.wait()

    def end_wide(step, _):
        copy_wide(step, (place + 32 - step) % 32).wait()
        return 0

    lax.fori_loop(1, 32, end_wide, 0)

    def put_layer(chip, _):
        halves = wide_got[chip * 2, :34].astype(F32) + wide_got[chip * 2 + 1, :34].astype(F32)
        layer_out[:, rows_of(chip * 256)] = halves + bias_ref[...]
        return 0

    lax.fori_loop(0, 16, put_layer, 0)

    def end_input(step, _):
        copy_input(step, (xy + 16 - step) % 16).wait()
        return 0

    lax.fori_loop(1, 16, end_input, 0)

    def put_input(chip, _):
        input_out[:, rows_of(chip * 256)] = input_got[chip, :34].astype(F32)
        return 0

    lax.fori_loop(0, 16, put_input, 0)
    for group in range(2):
        for step in range(1, 4):
            for c in z_copies(group, step):
                c.wait()
    for step in range(1, 4):
        z_columns(step).wait()
    column_out[...] = column_sum[0].astype(F32) + sum(z_column[i].astype(F32) for i in range(3))
    window = pl.ds(pl.multiple_of(iz * 256, 256), WINDOW)
    main_out[...] = sums[0, :, window].astype(F32) + sum(z_main[i].astype(F32) for i in range(3))
    tail_out[...] = sums[0, :, WIDE - LANE :].astype(F32) + sum(z_tail[i].astype(F32) for i in range(3))


def attend_back(
    send, seg_row, seg_col, qkv, out, lse, wide, out_part, dhidden, normed2, active, g, qkv_w, normed, standard, inv_std, gain, dresid, bias
):
    length = seg_row.shape[1]
    full = qkv_w.shape[-1]
    first_sems, first_bufs = ring_bufs(FIRST_FLOWS, WIDE)
    last_sems, last_bufs = ring_bufs(LAST_FLOWS, WIDE)
    down_sems, down_bufs = ring_bufs(DOWN_FLOWS, DOWN_MAIN, True)
    column_sems, column_bufs = ring_bufs(COLUMN_FLOWS, LANE)
    total = sum(SUM_ROWS)
    return pl.pallas_call(
        back_kernel,
        in_specs=[VMEM] * 6 + [ANY] + [VMEM] * 5 + [ANY, VMEM, ANY, VMEM, VMEM, ANY, VMEM],
        out_specs=[VMEM] * 6,
        out_shape=[
            jax.ShapeDtypeStruct((34, 4096), F32),
            jax.ShapeDtypeStruct((34, 4096), F32),
            jax.ShapeDtypeStruct((total, WINDOW), F32),
            jax.ShapeDtypeStruct((total, LANE), F32),
            jax.ShapeDtypeStruct((1, DOWN_ROWS, DOWN_MAIN), F32),
            jax.ShapeDtypeStruct((48, LANE), F32),
        ],
        scratch_shapes=[
            pltpu.VMEM(wide.shape, BF16),
            pltpu.VMEM((16, 48, 256), BF16),
            pltpu.VMEM((4, 4, FF_ROWS, WIDE), BF16),
            pltpu.VMEM((4, 16, DOWN_ROWS, DOWN_MAIN), BF16),
            pltpu.VMEM((3, 1, HD, length), BF16),
            pltpu.VMEM((3, 3, HD, length), BF16),
            pltpu.VMEM((HD, length), F32),
            pltpu.VMEM((HD, length), F32),
            pltpu.VMEM((4, 2, 3, 3, HD, 256), BF16),
            pltpu.VMEM((3, full, 256), F32),
            pltpu.VMEM((4, QKV_ROWS, 256), F32),
            pltpu.VMEM((32, QKV_ROWS, 256), BF16),
            pltpu.VMEM((2, 4, QKV_ROWS, full), BF16),
            pltpu.VMEM((256, full), F32),
            pltpu.VMEM((full, LANE), F32),
            pltpu.VMEM((32, 48, LANE), F32),
            pltpu.VMEM((4, 4, 48, LANE), BF16),
            pltpu.VMEM((1, 48, LANE), BF16),
            pltpu.VMEM((3, 48, LANE), BF16),
            pltpu.VMEM((4, 48, 256), F32),
            pltpu.VMEM((32, 48, 256), BF16),
            pltpu.VMEM((4, 4, QKV_ROWS, WIDE), BF16),
            pltpu.VMEM((1, total, WIDE), BF16),
            pltpu.VMEM((3, total, WINDOW), BF16),
            pltpu.VMEM((3, total, LANE), BF16),
            DMA((32,)),
            DMA((32,)),
            DMA((16,)),
            DMA((16,)),
            DMA((3, 2, 3)),
            DMA((3, 2, 3)),
            DMA,
            DMA((2,)),
            DMA((3, 3)),
            DMA((3, 3)),
            DMA((3, 4)),
            DMA((3, 4)),
        ]
        + first_sems
        + last_sems
        + down_sems
        + column_sems
        + first_bufs
        + last_bufs
        + down_bufs
        + column_bufs,
        compiler_params=params(6, 62),
    )(
        send, seg_row, seg_col, qkv, out, lse, wide, out_part, dhidden, normed2, active, g, qkv_w, normed, standard, inv_std, gain, dresid, bias
    )


def norm_back(dn, standard, inv_std, gain):
    dv = dn * gain
    back = inv_std * (
        dv - jnp.mean(dv, 0, keepdims=True) - standard * jnp.mean(dv * standard, 0, keepdims=True)
    )
    return back, jnp.sum(dn * standard, 1), jnp.sum(dn, 1)


def to_heads(v, core):
    n, _, tokens = v.shape
    heads = v.reshape(n, HEADS, HD, tokens).transpose(1, 0, 2, 3)
    pairs = heads[:16].reshape(2, 4, 2, n, HD, tokens)
    mine = lax.dynamic_index_in_dim(pairs, core, 2, keepdims=False)
    last = jnp.broadcast_to(heads[16:], (4, n, HD, tokens))
    return jnp.concatenate([mine.transpose(1, 0, 2, 3, 4), last[:, None]], 1)


def shards(
    layer_input,
    cotangent,
    segments,
    qkv_weight,
    qv_bias,
    out_weight,
    out_bias,
    up_weight,
    up_bias,
    down_weight,
    down_bias,
    first_gain,
    first_shift,
    second_gain,
    second_shift,
):
    ix, iy, core = lax.axis_index("x"), lax.axis_index("y"), lax.axis_index("core")
    width = layer_input.shape[0]
    rows = qkv_weight.shape[0]
    full = 4 * rows
    units = up_weight.shape[1]

    block = jnp.concatenate(
        [
            qkv_weight.transpose(1, 2, 0).reshape(3 * width, rows),
            jnp.pad(up_bias[None], ((0, QKV_ROWS - 3 * width - 1), (0, rows - units))),
            jnp.pad(out_weight.T, ((0, OUT_ROWS - width), (0, 0))),
            jnp.pad(up_weight.T, ((0, FF_ROWS - units), (0, 0))),
        ],
        0,
    )
    down_block = jnp.concatenate(
        [
            jnp.pad(down_weight[:, :DOWN_MAIN], ((0, FF_ROWS - units), (0, 0))),
            jnp.pad(down_weight[:, DOWN_MAIN:].T, ((0, 0), (0, DOWN_MAIN - units))),
        ],
        0,
    )
    small = jnp.concatenate(
        [qv_bias, jnp.stack([out_bias, first_gain, first_shift, second_gain, second_shift])], 0
    )
    small = jnp.tile(jnp.pad(small, ((0, 48 - width - 7), (0, 256 - width))), (1, 16))
    x_src = jnp.concatenate([layer_input, small], 0)
    g_src = jnp.pad(cotangent, ((0, 48 - width), (0, 0)))
    seg = lax.dynamic_index_in_dim(segments, ix, 0, keepdims=False)
    seg_row, seg_col = seg[None], seg[:, None]
    (
        qkv_w,
        out_w,
        up_w,
        down_w,
        g_low,
        normed1,
        standard1,
        inv_std1,
        units_qkv,
        units_out,
        lse,
        attn,
        resid,
        normed2,
        standard2,
        inv_std2,
        vectors,
    ) = front(x_src, g_src, block, down_block, seg_row, seg_col)
    qkv_w = qkv_w.reshape(32, QKV_ROWS, full)
    out_w = out_w.reshape(32, OUT_ROWS, full)
    up_w = up_w.reshape(16, FF_ROWS, full)
    down_w = down_w.reshape(4, 16, DOWN_ROWS, DOWN_MAIN)
    down_tail = down_w[:, :, FF_ROWS:, :FF_ROWS]
    g = g_low.astype(F32)
    gain1, gain2 = vectors[:, 5:6], vectors[:, 7:8]
    hidden_bias = lax.dynamic_index_in_dim(
        qkv_w[:, 3 * width, :units].reshape(16, 2, units), core, 1, keepdims=False
    ).astype(F32)
    hidden_bias = jnp.pad(hidden_bias, ((0, 0), (0, FF_ROWS - units)))
    hidden = jnp.einsum("xfd,dt->xft", up_w, normed2[:full], preferred_element_type=F32) + hidden_bias[..., None]
    active, gelu_back = jax.vjp(lambda h: jax.nn.gelu(h, approximate=True), hidden)
    active = active.astype(BF16)
    active_rows = jnp.pad(active, ((0, 0), (0, DOWN_ROWS - FF_ROWS), (0, 0)))
    out_main = [
        jnp.einsum("xfd,xft->dt", down_w[z], active_rows, preferred_element_type=F32) for z in range(4)
    ]
    out_tail = jnp.einsum("zxdf,xft->zdt", down_tail, active, preferred_element_type=F32)
    ff_out = jnp.concatenate([p for z in range(4) for p in (out_main[z], out_tail[z])], 0)
    send_out = (ff_out + jnp.where(core == 0, 1.0, 0.0) * resid).astype(BF16)
    send_out = jnp.pad(send_out.reshape(32, width, 256), ((0, 0), (0, 48 - width), (0, 0)))
    g_main = [g_low[z * rows : z * rows + DOWN_MAIN] for z in range(4)]
    g_tail = jnp.stack([g_low[z * rows + DOWN_MAIN : z * rows + rows] for z in range(4)])
    dactive = sum(
        jnp.einsum("xfd,dt->xft", down_w[z], g_main[z], preferred_element_type=F32) for z in range(4)
    )[:, :FF_ROWS]
    dactive = dactive + jnp.einsum("zxdf,zdt->xft", down_tail, g_tail, preferred_element_type=F32)
    dhidden = gelu_back(dactive)[0].astype(BF16)
    extra = WIDE - full
    ones_row = jnp.pad(jnp.ones((1, 256), BF16), ((0, extra - 1), (0, 0)))

    def widen(v):
        return jnp.concatenate([v, ones_row], 0)

    dn2 = jnp.einsum("xfd,xft->dt", up_w, dhidden, preferred_element_type=F32)
    dn2 = core_sum(dn2.astype(BF16))
    back2, gain2_grad, shift2_grad = norm_back(dn2, standard2, inv_std2, gain2)
    dresid = g + back2
    dproj = dresid.astype(BF16)
    dproj_block = jnp.pad(dproj.reshape(32, width, 256), ((0, 0), (0, OUT_ROWS - width), (0, 0)))
    dattn = jnp.einsum("ced,cet->dt", out_w, dproj_block, preferred_element_type=F32).astype(BF16)
    mine = lax.dynamic_index_in_dim(dproj_block.reshape(16, 2, OUT_ROWS, 256), core, 1, keepdims=False)
    cols = jnp.stack([jnp.sum(g, -1), gain2_grad, shift2_grad], -1).reshape(16, 2, width, 3)
    cols = lax.dynamic_index_in_dim(cols, core, 1, keepdims=False)
    cols = jnp.pad(cols, ((0, 0), (0, OUT_ROWS - width), (full + 1, extra - 4)))
    out_part = jnp.einsum("xrt,dt->xrd", mine, widen(attn), preferred_element_type=F32) + cols
    layer_output, input_grad, main, tail, down_sum, columns = attend_back(
        to_heads(dattn[None], core),
        seg_row,
        seg_col,
        units_qkv,
        units_out,
        lse,
        send_out,
        out_part.astype(BF16).reshape(4, 4, OUT_ROWS, WIDE),
        dhidden,
        normed2,
        active,
        g_low,
        qkv_w,
        normed1,
        standard1,
        inv_std1,
        gain1,
        dresid,
        down_bias.astype(F32)[:, None],
    )
    main = lax.dynamic_slice_in_dim(main, lax.axis_index("row") * (rows - 256), rows, 1)
    out_first, up_first, qkv_first = SUM_FIRST
    qkv_out = main[qkv_first : qkv_first + 3 * width].reshape(3, width, rows).transpose(2, 0, 1)
    qkv_tail = tail[qkv_first:, LANE - extra :]
    out_tail = tail[out_first : out_first + width, LANE - extra :]
    return (
        layer_output,
        input_grad,
        qkv_out,
        jnp.stack([qkv_tail[:width, 0], qkv_tail[2 * width : 3 * width, 0]]),
        main[out_first : out_first + width].T,
        out_tail[:, 0],
        main[up_first : up_first + units].T,
        tail[up_first : up_first + units, LANE - extra],
        jnp.concatenate([down_sum[0, :units], down_sum[0, FF_ROWS:, :units].T], 1),
        out_tail[:, 1],
        columns[:width, 65],
        columns[:width, 66],
        out_tail[:, 2],
        out_tail[:, 3],
    )


def solution(mesh):
    split = Mesh(mesh.devices.reshape(4, 4, 4, 2), ("row", "x", "y", "core"))
    vec = P(COL)
    return jax.shard_map(
        shards,
        mesh=split,
        in_specs=(
            P(COL, "row"),
            P(COL, "row"),
            P("row", None),
            P("row", None, COL),
            P(None, COL),
            P("row", COL),
            vec,
            P("row", COL),
            vec,
            P(COL, "row"),
            vec,
            vec,
            vec,
            vec,
            vec,
        ),
        out_specs=(
            P(COL, "row"),
            P(COL, "row"),
            P("row", None, COL),
            P(None, COL),
            P("row", COL),
            vec,
            P("row", COL),
            vec,
            P(COL, "row"),
            vec,
            vec,
            vec,
            vec,
            vec,
        ),
        check_vma=False,
    )
```

```python
import jax
import jax.numpy as jnp
from jax import lax
from jax.experimental import pallas as pl
from jax.experimental.pallas import tpu as pltpu
from jax.sharding import Mesh, PartitionSpec as P

HEADS = 17
HD = 64
EPS = 1e-05
XY = ("x", "y")
COL = ("x", "y", "core")
F32 = jnp.float32
BF16 = jnp.bfloat16
QB = 256


def nn(a, b):
    return lax.dot_general(a, b, (((1,), (0,)), ((), ())), preferred_element_type=F32)


def nt(a, b):
    return lax.dot_general(a, b, (((1,), (1,)), ((), ())), preferred_element_type=F32)


MESH = pl.DeviceIdType.MESH
ANY = pl.BlockSpec(memory_space=pl.ANY)
VMEM = pl.BlockSpec(memory_space=pltpu.VMEM)
DMA = pltpu.SemaphoreType.DMA


def params(collective_id, vmem=56):
    return pltpu.CompilerParams(
        collective_id=collective_id, has_side_effects=True, vmem_limit_bytes=vmem * 2**20
    )


def remote(src, dst, send_sem, recv_sem, where):
    return pltpu.make_async_remote_copy(
        src_ref=src,
        dst_ref=dst,
        send_sem=send_sem,
        recv_sem=recv_sem,
        device_id=where,
        device_id_type=MESH,
    )


def signal(where):
    pl.semaphore_signal(
        pltpu.get_barrier_semaphore(), inc=1, device_id=where, device_id_type=MESH
    )


def col_place():
    return (lax.axis_index("x") * 4 + lax.axis_index("y")) * 2 + lax.axis_index("core")


def col_device(place):
    return {"x": place // 8, "y": place // 2 % 4, "core": place % 2}


def greet_col():
    me = col_place()

    def greet(step, _):
        signal(col_device((me + step) % 32))
        return 0

    lax.fori_loop(1, 32, greet, 0)
    return me


def rows_of(n):
    return pl.ds(pl.multiple_of(n, 256), 256)


def token_swap(src, out, send, recv, local, me):
    def copy(step, owner):
        peer = (me + step) % 32
        return remote(
            src.at[:, rows_of(peer // 2 * 256)], out.at[owner], send.at[step], recv.at[step], col_device(peer)
        )

    own = pltpu.make_async_copy(src.at[:, rows_of(me // 2 * 256)], out.at[me], local)

    def begin():
        def one(step, _):
            copy(step, me).start()
            return 0

        lax.fori_loop(1, 32, one, 0)
        own.start()

    def end():
        def one(step, _):
            copy(step, (me + 32 - step) % 32).wait()
            return 0

        lax.fori_loop(1, 32, one, 0)
        own.wait()

    return begin, end


def ring(axis, step):
    return {axis: (lax.axis_index(axis) + 4 + step) % 4}


QKV_ROWS, OUT_ROWS, FF_ROWS = 112, 48, 144
ATTN_ROWS = QKV_ROWS + OUT_ROWS
ATTN_FLOWS = ((0, 0, 32, 16, 0), (1, 0, 48, 16, 0), (0, 32, 80, 32, 1))
UP_FLOWS = ((0, 0, 64, 32, 0), (0, 64, 80, 32, 1))
DOWN_FLOWS = ((0, 0, 160, 80, 1),)
DOWN_ROWS, DOWN_MAIN = 160, 256
FIRST_FLOWS = ((0, 0, 48, 16, 0), (1, 0, 48, 16, 0), (1, 48, 96, 48, 1))
LAST_FLOWS = ((0, 0, 48, 16, 0), (0, 48, 64, 32, 1))
COLUMN_FLOWS = ((0, 0, 48, 16, 0),)
WIDE, WINDOW, LANE = 1152, 384, 128
SUM_ROWS = (OUT_ROWS, FF_ROWS, QKV_ROWS)
SUM_FIRST = (0, 48, 192)


def ring_gather(flows, blocks, place, send, recv, stages=2):
    ix, iy, iz = (lax.axis_index(a) for a in ("x", "y", "row"))
    every = range(len(flows))

    def axis_of(flow, stage):
        return "row" if stage == 2 else "xy"[(flows[flow][4] + stage) % 2]

    def region(flow, stage, owner, half=None):
        by_x = axis_of(flow, stage) == "x"
        slab, first, count, cut, _ = flows[flow]
        if stage == 0:
            row, rows = ((0, count), (0, cut), (cut, count - cut))[0 if half is None else half + 1]
            return place(slab, owner if by_x else ix, iy if by_x else owner, pl.ds(first + row, rows), iz)
        part = pl.ds(0, 4) if half is None else pl.ds(2 * half, 2)
        if stage == 2:
            return place(slab, part, pl.ds(0, 4), pl.ds(first, count), owner)
        return place(slab, owner if by_x else part, part if by_x else owner, pl.ds(first, count), iz)

    def copy(flow, stage, kind, owner):
        half = None if kind < 2 else kind - 2
        there = region(flow, stage, owner, half)
        if stage == 0 and kind < 2:
            slab, first, count, _, _ = flows[flow]
            here = blocks[slab].at[pl.ds(first, count)]
        else:
            here = there
        return remote(
            here,
            there,
            send.at[flow, stage, kind],
            recv.at[flow, stage, kind],
            ring(axis_of(flow, stage), 1 if kind % 2 == 0 else -1),
        )

    def at(flow, stage, step):
        return (lax.axis_index(axis_of(flow, stage)) + 4 + step) % 4

    def begin(stage):
        for flow in every:
            for kind in (0, 1):
                copy(flow, stage, kind, at(flow, stage, 0)).start()

    def middle(stage, then=None):
        for flow in every:
            for kind, step in ((0, -1), (1, 1)):
                owner = at(flow, stage, step)
                copy(flow, stage, kind, owner).wait_recv()
                copy(flow, stage, kind + 2, owner).start()
                if then is not None:
                    then(flow, 1 + kind, owner)

    def finish(stage, then=None):
        for flow in every:
            owner = at(flow, stage, 2)
            for kind in (2, 3):
                copy(flow, stage, kind, owner).wait_recv()
            if then is not None:
                then(flow, 3, owner)

    def end():
        for stage in range(stages):
            for flow in every:
                for kind in range(4):
                    copy(flow, stage, kind, at(flow, stage, 0)).wait_send()

    return begin, middle, finish, end, at


def lay_out(source, quad, target, lanes=slice(None)):
    def one(step, _):
        for part in range(4):
            quad[34 * part : 34 * part + 34] = source(step * 4 + part)
        target[pl.ds(pl.multiple_of(step * 136, 8), 136)] = quad[...].astype(target.dtype)
        return 0

    lax.fori_loop(0, 8, one, 0)


def norm_in(v, gain, shift):
    centred = v - jnp.mean(v, 0, keepdims=True)
    inv_std = lax.rsqrt(jnp.mean(centred * centred, 0, keepdims=True) + EPS)
    standard = centred * inv_std
    return (standard * gain + shift).astype(BF16), standard, inv_std


def add_rows(out, *terms):
    def one(i, _):
        out[i] = sum(t[i].astype(F32) for t in terms).astype(out.dtype)
        return 0

    lax.fori_loop(0, out.shape[0], one, 0)


def ring_reduce(flows, ins, outs, bufs, send, recv, by_z=False):
    every = range(len(flows))
    stages = 3 if by_z else 2

    def axis_of(flow, stage):
        return ("row", "x", "y")[stage] if by_z else "yx"[(flows[flow][4] + stage) % 2]

    def at(flow, stage, step):
        return (lax.axis_index(axis_of(flow, stage)) + 4 + step) % 4

    def held(flow, stage):
        first = (flow * stages + stage) * 4
        return bufs[first : first + 4]

    def chunk(flow, stage, owner, half=None):
        slab, first, count, cut, _ = flows[flow]
        if stage == stages - 1:
            row, rows = ((0, count), (0, cut), (cut, count - cut))[0 if half is None else half + 1]
            return held(flow, stage - 1)[2].at[pl.ds(owner, 1), pl.ds(row, rows)]
        if stage == 1:
            return held(flow, 0)[2].at[pl.ds(owner * 4, 4) if half is None else pl.ds(owner * 4 + 2 * half, 2)]
        window = pl.ds(first, count)
        ref = ins[slab]
        if by_z:
            return ref.at[owner, pl.ds(0, 16) if half is None else pl.ds(8 * half, 8), window]
        part = pl.ds(0, 4) if half is None else pl.ds(2 * half, 2)
        return ref.at[part, owner, window] if axis_of(flow, 0) == "y" else ref.at[owner, part, window]

    def part_of(flow, stage, ref, half):
        if stage < stages - 1:
            count = ref.shape[0] // 2
            return ref.at[pl.ds(count * half, count)]
        _, _, count, cut, _ = flows[flow]
        return ref.at[:, pl.ds(0, cut) if half == 0 else pl.ds(cut, count - cut)]

    def copy(flow, stage, kind):
        from_left, from_right, all_left, all_right = held(flow, stage)
        right = kind % 2 == 0
        if kind < 2:
            src, dst = chunk(flow, stage, at(flow, stage, 2), kind), (from_left, from_right)[kind]
        elif kind < 4:
            src = chunk(flow, stage, at(flow, stage, 1 if right else -1), 1 if right else 0)
            dst = part_of(flow, stage, all_left if right else all_right, 1 if right else 0)
        else:
            src = from_left if right else from_right
            dst = part_of(flow, stage, all_left if right else all_right, 0 if right else 1)
        return remote(
            src,
            dst,
            send.at[flow, stage, kind],
            recv.at[flow, stage, kind],
            ring(axis_of(flow, stage), 1 if right else -1),
        )

    def begin(stage, kinds=(0, 1, 2, 3)):
        for kind in kinds:
            for flow in every:
                copy(flow, stage, kind).start()

    def middle(stage):
        for flow in every:
            from_left, from_right = held(flow, stage)[:2]
            for kind, buf, step in ((0, from_left, 1), (1, from_right, -1)):
                copy(flow, stage, kind).wait_recv()
                add_rows(buf, buf, chunk(flow, stage, at(flow, stage, step), kind))
                copy(flow, stage, kind + 4).start()

    def finish(stage):
        for flow in every:
            all_left, all_right = held(flow, stage)[2:4]
            for kind in (2, 3, 4, 5):
                copy(flow, stage, kind).wait_recv()
            out = all_left
            if stage == stages - 1:
                slab, first, count, _, _ = flows[flow]
                out = outs[slab].at[:, pl.ds(first, count)]
            add_rows(out, chunk(flow, stage, at(flow, stage, 0)), all_left, all_right)

    def end():
        for stage in range(stages):
            for flow in every:
                for kind in range(6):
                    copy(flow, stage, kind).wait_send()

    return begin, middle, finish, end


def ring_bufs(flows, columns, by_z=False):
    stages = 3 if by_z else 2
    bufs = []
    for _, _, count, cut, _ in flows:
        for n in (16, 4) if by_z else (4,):
            bufs += [(n // 2, count), (n // 2, count), (n, count), (n, count)]
        bufs += [(1, cut), (1, count - cut), (1, count), (1, count)]
    sems = [DMA((len(flows), stages, 6)), DMA((len(flows), stages, 6))]
    return sems, [pltpu.VMEM((n, rows, columns), BF16) for n, rows in bufs]


def core_kernel(mine, total, got, send, recv):
    partner = {"core": 1 - lax.axis_index("core")}
    signal(partner)
    pl.semaphore_wait(pltpu.get_barrier_semaphore(), 1)
    copy = remote(mine, got, send, recv, partner)
    copy.start()
    copy.wait()
    total[...] = mine[...].astype(F32) + got[...].astype(F32)


def core_sum(mine):
    return pl.pallas_call(
        core_kernel,
        in_specs=[VMEM],
        out_specs=VMEM,
        out_shape=jax.ShapeDtypeStruct(mine.shape, F32),
        scratch_shapes=[pltpu.VMEM(mine.shape, mine.dtype), DMA, DMA],
        compiler_params=params(4),
    )(mine)


def masked_scores(k, q_block, seg_col, seg_row, start, keys):
    scores = nn(k[:keys], q_block)
    key_pos = lax.broadcasted_iota(jnp.int32, scores.shape, 0)
    query_pos = lax.broadcasted_iota(jnp.int32, scores.shape, 1) + start
    allowed = (key_pos <= query_pos) & (seg_col[:keys] == seg_row[:, start : start + QB])
    return jnp.where(allowed, scores, -1e30)


def unit_place():
    return lax.axis_index("y") * 2 + lax.axis_index("core")


def unit_device(place):
    return {"y": place // 2, "core": place % 2}


def head_swap(send, units, sems, rsems):
    iy = lax.axis_index("y")

    def copy(slot, step, owner):
        return remote(
            send.at[(iy + step) % 4, slot],
            units.at[slot, :, :, rows_of(owner * 256)],
            sems.at[slot, step - 1],
            rsems.at[slot, step - 1],
            {"y": (iy + step) % 4},
        )

    def begin(slot):
        for step in range(1, 4):
            if slot < 2:
                copy(slot, step, iy).start()
            else:
                pl.when(((iy + step) % 4 == 0) & (lax.axis_index("core") == 0))(
                    lambda step=step: copy(2, step, iy).start()
                )

    def arrive(slot):
        units[slot, :, :, rows_of(iy * 256)] = send[iy, slot]
        for step in range(1, 4):
            copy(slot, step, (iy + 4 - step) % 4).wait_recv()

    def sent():
        for slot in range(2):
            for step in range(1, 4):
                copy(slot, step, iy).wait_send()
        for step in range(1, 4):
            pl.when(((iy + step) % 4 == 0) & (lax.axis_index("core") == 0))(
                lambda step=step: copy(2, step, iy).wait_send()
            )

    return begin, arrive, sent


def result_swap(units, got, sems, rsems):
    iy, core = lax.axis_index("y"), lax.axis_index("core")

    def copy(slot, step, owner):
        to = (iy + step) % 4
        return remote(
            units.at[slot, :, :, rows_of(to * 256)],
            got.at[owner, core, slot],
            sems.at[slot, step - 1],
            rsems.at[slot, step - 1],
            {"y": to},
        )

    def hand_on(slot, which):
        part = got.at[:, which, slot] if slot < 2 else got.at[pl.ds(0, 1), 0, 2]
        return remote(part, part, sems.at[slot, 3], rsems.at[slot, 3], {"core": 1 - core})

    def begin(slot):
        got[iy, core, slot] = units[slot, :, :, rows_of(iy * 256)]
        for step in range(1, 4):
            copy(slot, step, iy).start()

    def pass_on():
        for slot in range(2):
            for step in range(1, 4):
                copy(slot, step, (iy + 4 - step) % 4).wait_recv()
            hand_on(slot, core).start()

        @pl.when(core == 0)
        def _():
            for step in range(1, 4):
                pl.when(iy == step)(lambda step=step: copy(2, step, 0).wait_recv())
            hand_on(2, 0).start()

    def finish(count):
        for slot in range(2):
            hand_on(slot, 1 - core).wait_recv()
            hand_on(slot, core).wait_send()
        pl.when(core == 1)(lambda: hand_on(2, 0).wait_recv())
        pl.when(core == 0)(lambda: hand_on(2, 0).wait_send())

        def ends(slot, _):
            for step in range(1, 4):
                copy(slot, step, iy).wait_send()
            return 0

        lax.fori_loop(0, count, ends, 0)

    return begin, pass_on, finish


def front_kernel(
    x_src,
    g_src,
    block,
    down_block,
    seg_row_ref,
    seg_col_ref,
    qkv_w,
    out_w,
    up_w,
    down_w,
    g_ref,
    normed1_ref,
    standard1_ref,
    inv_std1_ref,
    qkv_ref,
    out_ref,
    lse_ref,
    attn_ref,
    resid_ref,
    normed2_ref,
    standard2_ref,
    inv_std2_ref,
    vector_ref,
    z_blocks,
    blocks,
    x_got,
    g_got,
    quad,
    quads,
    vector_quad,
    natural,
    x_ref,
    slabs_q,
    slabs_o,
    send,
    got,
    xsend,
    xrecv,
    gsend,
    grecv,
    zsend,
    zrecv,
    core_send,
    core_recv,
    local,
    *sems,
):
    me = greet_col()
    ix, iy, core, iz = (lax.axis_index(a) for a in ("x", "y", "core", "row"))
    for step in (1, -1):
        signal(ring("row", step))
    pl.semaphore_wait(pltpu.get_barrier_semaphore(), 33)
    groups = ((0, ATTN_ROWS), (ATTN_ROWS, FF_ROWS))

    d_begin, d_middle, d_finish, d_end, _ = ring_gather(
        DOWN_FLOWS, (down_block,), lambda slab, x, y, rows, z: down_w.at[z, x, y, rows], sems[8], sems[9], 3
    )

    def zcopy(group, kind, owner):
        first, count = groups[group]
        cut = count // 32 * 16
        part = (pl.ds(first, count), pl.ds(first, cut), pl.ds(first + cut, count - cut))[max(kind - 1, 0)]
        return remote(
            block.at[part] if kind < 2 else z_blocks.at[owner, part],
            z_blocks.at[owner, part],
            zsend.at[group, kind],
            zrecv.at[group, kind],
            ring("row", 1 if kind % 2 == 0 else -1),
        )

    for group in range(2):
        for kind in (0, 1):
            zcopy(group, kind, iz).start()
    x_begin, x_end = token_swap(x_src, x_got, xsend, xrecv, local.at[0], me)
    g_begin, g_end = token_swap(g_src, g_got, gsend, grecv, local.at[1], me)
    d_begin(0)
    own = pltpu.make_async_copy(down_block, down_w.at[iz, ix, iy], local.at[2])
    own.start()
    z_blocks[iz] = block[...]
    d_middle(0)
    d_finish(0)
    own.wait()
    d_begin(1)
    x_begin()
    for group in range(2):
        for kind in (0, 1):
            near = (iz + (3 if kind == 0 else 1)) % 4
            zcopy(group, kind, near).wait_recv()
            zcopy(group, kind + 2, near).start()

    def join(group):
        first, count = groups[group]
        for kind in (2, 3):
            zcopy(group, kind, (iz + 2) % 4).wait_recv()
        total = None
        for owner in range(4):
            shape = (block.shape[1], blocks.shape[1])
            row = lax.broadcasted_iota(jnp.int32, shape, 0) + owner * shape[0]
            place = (row == lax.broadcasted_iota(jnp.int32, shape, 1)).astype(F32).astype(BF16)
            part = nn(z_blocks[owner, first : first + count], place)
            total = part if total is None else total + part
        blocks[first : first + count] = total.astype(BF16)

    attn_blocks = (blocks.at[pl.ds(0, QKV_ROWS)], blocks.at[pl.ds(QKV_ROWS, OUT_ROWS)])
    up_block = blocks.at[pl.ds(ATTN_ROWS, FF_ROWS)]
    a_begin, a_middle, a_finish, a_end, a_at = ring_gather(
        ATTN_FLOWS,
        attn_blocks,
        lambda slab, x, y, rows, z: (slabs_q, slabs_o)[slab].at[x, y, core, rows],
        sems[0],
        sems[1],
    )
    f_begin, f_middle, f_finish, f_end, _ = ring_gather(
        UP_FLOWS, (up_block,), lambda slab, x, y, rows, z: up_w.at[x, y, rows], sems[2], sems[3]
    )
    swaps = []

    def swap(flow, part, owner):
        slab, first, count, _, _ = ATTN_FLOWS[flow]
        rows = pl.ds(first, count)
        every = pl.ds(0, 4)
        by_x = "xy"[(ATTN_FLOWS[flow][4] + 1) % 2] == "x"

        def view(which):
            ref = (slabs_q, slabs_o)[slab]
            return ref.at[owner if by_x else every, every if by_x else owner, which, rows]

        def copy(which):
            return remote(
                view(which), view(which), core_send.at[flow, part], core_recv.at[flow, part], {"core": 1 - core}
            )

        copy(core).start()
        swaps.append((copy(core), copy(1 - core)))

    join(0)
    slabs_q[ix, iy, core] = blocks[:QKV_ROWS]
    slabs_o[ix, iy, core] = blocks[QKV_ROWS:ATTN_ROWS]
    a_begin(0)
    join(1)
    f_begin(0)
    own_up = pltpu.make_async_copy(up_block, up_w.at[ix, iy], local.at[3])
    own_up.start()
    a_middle(0)
    a_finish(0)
    a_begin(1)
    for flow in range(len(ATTN_FLOWS)):
        swap(flow, 0, a_at(flow, 1, 0))
    d_middle(1)
    d_finish(1)
    d_begin(2)
    f_middle(0)
    f_finish(0)
    own_up.wait()

    x_end()
    lay_out(lambda device: x_got[device, :34].astype(F32), quad, x_ref)
    eye_shape = (48, 128)
    eye = lax.broadcasted_iota(jnp.int32, eye_shape, 0) == lax.broadcasted_iota(jnp.int32, eye_shape, 1)
    eye = eye.astype(F32).astype(BF16)

    def vectors(device):
        rows = x_got[device, 32:48, :128]
        turned = nt(eye, rows)
        return turned[:34]

    lay_out(vectors, vector_quad, vector_ref)

    def vector(i):
        return vector_ref[:, 2 + i : 3 + i]

    normed1, standard1, inv_std1 = norm_in(x_ref[...], vector(3), vector(4))
    full = x_ref.shape[0]
    extra = normed1_ref.shape[0] - full
    ones_row = (lax.broadcasted_iota(jnp.int32, (extra, 256), 0) == 0).astype(F32).astype(BF16)
    normed1_ref[:full] = normed1
    normed1_ref[full:] = ones_row
    standard1_ref[...] = standard1
    inv_std1_ref[...] = inv_std1

    a_middle(1, swap)
    f_begin(1)
    a_finish(1, swap)
    for out, come in swaps:
        come.wait_recv()

    keep = [
        pltpu.make_async_copy(slabs_q, qkv_w, local.at[4]),
        pltpu.make_async_copy(slabs_o, out_w, local.at[5]),
    ]
    for c in keep:
        c.start()

    def project(step, _):
        w = slabs_q[step // 2, pl.ds(step % 2 * 2, 2)]
        quads[...] = nn(w.reshape(4 * QKV_ROWS, full), normed1_ref[:full])
        rows = pl.ds(pl.multiple_of(step * 136, 8), 136)
        for j in range(3):
            for part in range(4):
                quad[34 * part : 34 * part + 34] = quads[112 * part + 34 * j : 112 * part + 34 * j + 34]
            value = quad[...]
            if j != 1:
                value = value + vector_ref[rows, 2 + j // 2 : 3 + j // 2]
            natural[j, rows] = value
        return 0

    lax.fori_loop(0, 8, project, 0)
    count = jnp.where(unit_place() == 0, 3, 2)
    begin, arrive, sent = head_swap(send, qkv_ref, sems[4], sems[5])
    begin_result, pass_on, finish = result_swap(out_ref, got, sems[6], sems[7])
    for slot in range(3):

        def heads(y, _, slot=slot):
            head = slot * 8 + y * 2 + core if slot < 2 else HEADS - 1
            start = head * HD if slot == 2 else pl.multiple_of(head * HD, HD)
            for j in range(3):
                send[y, slot, j] = natural[j, pl.ds(start, HD)].astype(BF16)
            return 0

        lax.fori_loop(0, 4, heads, 0)
        begin(slot)

    g_begin()

    def unit(slot, _):
        arrive(slot)
        q = qkv_ref[slot, 0] * (HD**-0.5)
        k = qkv_ref[slot, 1].T
        v = qkv_ref[slot, 2]
        for start in range(0, q.shape[1], QB):
            keys = start + QB
            scores = masked_scores(
                k, q[:, start:keys], seg_col_ref[...], seg_row_ref[...], start, keys
            )
            top = jnp.max(scores, 0, keepdims=True)
            weights = jnp.exp(scores - top)
            total = jnp.sum(weights, 0, keepdims=True)
            result = nn(v[:, :keys], weights.astype(BF16)) * (1.0 / total)
            out_ref[slot, 0, :, start:keys] = result.astype(BF16)
            lse_ref[slot, :, start:keys] = top + jnp.log(total)
        begin_result(slot)
        return 0

    d_middle(2)
    lax.fori_loop(0, count, unit, 0)
    f_middle(1)
    sent()
    pass_on()
    finish(count)

    for head in range(HEADS):
        owner = head % 8
        attn_ref[head * HD : head * HD + HD] = got[owner // 2, owner % 2, head // 8, 0]

    def project_out(step, _):
        w = slabs_o[step // 2, pl.ds(step % 2 * 2, 2)]
        result = nn(w.reshape(4 * OUT_ROWS, full), attn_ref[...])
        quads[: 4 * OUT_ROWS] = result
        rows = pl.ds(pl.multiple_of(step * 136, 8), 136)
        for part in range(4):
            quad[34 * part : 34 * part + 34] = quads[48 * part : 48 * part + 34]
        resid_ref[rows] = x_ref[rows] + quad[...] + vector_ref[rows, 4:5]
        return 0

    lax.fori_loop(0, 8, project_out, 0)
    normed2, standard2, inv_std2 = norm_in(resid_ref[...], vector(5), vector(6))
    normed2_ref[:full] = normed2
    normed2_ref[full:] = ones_row
    standard2_ref[...] = standard2
    inv_std2_ref[...] = inv_std2
    g_end()
    lay_out(lambda device: g_got[device, :34].astype(F32), quad, natural.at[0])
    g_ref[...] = natural[0].astype(BF16)

    f_finish(1)
    d_finish(2)
    a_end()
    f_end()
    d_end()
    for group in range(2):
        for kind in range(4):
            zcopy(group, kind, iz).wait_send()
    for out, _ in swaps:
        out.wait_send()
    for c in keep:
        c.wait()


def front(x_src, g_src, block, down_block, seg_row, seg_col):
    length = seg_row.shape[1]
    full = 4 * block.shape[1]
    total = block.shape[0]
    flat = jax.ShapeDtypeStruct((full, 256), F32)
    low = jax.ShapeDtypeStruct((full, 256), BF16)
    stat = jax.ShapeDtypeStruct((1, 256), F32)
    return pl.pallas_call(
        front_kernel,
        in_specs=[ANY, ANY, VMEM, ANY, VMEM, VMEM],
        out_specs=[ANY] * 4 + [VMEM] * 13,
        out_shape=[
            jax.ShapeDtypeStruct((4, 4, 2, QKV_ROWS, full), BF16),
            jax.ShapeDtypeStruct((4, 4, 2, OUT_ROWS, full), BF16),
            jax.ShapeDtypeStruct((4, 4, FF_ROWS, full), BF16),
            jax.ShapeDtypeStruct((4, 4, 4, DOWN_ROWS, DOWN_MAIN), BF16),
            low,
            jax.ShapeDtypeStruct((WIDE, 256), BF16),
            flat,
            stat,
            jax.ShapeDtypeStruct((3, 3, HD, length), BF16),
            jax.ShapeDtypeStruct((3, 1, HD, length), BF16),
            jax.ShapeDtypeStruct((3, 1, length), F32),
            low,
            flat,
            jax.ShapeDtypeStruct((WIDE, 256), BF16),
            flat,
            stat,
            jax.ShapeDtypeStruct((full, 16), F32),
        ],
        scratch_shapes=[
            pltpu.VMEM((4, total, block.shape[1]), BF16),
            pltpu.VMEM((total, full), BF16),
            pltpu.VMEM((32, 48, 256), BF16),
            pltpu.VMEM((32, 48, 256), BF16),
            pltpu.VMEM((136, 256), F32),
            pltpu.VMEM((4 * QKV_ROWS, 256), F32),
            pltpu.VMEM((136, 16), F32),
            pltpu.VMEM((3, full, 256), F32),
            pltpu.VMEM((full, 256), F32),
            pltpu.VMEM((4, 4, 2, QKV_ROWS, full), BF16),
            pltpu.VMEM((4, 4, 2, OUT_ROWS, full), BF16),
            pltpu.VMEM((4, 3, 3, HD, 256), BF16),
            pltpu.VMEM((4, 2, 3, 1, HD, 256), BF16),
            DMA((32,)),
            DMA((32,)),
            DMA((32,)),
            DMA((32,)),
            DMA((2, 4)),
            DMA((2, 4)),
            DMA((3, 4)),
            DMA((3, 4)),
            DMA((6,)),
            DMA((3, 2, 4)),
            DMA((3, 2, 4)),
            DMA((2, 2, 4)),
            DMA((2, 2, 4)),
            DMA((3, 3)),
            DMA((3, 3)),
            DMA((3, 4)),
            DMA((3, 4)),
            DMA((1, 3, 4)),
            DMA((1, 3, 4)),
        ],
        compiler_params=params(0, 60),
    )(x_src, g_src, block, down_block, seg_row, seg_col)


def regroup(step, source, target):
    quad = source[pl.ds(pl.multiple_of(step * 136, 8), 136)]
    for part in range(4):
        target(part, quad[34 * part : 34 * part + 34])


def back_kernel(
    send,
    seg_row_ref,
    seg_col_ref,
    qkv_ref,
    out_ref,
    lse_ref,
    wide,
    out_in,
    dhidden_ref,
    normed2_ref,
    active_ref,
    g_ref,
    qkv_w,
    normed_ref,
    standard_ref,
    inv_std_ref,
    gain_ref,
    dresid_ref,
    bias_ref,
    layer_out,
    input_out,
    main_out,
    tail_out,
    down_out,
    column_out,
    wide_got,
    input_got,
    up_in,
    down_in,
    grad_ref,
    dqkv_ref,
    dk_ref,
    dv_ref,
    got,
    natural,
    slab_ref,
    slabs,
    w_buf,
    acc,
    columns,
    column_slab,
    column_part,
    column_sum,
    z_column,
    input_slab,
    input_slabs,
    qkv_part,
    sums,
    z_main,
    z_tail,
    wsend,
    wrecv,
    isend,
    irecv,
    zsend,
    zrecv,
    local,
    w_sem,
    *rest,
):
    place = greet_col()
    ix, iy, core, iz = (lax.axis_index(a) for a in ("x", "y", "core", "row"))
    xy = ix * 4 + iy
    for step in range(1, 4):
        signal(ring("row", step))
    pl.semaphore_wait(pltpu.get_barrier_semaphore(), 34)
    count = jnp.where(unit_place() == 0, 3, 2)
    begin, arrive, sent = head_swap(send, grad_ref, rest[0], rest[1])
    begin_result, pass_on, finish = result_swap(dqkv_ref, got, rest[2], rest[3])
    counts = (len(FIRST_FLOWS) * 8, len(LAST_FLOWS) * 8)
    bufs = rest[12:]
    sum_refs = [sums.at[:, pl.ds(at, rows)] for at, rows in zip(SUM_FIRST, SUM_ROWS)]
    first = ring_reduce(FIRST_FLOWS, (out_in, up_in), sum_refs[:2], bufs[: counts[0]], rest[4], rest[5])
    last = ring_reduce(
        LAST_FLOWS, (qkv_part,), sum_refs[2:], bufs[counts[0] : sum(counts)], rest[6], rest[7]
    )
    down = ring_reduce(
        DOWN_FLOWS, (down_in,), (down_out,), bufs[sum(counts) : sum(counts) + 12], rest[8], rest[9], True
    )
    cols = ring_reduce(
        COLUMN_FLOWS, (column_part,), (column_sum,), bufs[sum(counts) + 12 :], rest[10], rest[11]
    )
    for slot in range(3):
        begin(slot)

    def up_part(slab, _):
        part = nt(dhidden_ref[slab], normed2_ref[...])
        up_in[slab // 4, slab % 4] = part.astype(BF16)
        return 0

    lax.fori_loop(0, 16, up_part, 0)
    first[0](0)

    tail_rows = g_ref.shape[0] // 4 - DOWN_MAIN

    def down_part(z):
        start = z * (DOWN_MAIN + tail_rows)
        main = g_ref[pl.ds(pl.multiple_of(start, 16), DOWN_MAIN)]
        tail = g_ref[pl.ds(pl.multiple_of(start + DOWN_MAIN, 16), tail_rows)]

        def one(slab, _):
            units = active_ref[slab]
            down_in[z, slab, :FF_ROWS] = nt(units, main).astype(BF16)
            turned = nt(tail, units).astype(BF16)
            down_in[z, slab, FF_ROWS:] = jnp.concatenate(
                [turned, jnp.zeros((tail_rows, DOWN_MAIN - FF_ROWS), BF16)], 1
            )
            return 0

        lax.fori_loop(0, 16, one, 0)

    down_part((iz + 2) % 4)
    down[0](0, (0, 1))

    def copy_wide(step, owner):
        peer = (place + step) % 32
        return remote(
            wide.at[peer], wide_got.at[owner], wsend.at[step], wrecv.at[step], col_device(peer)
        )

    def begin_wide(step, _):
        copy_wide(step, place).start()
        return 0

    own = pltpu.make_async_copy(wide.at[place], wide_got.at[place], local)
    own.start()

    def copy_w(step):
        return pltpu.make_async_copy(
            qkv_w.at[pl.ds(step * 4, 4)], w_buf.at[step % 2], w_sem.at[step % 2]
        )

    copy_w(0).start()

    def unit(slot, _):
        arrive(slot)
        q = qkv_ref[slot, 0] * (HD**-0.5)
        key_cols = qkv_ref[slot, 1]
        k = key_cols.T
        v = qkv_ref[slot, 2].T
        grad = grad_ref[slot, 0]
        delta = jnp.sum(grad.astype(F32) * out_ref[slot, 0].astype(F32), 0, keepdims=True)
        dk_ref[...] = jnp.zeros_like(dk_ref)
        dv_ref[...] = jnp.zeros_like(dv_ref)
        for start in range(0, q.shape[1], QB):
            keys = start + QB
            scores = masked_scores(
                k, q[:, start:keys], seg_col_ref[...], seg_row_ref[...], start, keys
            )
            weights = jnp.exp(scores - lse_ref[slot, :, start:keys])
            dweights = nn(v[:keys], grad[:, start:keys])
            dscores = (weights * (dweights - delta[:, start:keys])).astype(BF16)
            dq = nn(key_cols[:, :keys], dscores) * (HD**-0.5)
            dqkv_ref[slot, 0, :, start:keys] = dq.astype(BF16)
            dk_ref[:, :keys] += nt(q[:, start:keys], dscores)
            dv_ref[:, :keys] += nt(grad[:, start:keys], weights.astype(BF16))
        dqkv_ref[slot, 1] = dk_ref[...].astype(BF16)
        dqkv_ref[slot, 2] = dv_ref[...].astype(BF16)
        begin_result(slot)
        return 0

    lax.fori_loop(0, count, unit, 0)
    first[1](0)
    down_part((iz + 1) % 4)
    down_part((iz + 3) % 4)
    down[0](0, (2, 3))
    down[1](0)
    down_part(iz)
    lax.fori_loop(1, 32, begin_wide, 0)
    sent()
    pass_on()
    finish(count)

    for head in range(HEADS):
        owner = head % 8
        for j in range(3):
            natural[j, head * HD : head * HD + HD] = got[owner // 2, owner % 2, head // 8, j].astype(F32)
    slab_ref[...] = jnp.zeros_like(slab_ref)
    acc[...] = jnp.zeros_like(acc)

    def by_slab(step, _):
        for j in range(3):

            def put(part, rows, j=j):
                slab_ref[part, 34 * j : 34 * j + 34] = rows

            regroup(step, natural.at[j], put)
        four = slab_ref[...].astype(BF16)
        slabs[pl.ds(step * 4, 4)] = four
        return 0

    lax.fori_loop(0, 8, by_slab, 0)

    far_x, far_y = (ix + 2) % 4, (iy + 2) % 4

    def weight_part(dx, dy):
        px, py = (far_x + dx) % 4, (far_y + dy) % 4
        part = nt(slabs[(px * 4 + py) * 2 + core], normed_ref[...])
        qkv_part[px, py] = part.astype(BF16)
        return 0

    lax.fori_loop(0, 4, lambda step, _: weight_part(step, 0), 0)
    lax.fori_loop(1, 4, lambda step, _: weight_part(0, step), 0)
    last[0](0, (0, 1))
    lax.fori_loop(0, 9, lambda step, _: weight_part(1 + step // 3, 1 + step % 3), 0)
    last[0](0, (2, 3))

    def product(step, _):
        @pl.when(step < 7)
        def _():
            copy_w(step + 1).start()

        copy_w(step).wait()
        acc[...] += lax.dot_general(
            slabs[pl.ds(step * 4, 4)].reshape(4 * QKV_ROWS, 256),
            w_buf[step % 2].reshape(4 * QKV_ROWS, -1),
            (((0,), (0,)), ((), ())),
            preferred_element_type=F32,
        )
        return 0

    lax.fori_loop(0, 8, product, 0)
    last[1](0)
    first[2](0)
    first[0](1)

    late = [
        pltpu.make_async_copy(standard_ref, natural.at[1], w_sem.at[0]),
        pltpu.make_async_copy(dresid_ref, natural.at[2], w_sem.at[1]),
    ]
    for c in late:
        c.start()
    dnormed = acc[...].T
    for c in late:
        c.wait()
    standard = natural[1]
    dv = dnormed * gain_ref[...]
    back = inv_std_ref[...] * (
        dv - jnp.mean(dv, 0, keepdims=True) - standard * jnp.mean(dv * standard, 0, keepdims=True)
    )
    natural[0] = natural[2] + back
    lane = lax.broadcasted_iota(jnp.int32, columns.shape, 1)
    gain_col = jnp.sum(dnormed * standard, 1, keepdims=True)
    shift_col = jnp.sum(dnormed, 1, keepdims=True)
    columns[...] = jnp.where(lane == 65, gain_col, jnp.where(lane == 66, shift_col, 0.0))
    input_slab[...] = jnp.zeros_like(input_slab)
    column_slab[...] = jnp.zeros_like(column_slab)

    def spread(step, _):
        def put(part, rows):
            input_slab[part, :34] = rows

        def put_column(part, rows):
            column_slab[step * 4 + part, :34] = rows

        regroup(step, natural.at[0], put)
        regroup(step, columns, put_column)
        input_slabs[pl.ds(step * 4, 4)] = input_slab[...].astype(BF16)
        return 0

    lax.fori_loop(0, 8, spread, 0)

    def copy_input(step, owner):
        peer = (xy + step) % 16
        return remote(
            input_slabs.at[peer * 2 + core],
            input_got.at[owner],
            isend.at[step],
            irecv.at[step],
            {"x": peer // 4, "y": peer % 4},
        )

    def own_columns(step, _):
        column_part[step // 4, step % 4] = column_slab[step * 2 + core].astype(BF16)
        return 0

    lax.fori_loop(0, 16, own_columns, 0)
    cols[0](0)
    down[2](0)
    down[0](1)

    def begin_input(step, _):
        copy_input(step, xy).start()
        return 0

    lax.fori_loop(1, 16, begin_input, 0)
    input_got[xy] = input_slabs[xy * 2 + core]

    def z_columns(step):
        return remote(
            column_sum, z_column.at[pl.ds(step - 1, 1)], zsend.at[2, 0, step - 1], zrecv.at[2, 0, step - 1], ring("row", step)
        )

    def z_copies(group, step):
        rows = pl.ds(0, SUM_FIRST[2]) if group == 0 else pl.ds(SUM_FIRST[2], QKV_ROWS)
        window = pl.ds(pl.multiple_of((iz + step) % 4 * 256, 256), WINDOW)
        return [
            remote(
                sums.at[0, rows, lanes],
                out.at[step - 1, rows],
                zsend.at[group, i, step - 1],
                zrecv.at[group, i, step - 1],
                ring("row", step),
            )
            for i, (lanes, out) in enumerate(((window, z_main), (pl.ds(WIDE - LANE, LANE), z_tail)))
        ]

    def begin_z(group):
        for step in range(1, 4):
            for c in z_copies(group, step):
                c.start()

    first[1](1)
    down[1](1)
    first[2](1)
    begin_z(0)
    cols[1](0)
    last[2](0)
    last[0](1)
    cols[2](0)
    cols[0](1)
    down[2](1)
    down[0](2)
    last[1](1)
    cols[1](1)
    down[1](2)
    last[2](1)
    begin_z(1)
    cols[2](1)
    for step in range(1, 4):
        z_columns(step).start()
    down[2](2)
    first[3]()
    last[3]()
    down[3]()
    cols[3]()
    own.wait()

    def end_wide(step, _):
        copy_wide(step, (place + 32 - step) % 32).wait()
        return 0

    lax.fori_loop(1, 32, end_wide, 0)

    def put_layer(chip, _):
        halves = wide_got[chip * 2, :34].astype(F32) + wide_got[chip * 2 + 1, :34].astype(F32)
        layer_out[:, rows_of(chip * 256)] = halves + bias_ref[...]
        return 0

    lax.fori_loop(0, 16, put_layer, 0)

    def end_input(step, _):
        copy_input(step, (xy + 16 - step) % 16).wait()
        return 0

    lax.fori_loop(1, 16, end_input, 0)

    def put_input(chip, _):
        input_out[:, rows_of(chip * 256)] = input_got[chip, :34].astype(F32)
        return 0

    lax.fori_loop(0, 16, put_input, 0)
    for group in range(2):
        for step in range(1, 4):
            for c in z_copies(group, step):
                c.wait()
    for step in range(1, 4):
        z_columns(step).wait()
    column_out[...] = column_sum[0].astype(F32) + sum(z_column[i].astype(F32) for i in range(3))
    window = pl.ds(pl.multiple_of(iz * 256, 256), WINDOW)
    main_out[...] = sums[0, :, window].astype(F32) + sum(z_main[i].astype(F32) for i in range(3))
    tail_out[...] = sums[0, :, WIDE - LANE :].astype(F32) + sum(z_tail[i].astype(F32) for i in range(3))


def attend_back(
    send, seg_row, seg_col, qkv, out, lse, wide, out_part, dhidden, normed2, active, g, qkv_w, normed, standard, inv_std, gain, dresid, bias
):
    length = seg_row.shape[1]
    full = qkv_w.shape[-1]
    first_sems, first_bufs = ring_bufs(FIRST_FLOWS, WIDE)
    last_sems, last_bufs = ring_bufs(LAST_FLOWS, WIDE)
    down_sems, down_bufs = ring_bufs(DOWN_FLOWS, DOWN_MAIN, True)
    column_sems, column_bufs = ring_bufs(COLUMN_FLOWS, LANE)
    total = sum(SUM_ROWS)
    return pl.pallas_call(
        back_kernel,
        in_specs=[VMEM] * 6 + [ANY] + [VMEM] * 5 + [ANY, VMEM, ANY, VMEM, VMEM, ANY, VMEM],
        out_specs=[VMEM] * 6,
        out_shape=[
            jax.ShapeDtypeStruct((34, 4096), F32),
            jax.ShapeDtypeStruct((34, 4096), F32),
            jax.ShapeDtypeStruct((total, WINDOW), F32),
            jax.ShapeDtypeStruct((total, LANE), F32),
            jax.ShapeDtypeStruct((1, DOWN_ROWS, DOWN_MAIN), F32),
            jax.ShapeDtypeStruct((48, LANE), F32),
        ],
        scratch_shapes=[
            pltpu.VMEM(wide.shape, BF16),
            pltpu.VMEM((16, 48, 256), BF16),
            pltpu.VMEM((4, 4, FF_ROWS, WIDE), BF16),
            pltpu.VMEM((4, 16, DOWN_ROWS, DOWN_MAIN), BF16),
            pltpu.VMEM((3, 1, HD, length), BF16),
            pltpu.VMEM((3, 3, HD, length), BF16),
            pltpu.VMEM((HD, length), F32),
            pltpu.VMEM((HD, length), F32),
            pltpu.VMEM((4, 2, 3, 3, HD, 256), BF16),
            pltpu.VMEM((3, full, 256), F32),
            pltpu.VMEM((4, QKV_ROWS, 256), F32),
            pltpu.VMEM((32, QKV_ROWS, 256), BF16),
            pltpu.VMEM((2, 4, QKV_ROWS, full), BF16),
            pltpu.VMEM((256, full), F32),
            pltpu.VMEM((full, LANE), F32),
            pltpu.VMEM((32, 48, LANE), F32),
            pltpu.VMEM((4, 4, 48, LANE), BF16),
            pltpu.VMEM((1, 48, LANE), BF16),
            pltpu.VMEM((3, 48, LANE), BF16),
            pltpu.VMEM((4, 48, 256), F32),
            pltpu.VMEM((32, 48, 256), BF16),
            pltpu.VMEM((4, 4, QKV_ROWS, WIDE), BF16),
            pltpu.VMEM((1, total, WIDE), BF16),
            pltpu.VMEM((3, total, WINDOW), BF16),
            pltpu.VMEM((3, total, LANE), BF16),
            DMA((32,)),
            DMA((32,)),
            DMA((16,)),
            DMA((16,)),
            DMA((3, 2, 3)),
            DMA((3, 2, 3)),
            DMA,
            DMA((2,)),
            DMA((3, 3)),
            DMA((3, 3)),
            DMA((3, 4)),
            DMA((3, 4)),
        ]
        + first_sems
        + last_sems
        + down_sems
        + column_sems
        + first_bufs
        + last_bufs
        + down_bufs
        + column_bufs,
        compiler_params=params(6, 62),
    )(
        send, seg_row, seg_col, qkv, out, lse, wide, out_part, dhidden, normed2, active, g, qkv_w, normed, standard, inv_std, gain, dresid, bias
    )


def norm_back(dn, standard, inv_std, gain):
    dv = dn * gain
    back = inv_std * (
        dv - jnp.mean(dv, 0, keepdims=True) - standard * jnp.mean(dv * standard, 0, keepdims=True)
    )
    return back, jnp.sum(dn * standard, 1), jnp.sum(dn, 1)


def to_heads(v, core):
    n, _, tokens = v.shape
    heads = v.reshape(n, HEADS, HD, tokens).transpose(1, 0, 2, 3)
    pairs = heads[:16].reshape(2, 4, 2, n, HD, tokens)
    mine = lax.dynamic_index_in_dim(pairs, core, 2, keepdims=False)
    last = jnp.broadcast_to(heads[16:], (4, n, HD, tokens))
    return jnp.concatenate([mine.transpose(1, 0, 2, 3, 4), last[:, None]], 1)


def shards(
    layer_input,
    cotangent,
    segments,
    qkv_weight,
    qv_bias,
    out_weight,
    out_bias,
    up_weight,
    up_bias,
    down_weight,
    down_bias,
    first_gain,
    first_shift,
    second_gain,
    second_shift,
):
    ix, iy, core = lax.axis_index("x"), lax.axis_index("y"), lax.axis_index("core")
    width = layer_input.shape[0]
    rows = qkv_weight.shape[0]
    full = 4 * rows
    units = up_weight.shape[1]

    block = jnp.concatenate(
        [
            qkv_weight.transpose(1, 2, 0).reshape(3 * width, rows),
            jnp.pad(up_bias[None], ((0, QKV_ROWS - 3 * width - 1), (0, rows - units))),
            jnp.pad(out_weight.T, ((0, OUT_ROWS - width), (0, 0))),
            jnp.pad(up_weight.T, ((0, FF_ROWS - units), (0, 0))),
        ],
        0,
    )
    down_block = jnp.concatenate(
        [
            jnp.pad(down_weight[:, :DOWN_MAIN], ((0, FF_ROWS - units), (0, 0))),
            jnp.pad(down_weight[:, DOWN_MAIN:].T, ((0, 0), (0, DOWN_MAIN - units))),
        ],
        0,
    )
    small = jnp.concatenate(
        [qv_bias, jnp.stack([out_bias, first_gain, first_shift, second_gain, second_shift])], 0
    )
    small = jnp.tile(jnp.pad(small, ((0, 48 - width - 7), (0, 256 - width))), (1, 16))
    x_src = jnp.concatenate([layer_input, small], 0)
    g_src = jnp.pad(cotangent, ((0, 48 - width), (0, 0)))
    seg = lax.dynamic_index_in_dim(segments, ix, 0, keepdims=False)
    seg_row, seg_col = seg[None], seg[:, None]
    (
        qkv_w,
        out_w,
        up_w,
        down_w,
        g_low,
        normed1,
        standard1,
        inv_std1,
        units_qkv,
        units_out,
        lse,
        attn,
        resid,
        normed2,
        standard2,
        inv_std2,
        vectors,
    ) = front(x_src, g_src, block, down_block, seg_row, seg_col)
    qkv_w = qkv_w.reshape(32, QKV_ROWS, full)
    out_w = out_w.reshape(32, OUT_ROWS, full)
    up_w = up_w.reshape(16, FF_ROWS, full)
    down_w = down_w.reshape(4, 16, DOWN_ROWS, DOWN_MAIN)
    down_tail = down_w[:, :, FF_ROWS:, :FF_ROWS]
    g = g_low.astype(F32)
    gain1, gain2 = vectors[:, 5:6], vectors[:, 7:8]
    hidden_bias = lax.dynamic_index_in_dim(
        qkv_w[:, 3 * width, :units].reshape(16, 2, units), core, 1, keepdims=False
    ).astype(F32)
    hidden_bias = jnp.pad(hidden_bias, ((0, 0), (0, FF_ROWS - units)))
    hidden = jnp.einsum("xfd,dt->xft", up_w, normed2[:full], preferred_element_type=F32) + hidden_bias[..., None]
    active, gelu_back = jax.vjp(lambda h: jax.nn.gelu(h, approximate=True), hidden)
    active = active.astype(BF16)
    active_rows = jnp.pad(active, ((0, 0), (0, DOWN_ROWS - FF_ROWS), (0, 0)))
    out_main = [
        jnp.einsum("xfd,xft->dt", down_w[z], active_rows, preferred_element_type=F32) for z in range(4)
    ]
    out_tail = jnp.einsum("zxdf,xft->zdt", down_tail, active, preferred_element_type=F32)
    ff_out = jnp.concatenate([p for z in range(4) for p in (out_main[z], out_tail[z])], 0)
    send_out = (ff_out + jnp.where(core == 0, 1.0, 0.0) * resid).astype(BF16)
    send_out = jnp.pad(send_out.reshape(32, width, 256), ((0, 0), (0, 48 - width), (0, 0)))
    g_main = [g_low[z * rows : z * rows + DOWN_MAIN] for z in range(4)]
    g_tail = jnp.stack([g_low[z * rows + DOWN_MAIN : z * rows + rows] for z in range(4)])
    dactive = sum(
        jnp.einsum("xfd,dt->xft", down_w[z], g_main[z], preferred_element_type=F32) for z in range(4)
    )[:, :FF_ROWS]
    dactive = dactive + jnp.einsum("zxdf,zdt->xft", down_tail, g_tail, preferred_element_type=F32)
    dhidden = gelu_back(dactive)[0].astype(BF16)
    extra = WIDE - full
    ones_row = jnp.pad(jnp.ones((1, 256), BF16), ((0, extra - 1), (0, 0)))

    def widen(v):
        return jnp.concatenate([v, ones_row], 0)

    dn2 = jnp.einsum("xfd,xft->dt", up_w, dhidden, preferred_element_type=F32)
    dn2 = core_sum(dn2.astype(BF16))
    back2, gain2_grad, shift2_grad = norm_back(dn2, standard2, inv_std2, gain2)
    dresid = g + back2
    dproj = dresid.astype(BF16)
    dproj_block = jnp.pad(dproj.reshape(32, width, 256), ((0, 0), (0, OUT_ROWS - width), (0, 0)))
    dattn = jnp.einsum("ced,cet->dt", out_w, dproj_block, preferred_element_type=F32).astype(BF16)
    mine = lax.dynamic_index_in_dim(dproj_block.reshape(16, 2, OUT_ROWS, 256), core, 1, keepdims=False)
    cols = jnp.stack([jnp.sum(g, -1), gain2_grad, shift2_grad], -1).reshape(16, 2, width, 3)
    cols = lax.dynamic_index_in_dim(cols, core, 1, keepdims=False)
    cols = jnp.pad(cols, ((0, 0), (0, OUT_ROWS - width), (full + 1, extra - 4)))
    out_part = jnp.einsum("xrt,dt->xrd", mine, widen(attn), preferred_element_type=F32) + cols
    layer_output, input_grad, main, tail, down_sum, columns = attend_back(
        to_heads(dattn[None], core),
        seg_row,
        seg_col,
        units_qkv,
        units_out,
        lse,
        send_out,
        out_part.astype(BF16).reshape(4, 4, OUT_ROWS, WIDE),
        dhidden,
        normed2,
        active,
        g_low,
        qkv_w,
        normed1,
        standard1,
        inv_std1,
        gain1,
        dresid,
        down_bias.astype(F32)[:, None],
    )
    main = lax.dynamic_slice_in_dim(main, lax.axis_index("row") * (rows - 256), rows, 1)
    out_first, up_first, qkv_first = SUM_FIRST
    qkv_out = main[qkv_first : qkv_first + 3 * width].reshape(3, width, rows).transpose(2, 0, 1)
    qkv_tail = tail[qkv_first:, LANE - extra :]
    out_tail = tail[out_first : out_first + width, LANE - extra :]
    return (
        layer_output,
        input_grad,
        qkv_out,
        jnp.stack([qkv_tail[:width, 0], qkv_tail[2 * width : 3 * width, 0]]),
        main[out_first : out_first + width].T,
        out_tail[:, 0],
        main[up_first : up_first + units].T,
        tail[up_first : up_first + units, LANE - extra],
        jnp.concatenate([down_sum[0, :units], down_sum[0, FF_ROWS:, :units].T], 1),
        out_tail[:, 1],
        columns[:width, 65],
        columns[:width, 66],
        out_tail[:, 2],
        out_tail[:, 3],
    )


def solution(mesh):
    split = Mesh(mesh.devices.reshape(4, 4, 4, 2), ("row", "x", "y", "core"))
    vec = P(COL)
    return jax.shard_map(
        shards,
        mesh=split,
        in_specs=(
            P(COL, "row"),
            P(COL, "row"),
            P("row", None),
            P("row", None, COL),
            P(None, COL),
            P("row", COL),
            vec,
            P("row", COL),
            vec,
            P(COL, "row"),
            vec,
            vec,
            vec,
            vec,
            vec,
        ),
        out_specs=(
            P(COL, "row"),
            P(COL, "row"),
            P("row", None, COL),
            P(None, COL),
            P("row", COL),
            vec,
            P("row", COL),
            vec,
            P(COL, "row"),
            vec,
            vec,
            vec,
            vec,
            vec,
        ),
        check_vma=False,
    )
```
